32 devices in a mesh: space: 8 (over z, y), fsdp: 4 (over x, core).
Axes of the slice: x: 2, y: 2, z: 4, core: 2. Of those that a mesh axis runs over, the one named last changes fastest.
Arguments:
- frames: float32 [2, 4, 2, 16, 16], P(None, 'fsdp', None, 'space'), may hold values from -5 to 5
- targets: float32 [2, 4, 2, 16, 16], P(None, 'fsdp', None, 'space'), may hold values from -5 to 5
- sizes: int32 [2, 4], P(None, 'fsdp'), may hold values from 8 to 16, as said below
- horizon: int32 [2, 4, 2, 16, 16], P(None, 'fsdp', None, 'space'), may hold values from 0 to 4
- conv_weight: float32 [12800, 1024], P('space', 'fsdp'), may hold values from -0.0546875 to 0.0546875
- conv_m: float32 [12800, 1024], P('space', 'fsdp'), may hold values from -4.7683716e-06 to 4.7683716e-06
- conv_v: float32 [12800, 1024], P('space', 'fsdp'), may hold values from 7.627756e-15 to 3.0511025e-14
- gates_vec: float32 [2, 1024], P(None, 'space'), may hold values from 0.5 to 1.5
- gates_m: float32 [2, 1024], P(None, 'space'), may hold values from -4.7683716e-06 to 4.7683716e-06
- gates_v: float32 [2, 1024], P(None, 'space'), may hold values from 7.627756e-15 to 3.0511025e-14
- chan_vec: float32 [3, 256], P(None, 'space'), may hold values from -4 to 4
- chan_m: float32 [3, 256], P(None, 'space'), may hold values from -4.7683716e-06 to 4.7683716e-06
- chan_v: float32 [3, 256], P(None, 'space'), may hold values from 7.627756e-15 to 3.0511025e-14
Outputs:
- loss: float32 [], replicated
- grad_norm: float32 [], replicated
- conv_new: float32 [12800, 1024], P('space', 'fsdp')
- conv_m_new: float32 [12800, 1024], P('space', 'fsdp')
- conv_v_new: float32 [12800, 1024], P('space', 'fsdp')
- gates_new: float32 [2, 1024], P(None, 'space')
- gates_m_new: float32 [2, 1024], P(None, 'space')
- gates_v_new: float32 [2, 1024], P(None, 'space')
- chan_new: float32 [3, 256], P(None, 'space')
- chan_m_new: float32 [3, 256], P(None, 'space')
- chan_v_new: float32 [3, 256], P(None, 'space')
- hidden_final: float32 [4, 16, 16, 256], P('fsdp', 'space')
- cell_final: float32 [4, 16, 16, 256], P('fsdp', 'space')
The draws below stay inside these ranges and needn't reach their ends.
Inputs may be any that keep to these rules, and one draw needn't show every extreme that they name: `sizes`: each value is 8 or 16; stream 0 of every micro-batch has 16. `horizon`: the value 4 marks a pixel without a target.
All inputs are finite; a program needn't handle non-finite values.
Results may differ from the reference program's by a relative error of at most 0.00035.
The reference program's roundings to bfloat16 on the way count: a program that leaves them out, or rounds other values in their place, can miss the bound.
Values may be sent and summed in bfloat16 or wider, within the bound.
A program may use at most 256 MiB of HBM per device.

```python
import math
import jax
import jax.numpy as jnp
from jax import lax

HID = 256
GROUPS = 32
HOR = 4
COLS = 16
FRAMES = 2
MICRO = 2
STEP = 10
ROWS = 16
STREAMS = 4


def draw_sizes(key, part):
    key = jax.random.fold_in(key, 11)
    picks = jax.random.randint(key, (MICRO, STREAMS), 0, 2, dtype=jnp.int32)
    picks = picks.at[:, 0].set(1)
    return ROWS // 2 * (1 + picks)


def set_ends(drawn, rng, smallest, top_value):
    longest = drawn.shape.index(max(drawn.shape))
    spots = []
    for shift in (0, 1):
        where = [jax.random.randint(jax.random.fold_in(rng, axis), (), 0, length) for axis, length in enumerate(drawn.shape)]
        where[longest] = (where[longest] + shift) % drawn.shape[longest]
        spots.append(tuple(where))
    return drawn.at[spots[0]].set(smallest).at[spots[1]].set(top_value)


def shard_levels(stream_key, dims, pieces, smallest, largest):
    gain, own = 1.0, jax.random.fold_in(stream_key, 6)
    for dim, shards_of in pieces:
        steps = jnp.exp(jax.random.uniform(jax.random.fold_in(own, dim), (shards_of,), jnp.float32, smallest / len(pieces), largest / len(pieces)))
        gain = gain * jnp.repeat(steps, dims[dim] // shards_of).reshape([-1 if axis == dim else 1 for axis in range(len(dims))])
    return gain


def gaussian(rng, shape, spread, reach, pieces=(), held_as=jnp.bfloat16):
    drawn = jax.random.normal(rng, shape, jnp.float32) * spread
    if len(pieces) > 0:
        drawn = shard_levels(rng, shape, pieces, -0.22, 0.18) * drawn
    return jnp.clip(drawn, min=-reach, max=reach).astype(held_as)


def setup_inputs(seed: int = 0) -> dict:
    key_of = jax.random.split(jax.random.key(seed), 14)
    return {
        "frames": gaussian(key_of[0], (MICRO, STREAMS, FRAMES, ROWS, COLS), 1.0, 5.0, ((1, 4), (3, 8)), jnp.float32),
        "targets": gaussian(key_of[1], (MICRO, STREAMS, FRAMES, ROWS, COLS), 1.0, 5.0, ((1, 4), (3, 8)), jnp.float32),
        "sizes": draw_sizes(jax.random.fold_in(key_of[13], 71), 0),
        "horizon": set_ends(jax.random.randint(key_of[3], (MICRO, STREAMS, FRAMES, ROWS, COLS), 0, HOR + 1), jax.random.fold_in(key_of[3], 1), 0, HOR).astype(jnp.int32),
        "conv_weight": gaussian(key_of[4], (50 * HID, 4 * HID), (50 * HID) ** -0.5, 0.0546875, ((0, 8), (1, 4)), jnp.float32),
        "conv_m": gaussian(key_of[5], (50 * HID, 4 * HID), (0.11 * 0.01 / (200 * HID * HID + 11 * HID) ** 0.5), 4.76837158203125e-06, ((0, 8), (1, 4)), jnp.float32),
        "conv_v": jnp.clip(jnp.exp(math.log(3.051102461502399e-14) - 1.3862944 * jax.random.uniform(key_of[6], (50 * HID, 4 * HID), jnp.float32) ** shard_levels(key_of[6], (50 * HID, 4 * HID), ((0, 8), (1, 4)), -0.2, 0.2)), 7.627756153755997e-15, 3.051102461502399e-14),
        "gates_vec": jnp.clip(1.0 + 0.1 * jax.random.normal(key_of[7], (2, 4 * HID), jnp.float32), 0.5, 1.5),
        "gates_m": gaussian(key_of[8], (2, 4 * HID), (0.11 * 0.01 / (200 * HID * HID + 11 * HID) ** 0.5), 4.76837158203125e-06, ((1, 8),), jnp.float32),
        "gates_v": jnp.clip(jnp.exp(math.log(3.051102461502399e-14) - 1.3862944 * jax.random.uniform(key_of[9], (2, 4 * HID), jnp.float32) ** shard_levels(key_of[9], (2, 4 * HID), ((1, 8),), -0.2, 0.2)), 7.627756153755997e-15, 3.051102461502399e-14),
        "chan_vec": gaussian(key_of[10], (3, HID), 0.3, 4.0, ((1, 8),), jnp.float32),
        "chan_m": gaussian(key_of[11], (3, HID), (0.11 * 0.01 / (200 * HID * HID + 11 * HID) ** 0.5), 4.76837158203125e-06, ((1, 8),), jnp.float32),
        "chan_v": jnp.clip(jnp.exp(math.log(3.051102461502399e-14) - 1.3862944 * jax.random.uniform(key_of[12], (3, HID), jnp.float32) ** shard_levels(key_of[12], (3, HID), ((1, 8),), -0.2, 0.2)), 7.627756153755997e-15, 3.051102461502399e-14),
    }


@jax.custom_vjp
def low(v):
    return lax.optimization_barrier(v.astype(jnp.bfloat16)).astype(jnp.float32)

@jax.custom_vjp
def low_back(v):
    return v

def low_keep(v):
    return (low(v), None)

def low_pass(kept, grad):
    return (grad,)

def back_keep(v):
    return (v, None)

def back_low(kept, grad):
    return (low(grad),)
low.defvjp(low_keep, low_pass)
low_back.defvjp(back_keep, back_low)
EPS_NORM = 1e-05
CLIP = 0.01
RATE = 0.01
BETA1 = 0.9
BETA2 = 0.999
DECAY = 0.01
EPS_ADAM = 1e-08

def cell_head(gates, cell_prev, valid, head_w):
    width = cell_prev.shape[-1]
    gate_in = jax.nn.sigmoid(gates[..., :width])
    gate_forget = jax.nn.sigmoid(gates[..., width:2 * width])
    gate_out = jax.nn.sigmoid(gates[..., 2 * width:3 * width])
    candidate = jnp.tanh(gates[..., 3 * width:])
    cell_new = (gate_forget * cell_prev + gate_in * candidate) * valid
    hidden_new = gate_out * jnp.tanh(cell_new) * valid
    return (hidden_new, cell_new, lax.optimization_barrier(jnp.sum(hidden_new * head_w, axis=-1)))

def adam_update(weight, first, second, grad):
    first = BETA1 * first + (1.0 - BETA1) * grad
    second = BETA2 * second + (1.0 - BETA2) * grad * grad
    first_hat = first / (1.0 - BETA1 ** STEP)
    second_hat = second / (1.0 - BETA2 ** STEP)
    weight = weight - RATE * (first_hat / (jnp.sqrt(second_hat) + EPS_ADAM) + DECAY * weight)
    return (weight, first, second)

def reference(frames, targets, sizes, horizon, conv_weight, conv_m, conv_v, gates_vec, gates_m, gates_v, chan_vec, chan_m, chan_v):
    total_streams = MICRO * STREAMS
    row_ids = jnp.arange(ROWS, dtype=jnp.int32)
    inside_all = (row_ids[None, :] >= ROWS - sizes.reshape(-1)[:, None]).astype(jnp.float32)
    picks = (horizon.reshape(total_streams, FRAMES, ROWS, COLS)[..., None] == jnp.arange(HOR, dtype=jnp.int32)).astype(jnp.float32)
    picks = picks * inside_all[:, None, :, None, None]
    counts = lax.optimization_barrier(jnp.sum(picks, axis=(0, 1, 2, 3)))
    hweight = 1.0 / (HOR * jnp.maximum(counts, 1.0))
    group_count = sizes.reshape(-1).astype(jnp.float32) * (COLS * (4 * HID // GROUPS))
    seqs = frames.reshape(total_streams, FRAMES, ROWS, COLS)
    goals = targets.reshape(total_streams, FRAMES, ROWS, COLS)

    def total(conv_w, gvec_w, cvec_w):
        kernel = low(conv_w).reshape(5, 5, 2 * HID, 4 * HID)
        gains = low(gvec_w)
        chans = low(cvec_w)

        def one(item):
            seq, goal, chosen, inside, count = item
            valid = inside[:, None, None]

            def frame(carry, inputs):
                hidden, cell = carry
                pixels, target, picked = inputs
                lifted = (pixels[..., None] * chans[0] + chans[1]) * valid
                joined = low(jnp.concatenate([lifted, hidden], -1))
                pre = lax.conv_general_dilated(joined[None], kernel, (1, 1), ((2, 2), (2, 2)), dimension_numbers=('NHWC', 'HWIO', 'NHWC'), precision=lax.Precision.HIGHEST)[0]
                pre = low_back(pre)
                grouped = pre.reshape(ROWS, COLS, GROUPS, -1)
                weighted = grouped * valid[..., None]
                first = lax.optimization_barrier(jnp.sum(weighted, axis=(0, 1, 3)))
                second = lax.optimization_barrier(jnp.sum(weighted * grouped, axis=(0, 1, 3)))
                centre = first / count
                scale = lax.rsqrt(second / count - centre * centre + EPS_NORM)
                normed = ((grouped - centre[:, None]) * scale[:, None]).reshape(ROWS, COLS, 4 * HID)
                gates = normed * gains[0] + gains[1]
                hidden, cell, output = cell_head(gates, cell, valid, chans[2])
                error = output - target
                return ((hidden, cell), lax.optimization_barrier(jnp.sum(picked * (error * error)[..., None], axis=(0, 1))))
            zeros = jnp.zeros((ROWS, COLS, HID), jnp.float32)
            (hidden, cell), sse = lax.scan(frame, (zeros, zeros), (seq, goal, chosen))
            return (lax.optimization_barrier(jnp.sum(sse, axis=0)), hidden, cell)
        sse, hiddens, cells = lax.map(jax.checkpoint(one), (seqs, goals, picks, inside_all, group_count))
        sse_total = lax.optimization_barrier(jnp.sum(sse, axis=0))
        return (jnp.sum(sse_total * hweight), (hiddens, cells))
    loss, pull, (hiddens, cells) = jax.vjp(total, conv_weight, gates_vec, chan_vec, has_aux=True)
    grads = pull(jnp.ones((), jnp.float32))
    norm = jnp.sqrt(sum((jnp.sum(g * g) for g in grads)))
    factor = jnp.minimum(1.0, CLIP / (norm + 1e-06))
    conv_new, conv_m_new, conv_v_new = adam_update(conv_weight, conv_m, conv_v, grads[0] * factor)
    gates_new, gates_m_new, gates_v_new = adam_update(gates_vec, gates_m, gates_v, grads[1] * factor)
    chan_new, chan_m_new, chan_v_new = adam_update(chan_vec, chan_m, chan_v, grads[2] * factor)
    hidden_final = hiddens.reshape(MICRO, STREAMS, ROWS, COLS, HID)[MICRO - 1]
    cell_final = cells.reshape(MICRO, STREAMS, ROWS, COLS, HID)[MICRO - 1]
    return (loss, norm, conv_new, conv_m_new, conv_v_new, gates_new, gates_m_new, gates_v_new, chan_new, chan_m_new, chan_v_new, hidden_final, cell_final)
```

```python
import functools

import jax
import jax.numpy as jnp
from jax import lax
from jax.experimental import pallas as pl
from jax.experimental.pallas import tpu as pltpu
from jax.sharding import PartitionSpec as P

GROUPS = 32
HOR = 4
STEP = 10


EPS_NORM = 1e-05
CLIP = 0.01
RATE = 0.01
BETA1 = 0.9
BETA2 = 0.999
DECAY = 0.01
EPS_ADAM = 1e-08


def with_halo(shard, sides, width):
    for axis, dim in sides:
        count, length = (lax.axis_size(axis), shard.shape[dim])
        up = [(i, (i + 1) % count) for i in range(count - 1)]
        down = [(j, i) for i, j in up]
        last = lax.slice_in_dim(shard, length - width, length, axis=dim)
        first = lax.slice_in_dim(shard, 0, width, axis=dim)
        before = lax.ppermute(last, axis, up)
        after = lax.ppermute(first, axis, down)
        shard = jnp.concatenate([before, shard, after], axis=dim)
    return shard


def cell_head(gates, cell_prev, valid, head_w):
    width = cell_prev.shape[-1]
    gate_in = jax.nn.sigmoid(gates[..., :width])
    gate_forget = jax.nn.sigmoid(gates[..., width : 2 * width])
    gate_out = jax.nn.sigmoid(gates[..., 2 * width : 3 * width])
    candidate = jnp.tanh(gates[..., 3 * width :])
    cell_new = (gate_forget * cell_prev + gate_in * candidate) * valid
    hidden_new = gate_out * jnp.tanh(cell_new) * valid
    return (hidden_new, cell_new, jnp.sum(hidden_new * head_w, axis=-1))


def adam_update(weight, first, second, grad):
    first = BETA1 * first + (1.0 - BETA1) * grad
    second = BETA2 * second + (1.0 - BETA2) * grad * grad
    first_hat = first / (1.0 - BETA1**STEP)
    second_hat = second / (1.0 - BETA2**STEP)
    weight = weight - RATE * (first_hat / (jnp.sqrt(second_hat) + EPS_ADAM) + DECAY * weight)
    return (weight, first, second)


def gather_weights(conv_weight, gates_vec, chan_vec):
    col_block = lax.all_gather(conv_weight.astype(jnp.bfloat16), "fsdp", axis=1, tiled=True)
    kernel, gains, chans = (
        lax.all_gather(col_block, "space", axis=0, tiled=True),
        lax.all_gather(gates_vec.astype(jnp.bfloat16), "space", axis=1, tiled=True),
        lax.all_gather(chan_vec.astype(jnp.bfloat16), "space", axis=1, tiled=True),
    )
    inputs_n = kernel.shape[0] // 25
    gates_n = kernel.shape[1]
    flipped = (
        kernel.reshape(25, inputs_n, gates_n).transpose(0, 2, 1).reshape(25 * gates_n, inputs_n)
    )
    return (kernel, flipped, gains.astype(jnp.float32), chans.astype(jnp.float32))


def lifted_patches(joined):
    rows, cols = (joined.shape[1], joined.shape[2])
    padded = with_halo(joined, (("space", 1),), 2)
    padded = jnp.pad(padded, ((0, 0), (0, 0), (2, 2), (0, 0)))
    pieces = [padded[:, a : a + rows, b : b + cols, :] for a in range(5) for b in range(5)]
    return jnp.concatenate(pieces, -1).reshape(-1, 25 * joined.shape[3])


def spread_back(delta, flipped):
    rows, cols = (delta.shape[1], delta.shape[2])
    padded = with_halo(delta, (("space", 1),), 2)
    padded = jnp.pad(padded, ((0, 0), (0, 0), (2, 2), (0, 0)))
    pieces = [
        padded[:, 4 - a : 4 - a + rows, 4 - b : 4 - b + cols, :] for a in range(5) for b in range(5)
    ]
    stacked = jnp.concatenate(pieces, -1).reshape(-1, 25 * delta.shape[3])
    result = jnp.dot(stacked, flipped, preferred_element_type=jnp.float32)
    return result.reshape(delta.shape[0], rows, cols, -1)


def time_major(array):
    return jnp.moveaxis(array, 1, 0)


def forward(weights, seq, goal, chosen, inside, count, hweight):
    kernel, flipped, gains, chans = weights
    streams, nframes, rows, cols = seq.shape
    width = chans.shape[1]
    valid = inside[:, :, None, None]

    def forward_frame(carry, inputs):
        hidden, cell = carry
        pixels, target, picked = inputs
        lifted = (pixels[..., None] * chans[0] + chans[1]) * valid
        joined = jnp.concatenate([lifted, hidden], -1).astype(jnp.bfloat16)
        patches = lifted_patches(joined)
        pre = jnp.dot(patches, kernel, preferred_element_type=jnp.float32).reshape(
            streams, rows, cols, GROUPS, -1
        )
        weighted = pre * valid[..., None]
        first, second = lax.psum(
            (jnp.sum(weighted, axis=(1, 2, 4)), jnp.sum(weighted * pre, axis=(1, 2, 4))), "space"
        )
        centre = first / count[:, None]
        scale = lax.rsqrt(second / count[:, None] - centre * centre + EPS_NORM)
        normed = ((pre - centre[:, None, None, :, None]) * scale[:, None, None, :, None]).reshape(
            streams, rows, cols, 4 * width
        )
        gates = normed * gains[0] + gains[1]
        hidden_new, cell_new, output = cell_head(gates, cell, valid, chans[2])
        error = output - target
        sse = jnp.sum(picked * (error * error)[..., None], axis=(0, 1, 2))
        slope = 2.0 * error * jnp.sum(picked * hweight, axis=-1)
        return ((hidden_new, cell_new), (sse, (patches, normed, scale, cell, gates, slope)))

    zeros = jnp.zeros((streams, rows, cols, width), jnp.float32)
    (hidden, cell), (sse, kept) = lax.scan(
        forward_frame, (zeros, zeros), (time_major(seq), time_major(goal), time_major(chosen))
    )
    return (hidden, cell, jnp.sum(sse, axis=0), kept)


def backward(weights, kept, seq, inside, count):
    kernel, flipped, gains, chans = weights
    patches, normed, scale, cells, gates, slope = kept
    streams, nframes, rows, cols = seq.shape
    width = chans.shape[1]
    valid = inside[:, :, None, None]

    def cell_part(gate_vals, cell_prev, head_w):
        return cell_head(gate_vals, cell_prev, valid, head_w)

    def backward_frame(carry, inputs):
        d_hidden, d_cell, d_gain, d_bias, d_head, d_lift_w, d_lift_b = carry
        normed_t, scale_t, cell_prev, gates_t, slope_t, pixels = inputs
        unused, pull = jax.vjp(cell_part, gates_t, cell_prev, chans[2])
        d_gates, d_cell_prev, d_head_t = pull((d_hidden, d_cell, slope_t))
        d_normed = (d_gates * gains[0]).reshape(streams, rows, cols, GROUPS, -1)
        grouped = normed_t.reshape(streams, rows, cols, GROUPS, -1)
        masked = d_normed * valid[..., None]
        first, second = lax.psum(
            (jnp.sum(masked, axis=(1, 2, 4)), jnp.sum(masked * grouped, axis=(1, 2, 4))), "space"
        )
        first = (first / count[:, None])[:, None, None, :, None]
        second = (second / count[:, None])[:, None, None, :, None]
        d_pre = (
            scale_t[:, None, None, :, None]
            * (d_normed - first - grouped * second)
            * valid[..., None]
        )
        d_pre = d_pre.reshape(streams, rows, cols, -1).astype(jnp.bfloat16)
        d_joined = spread_back(d_pre, flipped)
        d_lifted = d_joined[..., :width] * valid
        carry_new = (
            d_joined[..., width:],
            d_cell_prev,
            d_gain + jnp.sum(d_gates * normed_t, axis=(0, 1, 2)),
            d_bias + jnp.sum(d_gates, axis=(0, 1, 2)),
            d_head + d_head_t,
            d_lift_w + jnp.sum(d_lifted * pixels[..., None], axis=(0, 1, 2)),
            d_lift_b + jnp.sum(d_lifted, axis=(0, 1, 2)),
        )
        return (carry_new, d_pre)

    zeros = jnp.zeros((streams, rows, cols, width), jnp.float32)
    wide_zero = jnp.zeros((4 * width,), jnp.float32)
    narrow_zero = jnp.zeros((width,), jnp.float32)
    start = (zeros, zeros, wide_zero, wide_zero, narrow_zero, narrow_zero, narrow_zero)
    final, d_pre_all = lax.scan(
        backward_frame, start, (normed, scale, cells, gates, slope, time_major(seq)), reverse=True
    )
    d_kernel = lax.dot_general(
        patches.reshape(-1, patches.shape[-1]),
        d_pre_all.reshape(-1, 4 * width),
        (((0,), (0,)), ((), ())),
        preferred_element_type=jnp.float32,
    )
    d_gains = jnp.stack([final[2], final[3]])
    d_chans = jnp.stack([final[5], final[6], final[4]])
    return (d_kernel, d_gains, d_chans)


def reduce_grads(d_kernel, d_gains, d_chans):
    col_part = lax.psum_scatter(d_kernel, "fsdp", scatter_dimension=1, tiled=True)
    kernel_part, gains_part, chans_part = (
        lax.psum_scatter(col_part, "space", scatter_dimension=0, tiled=True),
        lax.psum_scatter(d_gains, "space", scatter_dimension=1, tiled=True),
        lax.psum_scatter(d_chans, "space", scatter_dimension=1, tiled=True),
    )
    gains_part, chans_part = lax.psum((gains_part, chans_part), "fsdp")
    return (kernel_part, gains_part, chans_part)


def per_device(
    frames,
    targets,
    sizes,
    horizon,
    conv_weight,
    conv_m,
    conv_v,
    gates_vec,
    gates_m,
    gates_v,
    chan_vec,
    chan_m,
    chan_v,
):
    micro, streams, nframes, rows, cols = frames.shape
    width = chan_vec.shape[1] * lax.axis_size("space")
    total_rows = rows * lax.axis_size("space")
    row_ids = lax.axis_index("space") * rows + jnp.arange(rows, dtype=jnp.int32)
    inside = (row_ids[None, None, :] >= total_rows - sizes[:, :, None]).astype(jnp.float32)
    select = (horizon[..., None] == jnp.arange(HOR, dtype=jnp.int32)).astype(jnp.float32) * inside[
        :, :, None, :, None, None
    ]
    counts = lax.psum(jnp.sum(select, axis=(0, 1, 2, 3, 4)), ("space", "fsdp"))
    hweight = 1.0 / (HOR * jnp.maximum(counts, 1.0))
    group_count = sizes.astype(jnp.float32) * (cols * (4 * width // GROUPS))
    held = gather_weights(conv_weight, gates_vec, chan_vec)
    sse_total = jnp.zeros((HOR,), jnp.float32)
    summed = None
    for batch in range(micro):
        hidden, cell, sse, kept = forward(
            held,
            frames[batch],
            targets[batch],
            select[batch],
            inside[batch],
            group_count[batch],
            hweight,
        )
        sse_total = sse_total + sse
        grads = backward(held, kept, frames[batch], inside[batch], group_count[batch])
        summed = grads if summed is None else jax.tree.map(jnp.add, summed, grads)
    summed = reduce_grads(*summed)
    kernel_grad, gains_grad, chans_grad = summed
    leading = (lax.axis_index("fsdp") == 0).astype(jnp.float32)
    squares = jnp.sum(kernel_grad * kernel_grad) + leading * (
        jnp.sum(gains_grad * gains_grad) + jnp.sum(chans_grad * chans_grad)
    )
    sse_total, squares = lax.psum((sse_total, squares), ("space", "fsdp"))
    loss = jnp.sum(sse_total * hweight)
    norm = jnp.sqrt(squares)
    factor = jnp.minimum(1.0, CLIP / (norm + 1e-06))
    conv_new, conv_m_new, conv_v_new = adam_update(
        conv_weight, conv_m, conv_v, kernel_grad * factor
    )
    gates_new, gates_m_new, gates_v_new = adam_update(
        gates_vec, gates_m, gates_v, gains_grad * factor
    )
    chan_new, chan_m_new, chan_v_new = adam_update(chan_vec, chan_m, chan_v, chans_grad * factor)
    return (
        loss,
        norm,
        conv_new,
        conv_m_new,
        conv_v_new,
        gates_new,
        gates_m_new,
        gates_v_new,
        chan_new,
        chan_m_new,
        chan_v_new,
        hidden,
        cell,
    )


MESH = pl.DeviceIdType.MESH
F32 = jnp.float32
BF16 = jnp.bfloat16
TAPS = 25


def low(v):
    return v.astype(BF16).astype(F32)


def dot(a, b):
    return jnp.dot(a, b, preferred_element_type=F32)


def dot_nt(a, b):
    return lax.dot_general(a, b, (((1,), (1,)), ((), ())), preferred_element_type=F32)


def step_kernel(
    geo,
    frames_in,
    targets_in,
    horizon_in,
    sizes_in,
    gates_in,
    chan_in,
    w_ref,
    m_ref,
    v_ref,
    grad,
    wf,
    m_out,
    v_out,
    small_ref,
    h_ref,
    c_ref,
    frames_ref,
    targets_ref,
    horizon_ref,
    sizes_ref,
    gates_ref,
    chan_ref,
    stage,
    wr,
    wl,
    wh,
    wht,
    tiles,
    pix,
    cols,
    xb,
    sa,
    sb,
    pre1,
    save,
    h1,
    yrow,
    dst,
    dhp,
    dhy,
    dhr,
    d_own,
    dall,
    dt,
    ht,
    hr,
    xt,
    ps,
    vt,
    vf,
    vs,
    qf,
    qs,
    in_sem,
    w_sem,
    local_sem,
    sp_send,
    sp_recv,
    wsend,
    wrecv,
    wfs,
    wfr,
    f_send,
    f_recv,
):
    S, F, R, rows, PX = geo
    width = 8 * 32
    s, f = lax.axis_index("space"), lax.axis_index("fsdp")
    xx, cc = f // 2, lax.rem(f, 2)
    f_x, f_c, f_d = (1 - xx) * 2 + cc, xx * 2 + 1 - cc, (1 - xx) * 2 + 1 - cc
    fpeers = (f_x, f_c, f_d)
    pending = []

    def ahead(k):
        return lax.rem(s + k, S)

    def behind(k):
        return lax.rem(s - k + S, S)

    def only(when, do):
        if when is None:
            do()
        else:
            pl.when(when)(do)

    def copy_to(src, dst_, ssem, rsem, dev, when=None):
        cp = pltpu.make_async_remote_copy(
            src_ref=src, dst_ref=dst_, send_sem=ssem, recv_sem=rsem,
            device_id=dev, device_id_type=MESH,
        )
        pending.append((cp, when))
        return cp

    def send(src, dst_, ssem, rsem, dev, when=None):
        cp = copy_to(src, dst_, ssem, rsem, dev, when)
        only(when, cp.start)

    def landing(slot, rsem):
        return pltpu.make_async_remote_copy(
            src_ref=slot, dst_ref=slot, send_sem=rsem, recv_sem=rsem,
            device_id=(s, f_c), device_id_type=MESH,
        )

    def arrived(slot, rsem, when=None):
        only(when, landing(slot, rsem).wait_recv)

    barrier = pltpu.get_barrier_semaphore()
    for k in range(1, S):
        pl.semaphore_signal(barrier, inc=1, device_id=(ahead(k), f), device_id_type=MESH)
    for p in fpeers:
        pl.semaphore_signal(barrier, inc=1, device_id=(s, p), device_id_type=MESH)
    small_ins = []
    for n, (src, held) in enumerate(
        (
            (frames_in, frames_ref), (targets_in, targets_ref), (horizon_in, horizon_ref),
            (sizes_in, sizes_ref), (gates_in, gates_ref), (chan_in, chan_ref),
        )
    ):
        small_ins.append(pltpu.make_async_copy(src, held, in_sem.at[n]))
        small_ins[-1].start()
    base = lax.rem(s * R, 2 * width)
    zero_rows = jnp.zeros((2 * width, wf.shape[1]), F32)
    wf[0 : 2 * width, :] = zero_rows
    wf[wf.shape[0] - 2 * width :, :] = zero_rows
    get_w = []
    for q in range(4):
        own_w = wf.at[pl.ds(pl.multiple_of(base + R // 4 * q, 16), R // 4), :]
        get_w.append(
            pltpu.make_async_copy(w_ref.at[R // 4 * q : R // 4 * (q + 1), :], own_w, w_sem.at[q])
        )
        get_w[-1].start()

    for cp in small_ins:
        cp.wait()

    def line(ref):
        parts = [
            ref[m, 0, t, r : r + 1, :].astype(F32)
            for t in range(2) for r in range(2) for m in range(2)
        ]
        return jnp.concatenate(parts, axis=1)

    lane128 = lax.broadcasted_iota(jnp.int32, (1, 128), 1)
    tall = jnp.where(lax.rem(lane128 // 16, 2) == 0, sizes_ref[0:1, 0:1], sizes_ref[0:1, 1:2])
    chans = [chan_ref[q : q + 1, :] for q in range(3)] + [jnp.zeros((1, 32), F32)]
    tiles[f, s] = jnp.concatenate(
        [
            line(frames_ref), line(targets_ref), line(horizon_ref), gates_ref[...],
            jnp.concatenate(chans, axis=1), tall.astype(F32), jnp.zeros((1, 128), F32),
        ],
        axis=0,
    )
    pl.semaphore_wait(barrier, S - 1 + 3)

    for k in range(1, S):
        send(tiles.at[f, s], tiles.at[f, s], sp_send.at[0, k], sp_recv.at[0, k], (ahead(k), f))

    def holds(src, kind, i):
        lo = 512 * i + 256 * kind
        if all((q * R) % 512 + R > lo and (q * R) % 512 < lo + 256 for q in range(S)):
            return None
        first = lax.rem(src * R, 512)
        return (lo < first + R) & (lo + 256 > first)

    def stage_slot(kind, i):
        for j in range(2):
            r0 = 512 * i + 256 * kind + 128 * j
            block = wf[r0 : r0 + 128, :].T.astype(BF16)
            stage[kind, i, j] = block.reshape(8, 32, 128)

    def send_slot(kind, i):
        when = holds(s, kind, i)
        for k in range(1, S):
            to = ahead(k)
            send(
                stage.at[kind, i, :, to], wr.at[s, kind, i, :, f],
                wsend.at[kind, i, k], wrecv.at[kind, i, k], (to, f), when,
            )

    for i, q in ((0, (0,)), (1, (1,)), (2, (2, 3)), (3, ())):
        for n in q:
            get_w[n].wait()
        stage_slot(0, i)
        send_slot(0, i)
    stage_slot(1, 0)
    stage_slot(1, 1)
    for i in range(4):
        wr[s, 0, i, :, f] = stage[0, i, :, s]

    for k in range(1, S):
        arrived(tiles.at[f, behind(k)], sp_recv.at[0, k])
    for n, p in enumerate(fpeers):
        send(tiles.at[f], tiles.at[f], f_send.at[0, n], f_recv.at[0, n], (s, p))

    lane = lax.broadcasted_iota(jnp.int32, (1, PX), 1)
    row_of = lane // 32
    micro_of = lax.rem(lane // 16, 2)
    col_of = lax.rem(lane, 16)

    def build_pix(p):
        for t in range(2):
            halves = []
            for k in range(4):
                left = tiles[p, 2 * k][:, t * 64 : t * 64 + 64]
                right = tiles[p, 2 * k + 1][:, t * 64 : t * 64 + 64]
                halves.append(jnp.concatenate([left, right], axis=1))
            whole = jnp.concatenate(halves, axis=1)
            within = (row_of.astype(F32) >= rows - whole[6:7, :]).astype(F32)
            sub = lax.broadcasted_iota(jnp.int32, (8, PX), 0)
            pix[p, t] = jnp.where(sub == 7, within, whole)

    build_pix(f)

    sub32 = lax.broadcasted_iota(jnp.int32, (32, 128), 0)
    lane32 = lax.broadcasted_iota(jnp.int32, (32, 128), 1)

    def column(row, first):
        picked = jnp.where(lane32 == sub32 + first, row, 0.0)
        return low(jnp.sum(picked, axis=1, keepdims=True))

    for g in range(4):
        at = 2 * g + s // 4
        off = 32 * lax.rem(s, 4)
        for q in range(2):
            cols[q, 32 * g : 32 * g + 32, :] = jnp.broadcast_to(
                column(tiles[f, at][3 + q : 4 + q, :], off), (32, 128)
            )
    cols[2, 0:32, :] = jnp.broadcast_to(column(tiles[f, s][5:6, :], 64), (32, 128))
    for k in range(8):
        row5 = tiles[f, k][5:6, :]
        for q in range(2):
            cols[3 + q, 32 * k : 32 * k + 32, :] = jnp.broadcast_to(
                column(row5, 32 * q), (32, 128)
            )

    gain, shift, head = cols[0, 0:128, 0:1], cols[1, 0:128, 0:1], cols[2, 0:32, 0:1]

    def lifted(pixels, within):
        return ((pixels * cols[3, :, 0:1] + cols[4, :, 0:1]) * within).astype(BF16)

    inside = pix[f, 0, 7:8, :]

    def relay(kind):
        def first_hop(i, k):
            src = behind(k)
            when = holds(src, kind, i)
            block = wr.at[src, kind, i, :, f]
            to_x = copy_to(block, block, wfs.at[kind, i, k, 0], wfr.at[kind, i, k, 0], (s, f_x), when)
            to_c = copy_to(block, block, wfs.at[kind, i, k, 1], wfr.at[kind, i, k, 1], (s, f_c), when)
            here = landing(block, wrecv.at[kind, i, k]) if k > 0 else None

            def hop():
                if k > 0:
                    here.wait_recv()
                to_x.start()
                to_c.start()

            only(when, hop)

        def second_hop(i, k):
            src = behind(k)
            when = holds(src, kind, i)
            block = wr.at[src, kind, i, :, f_x]
            to_c = copy_to(block, block, wfs.at[kind, i, k, 2], wfr.at[kind, i, k, 2], (s, f_c), when)
            here = landing(block, wfr.at[kind, i, k, 0])

            def hop():
                here.wait_recv()
                to_c.start()

            only(when, hop)

        for i in range(4):
            for k in range(S):
                first_hop(i, k)
            if kind == 0 and i > 0:
                send_slot(1, i - 1)
            if kind == 0 and i == 3:
                send_slot(1, 3)
            if i > 0:
                for k in range(S):
                    second_hop(i - 1, k)
        for k in range(S):
            second_hop(3, k)
        for i in range(4):
            for k in range(S):
                src = behind(k)
                when = holds(src, kind, i)
                own_c = landing(wr.at[src, kind, i, :, f_c], wfr.at[kind, i, k, 1])
                far_c = landing(wr.at[src, kind, i, :, f_d], wfr.at[kind, i, k, 2])

                def both():
                    own_c.wait_recv()
                    far_c.wait_recv()

                only(when, both)

    def merge(kind, out):
        for tap in range(TAPS):
            lo = 512 * tap + 256 * kind
            total = None
            for sp in range(S):
                if sp * R < lo + 256 and sp * R + R > lo:
                    part = wr[sp, kind, tap - (sp * R) // 512]
                    total = part if total is None else total + part
            total = total.reshape(2, 128, 128)
            a, b = tap // 5, tap % 5
            out[128 * a : 128 * a + 128, 256 * b : 256 * b + 128] = total[0]
            out[128 * a : 128 * a + 128, 256 * b + 128 : 256 * b + 256] = total[1]

    cmask = [
        ((col_of + (b - 2) >= 0) & (col_of + (b - 2) < 16)).astype(F32) for b in range(5)
    ]
    rmask = [
        ((row_of + (a - 2) >= 0) & (row_of + (a - 2) < rows)).astype(F32) for a in range(5)
    ]

    def slide(v, d):
        if d == 0:
            return v
        parts = [
            pltpu.roll(v[:, q : q + 128], (-d) % 128, 1) for q in range(0, v.shape[1], 128)
        ]
        return jnp.concatenate(parts, axis=1) * cmask[d + 2]

    def conv(weights):
        sa[...] = dot(weights[...], xb[...]).reshape(5, 128, PX)
        out = sa[2]
        for a in (0, 1, 3, 4):
            out = out + pltpu.roll(sa[a], (-32 * (a - 2)) % PX, 1) * rmask[a]
        return out

    def slid_lift(t):
        line = jnp.concatenate([pix[f, t, 0:1, :], inside], axis=0)
        for b in range(5):
            moved = slide(line, b - 2)
            xb[256 * b : 256 * b + 256, :] = lifted(moved[0:1], moved[1:2])

    count = pix[f, 0, 6:7, :] * (16.0 * 32.0)

    def per_stream(v):
        first = jnp.sum(jnp.where(micro_of == 0, v, 0.0), axis=1, keepdims=True)
        second = jnp.sum(jnp.where(micro_of == 0, 0.0, v), axis=1, keepdims=True)
        return jnp.where(micro_of == 0, first, second)

    def cell_forward(t, pre, cell_prev):
        groups = [pre[32 * g : 32 * g + 32, :] for g in range(4)]
        sums = [
            jnp.sum(v * inside, axis=0, keepdims=True) for v in groups
        ] + [jnp.sum(v * inside * v, axis=0, keepdims=True) for v in groups]
        sums = per_stream(jnp.concatenate(sums, axis=0)) / count
        centre = sums[0:4]
        scale = lax.rsqrt(sums[4:8] - centre * centre + EPS_NORM)
        acts = []
        for g in range(4):
            normed = (groups[g] - centre[g : g + 1]) * scale[g : g + 1]
            save[t, 0, 32 * g : 32 * g + 32, :] = normed
            z = normed * gain[32 * g : 32 * g + 32] + shift[32 * g : 32 * g + 32]
            act = jnp.tanh(z) if g == 3 else 1.0 / (1.0 + jnp.exp(-z))
            save[t, 1, 32 * g : 32 * g + 32, :] = act
            acts.append(act)
        i, fo, o, cand = acts
        cell = i * cand * inside if cell_prev is None else (fo * cell_prev + i * cand) * inside
        tanh_c = jnp.tanh(cell)
        hidden = o * tanh_c * inside
        save[t, 2, 0:8, :] = jnp.concatenate([scale, scale], axis=0)
        save[t, 2, 32:64, :] = cell
        save[t, 2, 64:96, :] = tanh_c
        save[t, 2, 96:128, :] = hidden
        yrow[s, t : t + 1, :] = jnp.sum(hidden * head, axis=0, keepdims=True)
        return hidden, cell

    moments = [
        pltpu.make_async_copy(m_ref, m_out, in_sem.at[6]),
        pltpu.make_async_copy(v_ref, v_out, in_sem.at[7]),
    ]
    for cp in moments:
        cp.start()
    stage_slot(1, 2)
    stage_slot(1, 3)
    for i in range(4):
        wr[s, 1, i, :, f] = stage[1, i, :, s]
    slid_lift(0)
    relay(0)
    merge(0, wl)
    hidden0, cell0 = cell_forward(0, conv(wl), None)
    mine = pl.ds(pl.multiple_of(32 * s, 32), 32)
    h1[f, mine, :] = hidden0.astype(BF16)
    for k in range(1, S):
        send(h1.at[f, mine, :], h1.at[f, mine, :], sp_send.at[1, k], sp_recv.at[1, k], (ahead(k), f))

    relay(1)
    slid_lift(1)
    pre1[...] = conv(wl)
    merge(1, wh)
    for a in range(5):
        for b in range(5):
            block = wh[128 * a : 128 * a + 128, 256 * b : 256 * b + 256]
            wht[256 * a : 256 * a + 256, 128 * b : 128 * b + 128] = block.astype(F32).T.astype(BF16)
    for k in range(1, S):
        their = pl.ds(pl.multiple_of(32 * behind(k), 32), 32)
        arrived(h1.at[f, their, :], sp_recv.at[1, k])
    send(h1.at[f], h1.at[f], f_send.at[1, 0], f_recv.at[1, 0], (s, f_x))
    send(h1.at[f], h1.at[f], f_send.at[1, 1], f_recv.at[1, 1], (s, f_c))
    hidden_in = h1[f].astype(F32)
    for b in range(5):
        xb[256 * b : 256 * b + 256, :] = slide(hidden_in, b - 2).astype(BF16)
    pre1[...] = pre1[...] + conv(wh)
    hidden1, cell1 = cell_forward(1, pre1[...], cell0)
    for k in range(1, S):
        send(yrow.at[s], yrow.at[s], sp_send.at[2, k], sp_recv.at[2, k], (ahead(k), f))

    for n, p in enumerate(fpeers):
        arrived(tiles.at[p], f_recv.at[0, n])
    for p in fpeers:
        build_pix(p)
    weight_rows = []
    for k in range(HOR):
        total = None
        for p in range(F):
            for t in range(2):
                picked = jnp.where(pix[p, t, 2:3, :] == float(k), pix[p, t, 7:8, :], 0.0)
                total = picked if total is None else total + picked
        counted = jnp.sum(total, axis=1, keepdims=True)
        weight_rows.append(1.0 / (HOR * jnp.maximum(counted, 1.0)))
    state = jnp.concatenate([hidden1, cell1, hidden1, cell1], axis=0).T
    state = state.reshape(rows // 2, 2, 2, 16, 128)
    ht[...] = jnp.where(
        lax.broadcasted_iota(jnp.int32, (rows // 2, 16, 128), 2) < 64,
        state[:, 0, 1], state[:, 1, 1],
    )
    for k in range(1, S):
        send(ht.at[ahead(k)], hr.at[s], sp_send.at[6, k], sp_recv.at[6, k], (ahead(k), f))
    hr[s] = ht[s]

    for k in range(1, S):
        arrived(yrow.at[behind(k)], sp_recv.at[2, k])
    ysum = yrow[0]
    for k in range(1, S):
        ysum = ysum + yrow[k]
    slopes, sse = [], [None] * HOR
    for t in range(2):
        err = ysum[t : t + 1] - pix[f, t, 1:2, :]
        which = pix[f, t, 2:3, :]
        hw = jnp.zeros((1, PX), F32)
        for k in range(HOR):
            chosen = jnp.where(which == float(k), inside, 0.0)
            hw = hw + chosen * weight_rows[k]
            part = chosen * (err * err)
            sse[k] = part if sse[k] is None else sse[k] + part
        slopes.append(2.0 * err * hw)
    sse = [jnp.sum(v, axis=1, keepdims=True) for v in sse]

    def cell_backward(t, d_hidden, d_cell, cell_prev):
        slope = slopes[t]
        i, fo = save[t, 1, 0:32, :], save[t, 1, 32:64, :]
        o, cand = save[t, 1, 64:96, :], save[t, 1, 96:128, :]
        tanh_c, hidden = save[t, 2, 64:96, :], save[t, 2, 96:128, :]
        dh = slope * head
        if d_hidden is not None:
            dh = dh + d_hidden
        dh = dh * inside
        d_o = dh * tanh_c
        dc = dh * o * (1.0 - tanh_c * tanh_c)
        if d_cell is not None:
            dc = dc + d_cell
        dc = dc * inside
        d_f = jnp.zeros_like(dc) if cell_prev is None else dc * cell_prev
        raw = [
            dc * cand * i * (1.0 - i),
            d_f * fo * (1.0 - fo),
            d_o * o * (1.0 - o),
            dc * i * (1.0 - cand * cand),
        ]
        scale = save[t, 2, 0:8, :]
        d_head = jnp.sum(hidden * slope, axis=1, keepdims=True)
        d_gain, d_shift, dn, sums = [], [], [], [[], []]
        for g in range(4):
            normed = save[t, 0, 32 * g : 32 * g + 32, :]
            d_gain.append(jnp.sum(raw[g] * normed, axis=1, keepdims=True))
            d_shift.append(jnp.sum(raw[g], axis=1, keepdims=True))
            v = raw[g] * gain[32 * g : 32 * g + 32]
            dn.append(v)
            sums[0].append(jnp.sum(v * inside, axis=0, keepdims=True))
            sums[1].append(jnp.sum(v * inside * normed, axis=0, keepdims=True))
        sums = per_stream(jnp.concatenate(sums[0] + sums[1], axis=0)) / count
        for g in range(4):
            normed = save[t, 0, 32 * g : 32 * g + 32, :]
            d_pre = scale[g : g + 1] * (dn[g] - sums[g : g + 1] - normed * sums[4 + g : 5 + g])
            d_own[t, g] = (d_pre * inside).astype(BF16)
        return (
            dc * fo,
            d_head,
            jnp.concatenate(d_gain, axis=0),
            jnp.concatenate(d_shift, axis=0),
        )

    def share_gates(t):
        for n, p in enumerate(fpeers):
            send(d_own.at[t, p], dall.at[t, f, s], f_send.at[3 + t, n], f_recv.at[3 + t, n], (s, p))
        own = pltpu.make_async_copy(d_own.at[t, f], dall.at[t, f, s], local_sem.at[3 + t])
        own.start()
        return own

    z, y = s // 2, lax.rem(s, 2)
    across = 2 * z + 1 - y

    def line_peer(k):
        return lax.rem(z + k, 4) * 2 + y

    def line_source(k):
        return lax.rem(z + 4 - k, 4) * 2 + y

    def share_blocks(t, own):
        own.wait()
        for n, p in enumerate(fpeers):
            arrived(dall.at[t, p, s], f_recv.at[3 + t, n])
        block = dall.at[t, :, s]
        for k in (2, 3, 1):
            send(block, block, sp_send.at[4 + t, k], sp_recv.at[4 + t, k], (line_peer(k), f))
        send(block, block, sp_send.at[4 + t, 0], sp_recv.at[4 + t, 0], (across, f))

    def relay_blocks(t):
        for k in (1, 3, 2):
            block = dall.at[t, :, line_source(k)]
            arrived(block, sp_recv.at[4 + t, k])
            send(block, block, sp_send.at[4 + t, 4 + k], sp_recv.at[4 + t, 4 + k], (across, f))

    def gathered(t):
        arrived(dall.at[t, :, across], sp_recv.at[4 + t, 0])
        for k in range(1, 4):
            there = lax.rem(z + 4 - k, 4) * 2 + 1 - y
            arrived(dall.at[t, :, there], sp_recv.at[4 + t, 4 + k])
        for p in range(F):
            block = dall[t, p].reshape(256, PX)
            dt[p] = block.astype(F32).T.astype(BF16)

    d_cell0, d_head1, d_gain1, d_shift1 = cell_backward(1, None, None, cell0)
    own_d1 = share_gates(1)

    d1 = d_own[1].reshape(128, PX).astype(F32)
    for b in range(5):
        dst[128 * b : 128 * b + 128, :] = slide(d1, 2 - b).astype(BF16)
    sb[...] = dot(wht[...], dst[...]).reshape(5, 256, PX)
    dh = sb[2]
    for a in (0, 1, 3, 4):
        dh = dh + pltpu.roll(sb[a], (32 * (a - 2)) % PX, 1) * rmask[4 - a]
    dhp[...] = dh
    steps = (2, 1, 3, 0)

    def part_of(zz, yy):
        return pl.ds(pl.multiple_of(32 * (2 * zz + yy), 32), 32)

    for k in steps:
        zz = lax.rem(z + k, 4)
        send(
            dhp.at[part_of(zz, 1 - y), :], dhy.at[k], sp_send.at[3, k], sp_recv.at[3, k], (across, f)
        )
    for k in steps:
        zz = lax.rem(z + k, 4)
        arrived(dhy.at[k], sp_recv.at[3, k])
        both = dhp[part_of(zz, y), :] + dhy[k]
        if k == 0:
            dhr[z] = both
        else:
            dhy[k] = both
            send(
                dhy.at[k], dhr.at[z], sp_send.at[3, 4 + k], sp_recv.at[3, 4 + k], (line_peer(k), f)
            )
    share_blocks(1, own_d1)

    first_tap = (s * R) // 512

    def tap_inputs(n, carry):
        p, i = n // 4, lax.rem(n, 4)
        tap = first_tap + i
        da, db = tap // 5 - 2, lax.rem(tap, 5) - 2
        back = lax.rem(2 * PX - 32 * da - db, PX)
        ok = (row_of + da >= 0) & (row_of + da < rows) & (col_of + db >= 0) & (col_of + db < 16)
        ok = ok.astype(F32)
        for t in range(2):
            moved = pltpu.roll(pix[p, t], back, 1)
            xt[t, p, i] = lifted(moved[0:1], moved[7:8] * ok)
        return carry

    arrived(h1.at[f_x], f_recv.at[1, 0])
    send(h1.at[f_x], h1.at[f_x], f_send.at[2, 0], f_recv.at[2, 0], (s, f_c))
    lax.fori_loop(0, 4 * F, tap_inputs, 0)
    arrived(h1.at[f_c], f_recv.at[1, 1])
    arrived(h1.at[f_d], f_recv.at[2, 0])

    def tap_hidden(n, carry):
        p, i = n // 4, lax.rem(n, 4)
        tap = first_tap + i
        da, db = tap // 5 - 2, lax.rem(tap, 5) - 2
        back = lax.rem(2 * PX - 32 * da - db, PX)
        ok = (row_of + da >= 0) & (row_of + da < rows) & (col_of + db >= 0) & (col_of + db < 16)
        xt[2, p, i] = (pltpu.roll(h1[p].astype(F32), back, 1) * ok.astype(F32)).astype(BF16)
        return carry

    lax.fori_loop(0, 4 * F, tap_hidden, 0)

    def moved_pixels(t):
        pixels = pix[f, t, 0:1, :] * inside
        high = low(pixels)
        mid = low(pixels - high)
        rest = low(pixels - high - mid)
        four = jnp.concatenate([high, mid, rest, inside, jnp.zeros((4, PX), F32)], axis=0)
        for a in range(5):
            lines = four if a == 2 else pltpu.roll(four, (-32 * (a - 2)) % PX, 1) * rmask[a]
            for b in range(5):
                n = 8 * (5 * a + b)
                ps[t, n : n + 8, :] = slide(lines, b - 2)
        return dot_nt(d_own[t].reshape(128, PX), ps[t].astype(BF16))

    q1 = moved_pixels(1)

    for k in range(1, 4):
        arrived(dhr.at[lax.rem(z + 4 - k, 4)], sp_recv.at[3, 4 + k])
    d_hidden0 = (dhr[0] + dhr[1]) + (dhr[2] + dhr[3])
    unused, d_head0, d_gain0, d_shift0 = cell_backward(0, d_hidden0, d_cell0, None)
    own_d0 = share_gates(0)

    q = q1 + moved_pixels(0)
    total_w = jnp.zeros((128, 256), F32)
    total_b = jnp.zeros((128, 256), F32)
    for tap in range(TAPS):
        a, b = tap // 5, tap % 5
        w = wl[128 * a : 128 * a + 128, 256 * b : 256 * b + 256].astype(F32)
        n = 8 * tap
        total_w = total_w + w * (q[:, n : n + 1] + q[:, n + 1 : n + 2] + q[:, n + 2 : n + 3])
        total_b = total_b + w * q[:, n + 3 : n + 4]
    lift_w = jnp.sum(total_w, axis=0, keepdims=True)
    lift_b = jnp.sum(total_b, axis=0, keepdims=True)

    share_blocks(0, own_d0)

    lane_sq = lax.broadcasted_iota(jnp.int32, (128, 128), 1)
    d_head = jnp.concatenate(
        [d_head0 + d_head1] + sse_rows(sse), axis=0
    )
    packed = jnp.where(lane_sq == 0, d_gain0 + d_gain1, 0.0)
    packed = jnp.where(lane_sq == 1, d_shift0 + d_shift1, packed)
    packed = jnp.where(lane_sq == 2, d_head, packed)
    packed = packed.T[0:3, :]
    vt[...] = jnp.concatenate(
        [packed, lift_w[:, 0:128], lift_w[:, 128:256], lift_b[:, 0:128], lift_b[:, 128:256],
         jnp.zeros((1, 128), F32)], axis=0,
    )
    vf[f] = vt[...]
    for n, p in enumerate(fpeers):
        send(vt, vf.at[f], f_send.at[5, n], f_recv.at[5, n], (s, p))
    relay_blocks(1)
    for n, p in enumerate(fpeers):
        arrived(vf.at[p], f_recv.at[5, n])
    vs[s] = (vf[0] + vf[1]) + (vf[2] + vf[3])
    for k in range(1, S):
        send(vs.at[s], vs.at[s], sp_send.at[7, k], sp_recv.at[7, k], (ahead(k), f))

    relay_blocks(0)
    gathered(1)

    def grad_one(i, carry):
        for kind in range(2):
            total = None
            for p in range(F):
                part = dot(xt[1 + kind, p, i], dt[p])
                total = part if total is None else total + part
            grad[pl.ds(pl.multiple_of(512 * i + 256 * kind, 256), 256), :] = total
        return carry

    lax.fori_loop(0, 4, grad_one, 0)

    for k in range(1, S):
        arrived(hr.at[behind(k)], sp_recv.at[6, k])
    for k in range(S):
        for r in range(2):
            h_ref[16 * r : 16 * r + 16, 32 * k : 32 * k + 32] = hr[k, :, 64 * r : 64 * r + 32]
            c_ref[16 * r : 16 * r + 16, 32 * k : 32 * k + 32] = hr[k, :, 64 * r + 32 : 64 * r + 64]

    for k in range(1, S):
        arrived(vs.at[behind(k)], sp_recv.at[7, k])
    lane8 = lax.broadcasted_iota(jnp.int32, (8, 128), 1)
    sub8 = lax.broadcasted_iota(jnp.int32, (8, 128), 0)
    lift = vs[0]
    small_sq = jnp.zeros((8, 128), F32)
    for k in range(S):
        own_rows = jnp.where((sub8 < 2) | ((sub8 == 2) & (lane8 < 32)), vs[k], 0.0)
        small_sq = small_sq + own_rows * own_rows
        if k > 0:
            lift = lift + vs[k]
    lift = jnp.where((sub8 >= 3) & (sub8 < 7), lift, 0.0)
    small_sq = jnp.sum(small_sq + lift * lift)
    gate, half = s // 2, lax.rem(s, 2)
    d_gates = jnp.zeros((8, 128), F32)
    for k in range(4):
        turned = pltpu.roll(vs[4 * half + k], lax.rem(32 * k - 32 * gate + 128, 128), 1)
        d_gates = jnp.where((lane8 >= 32 * k) & (lane8 < 32 * k + 32), turned, d_gates)
    quarter = 32 * lax.rem(s, 4)
    upper = s // 4
    turned = pltpu.roll(lift, lax.rem(128 - quarter, 128), 1)
    line_w = jnp.where(upper == 0, turned[3:4], turned[4:5])
    line_b = jnp.where(upper == 0, turned[5:6], turned[6:7])
    line_h = vs[s][2:3, :]
    lane1 = lane8[0:1]
    d_chans = jnp.where(
        lane1 < 32, line_w,
        jnp.where(lane1 < 64, pltpu.roll(line_b, 32, 1), pltpu.roll(line_h, 64, 1)),
    )
    loss = jnp.zeros((1, 1), F32)
    for k in range(HOR):
        loss = loss + vs[s][2:3, 32 + k : 33 + k] * weight_rows[k]

    gathered(0)

    def grad_zero(i, carry):
        total = None
        for p in range(F):
            part = dot(xt[0, p, i], dt[p])
            total = part if total is None else total + part
        at = pl.ds(pl.multiple_of(512 * i, 256), 256)
        grad[at, :] = grad[at, :] + total
        return carry

    lax.fori_loop(0, 4, grad_zero, 0)

    def square(n, carry):
        v = grad[pl.ds(pl.multiple_of(base + 64 * n, 64), 64), :]
        return carry + v * v

    total = lax.fori_loop(0, R // 64, square, jnp.zeros((64, 256), F32))
    qf[f] = jnp.full((8, 128), jnp.sum(total), F32)
    for n, p in enumerate(fpeers):
        send(qf.at[f], qf.at[f], f_send.at[6, n], f_recv.at[6, n], (s, p))
    for n, p in enumerate(fpeers):
        arrived(qf.at[p], f_recv.at[6, n])
    qs[s] = (qf[0] + qf[1]) + (qf[2] + qf[3])
    for k in range(1, S):
        send(qs.at[s], qs.at[s], sp_send.at[8, k], sp_recv.at[8, k], (ahead(k), f))
    for k in range(1, S):
        arrived(qs.at[behind(k)], sp_recv.at[8, k])
    squares = qs[0]
    for k in range(1, S):
        squares = squares + qs[k]
    norm = jnp.sqrt(squares + small_sq)
    factor = jnp.minimum(1.0, CLIP / (norm + 1e-06))
    out = jnp.where(sub8 < 2, d_gates, d_chans)
    out = jnp.where(sub8 == 3, loss, out)
    out = jnp.where(sub8 == 4, norm, out)
    out = jnp.where(sub8 == 5, factor, out)
    small_ref[...] = out

    for cp in moments:
        cp.wait()
    for cp, when in pending:
        only(when, cp.wait_send)


def sse_rows(sse):
    return sse + [jnp.zeros((128 - 32 - HOR, 1), F32)]


def step_fast(
    frames, targets, sizes, horizon, conv_weight, conv_m, conv_v, gates_vec, chan_vec
):
    S, F = lax.axis_size("space"), lax.axis_size("fsdp")
    R, N = conv_weight.shape
    rows, cols = frames.shape[3] * S, frames.shape[4]
    PX = 2 * rows * cols

    VM = pltpu.VMEM
    DMA = pltpu.SemaphoreType.DMA
    geo = (S, F, R, rows, PX)
    out = pl.pallas_call(
        functools.partial(step_kernel, geo),
        out_shape=(
            VM((2048, N), F32),
            VM((2048, N), F32),
            VM((R, N), F32),
            VM((R, N), F32),
            VM((8, 128), F32),
            VM((32, 256), F32),
            VM((32, 256), F32),
        ),
        in_specs=[pl.BlockSpec(memory_space=pltpu.HBM)] * 9,
        out_specs=(pl.BlockSpec(memory_space=VM),) * 7,
        scratch_shapes=[
            VM(frames.shape, F32),
            VM(frames.shape, F32),
            VM(frames.shape, jnp.int32),
            VM((1, 2), jnp.int32),
            VM(gates_vec.shape, F32),
            VM(chan_vec.shape, F32),
            VM((2, 4, 2, 8, 32, 128), BF16),
            VM((S, 2, 4, 2, 4, 32, 128), BF16),
            VM((640, 1280), BF16),
            VM((640, 1280), BF16),
            VM((1280, 640), BF16),
            VM((F, S, 8, 128), F32),
            VM((F, 2, 8, PX), F32),
            VM((5, 256, 128), F32),
            VM((1280, PX), BF16),
            VM((5, 128, PX), F32),
            VM((5, 256, PX), F32),
            VM((128, PX), F32),
            VM((2, 3, 128, PX), F32),
            VM((F, 256, PX), BF16),
            VM((S, 8, PX), F32),
            VM((640, PX), BF16),
            VM((256, PX), F32),
            VM((4, 32, PX), F32),
            VM((4, 32, PX), F32),
            VM((2, 4, 32, PX), BF16),
            VM((2, F, S, 32, PX), BF16),
            VM((F, PX, 256), BF16),
            VM((rows // 2, cols, 128), F32),
            VM((S, cols, 128), F32),
            VM((3, F, 4, 256, PX), BF16),
            VM((2, 8 * TAPS, PX), F32),
            VM((8, 128), F32),
            VM((F, 8, 128), F32),
            VM((S, 8, 128), F32),
            VM((F, 8, 128), F32),
            VM((S, 8, 128), F32),
            DMA((8,)),
            DMA((4,)),
            DMA((6,)),
            DMA((9, S)),
            DMA((9, S)),
            DMA((2, 4, S)),
            DMA((2, 4, S)),
            DMA((2, 4, S, 3)),
            DMA((2, 4, S, 3)),
            DMA((7, 3)),
            DMA((7, 3)),
        ],
        compiler_params=pltpu.CompilerParams(
            collective_id=0, has_side_effects=True, vmem_limit_bytes=44 * 2**20
        ),
    )(
        *(
            pltpu.with_memory_space_constraint(v, pltpu.HBM)
            for v in (
                frames, targets, horizon, sizes.reshape(1, 2), gates_vec, chan_vec,
                conv_weight, conv_m, conv_v,
            )
        )
    )
    return out


def adam_kernel(
    steps,
    small_ref, h_ref, c_ref, g_ref,
    w_ref, m_ref, v_ref, gw_ref, gm_ref, gv_ref, cw_ref, cm_ref, cv_ref,
    loss_ref, norm_ref,
    wo_ref, mo_ref, vo_ref, gwo_ref, gmo_ref, gvo_ref, cwo_ref, cmo_ref, cvo_ref,
    ho_ref, co_ref,
    held, sems,
):
    factor = small_ref[5:6, 0:1]
    R = m_ref.shape[0]
    size = R // steps
    base = lax.rem(lax.axis_index("space") * R, 512)
    copies = []
    for n in range(steps):
        at = slice(size * n, size * n + size)
        moved = pl.ds(pl.multiple_of(base + size * n, 64), size)
        news = adam_update(w_ref[moved, :], m_ref[at, :], v_ref[at, :], g_ref[moved, :] * factor)
        for q, (new, out) in enumerate(zip(news, (wo_ref, mo_ref, vo_ref))):
            held[q, at, :] = new
            copy = pltpu.make_async_copy(held.at[q, at, :], out.at[at, :], sems.at[q, n])
            copy.start()
            copies.append(copy)

    def update(w, m, v, grad, outs):
        for ref, new in zip(outs, adam_update(w[...], m[...], v[...], grad * factor)):
            ref[...] = new

    loss_ref[...] = small_ref[3:4, 0:1]
    norm_ref[...] = small_ref[4:5, 0:1]
    update(gw_ref, gm_ref, gv_ref, small_ref[0:2, :], (gwo_ref, gmo_ref, gvo_ref))
    chans = [small_ref[2:3, 32 * q : 32 * q + 32] for q in range(3)]
    update(cw_ref, cm_ref, cv_ref, jnp.concatenate(chans, axis=0), (cwo_ref, cmo_ref, cvo_ref))
    for r in range(2):
        ho_ref[0, r] = h_ref[16 * r : 16 * r + 16, :]
        co_ref[0, r] = c_ref[16 * r : 16 * r + 16, :]
    for copy in copies:
        copy.wait()


def adam_step(small, hidden, cell, grad, weights, frame_shape):
    R, N = weights[0][1].shape
    steps = 5
    rows, cols = frame_shape
    vmem, any_ = pl.BlockSpec(memory_space=pltpu.VMEM), pl.BlockSpec(memory_space=pl.ANY)
    conv, gates, chan = weights
    flat = [*conv, *gates, *chan]
    shapes = [jax.ShapeDtypeStruct(v.shape, F32) for v in (*conv[1:], conv[1], *gates, *chan)]
    scalar = jax.ShapeDtypeStruct((1, 1), F32)
    state = jax.ShapeDtypeStruct((1, rows, cols, hidden.shape[1]), F32)
    out = pl.pallas_call(
        functools.partial(adam_kernel, steps),
        out_shape=(scalar, scalar, *shapes, state, state),
        in_specs=[vmem] * (4 + len(flat)),
        out_specs=(vmem, vmem, *([any_] * 3), *([vmem] * 8)),
        scratch_shapes=[pltpu.VMEM((3, R, N), F32), pltpu.SemaphoreType.DMA((3, steps))],
        compiler_params=pltpu.CompilerParams(vmem_limit_bytes=7 * 2**20),
    )(small, hidden, cell, grad, *flat)
    return (out[0].reshape(()), out[1].reshape(()), *out[2:])


def per_device_fast(
    frames, targets, sizes, horizon,
    conv_weight, conv_m, conv_v,
    gates_vec, gates_m, gates_v,
    chan_vec, chan_m, chan_v,
):
    grad, weight, first, second, small, hidden, cell = step_fast(
        frames, targets, sizes, horizon, conv_weight, conv_m, conv_v, gates_vec, chan_vec
    )
    weights = ((weight, first, second), (gates_vec, gates_m, gates_v), (chan_vec, chan_m, chan_v))
    return adam_step(small, hidden, cell, grad, weights, frames.shape[3:])


def fits(mesh, shapes):
    S, F = mesh.shape["space"], mesh.shape["fsdp"]
    frames, conv, chan = shapes
    return (
        (S, F) == (8, 4)
        and frames == (2, F, 2, 2 * S, 16)
        and conv == (TAPS * 512, 1024)
        and chan == (3, 256)
    )


def solution(mesh):
    in_specs = (
        P(None, "fsdp", None, "space", None),
        P(None, "fsdp", None, "space", None),
        P(None, "fsdp"),
        P(None, "fsdp", None, "space", None),
        P("space", "fsdp"),
        P("space", "fsdp"),
        P("space", "fsdp"),
        P(None, "space"),
        P(None, "space"),
        P(None, "space"),
        P(None, "space"),
        P(None, "space"),
        P(None, "space"),
    )
    out_specs = (
        P(),
        P(),
        P("space", "fsdp"),
        P("space", "fsdp"),
        P("space", "fsdp"),
        P(None, "space"),
        P(None, "space"),
        P(None, "space"),
        P(None, "space"),
        P(None, "space"),
        P(None, "space"),
        P("fsdp", "space", None, None),
        P("fsdp", "space", None, None),
    )

    def run(*args):
        shapes = (args[0].shape, args[4].shape, args[10].shape)
        body = per_device_fast if fits(mesh, shapes) else per_device
        return jax.shard_map(
            body, mesh=mesh, in_specs=in_specs, out_specs=out_specs, check_vma=False
        )(*args)

    return run
```

```python
import functools

import jax
import jax.numpy as jnp
from jax import lax
from jax.experimental import pallas as pl
from jax.experimental.pallas import tpu as pltpu
from jax.sharding import PartitionSpec as P

GROUPS = 32
HOR = 4
STEP = 10


EPS_NORM = 1e-05
CLIP = 0.01
RATE = 0.01
BETA1 = 0.9
BETA2 = 0.999
DECAY = 0.01
EPS_ADAM = 1e-08


def with_halo(shard, sides, width):
    for axis, dim in sides:
        count, length = (lax.axis_size(axis), shard.shape[dim])
        up = [(i, (i + 1) % count) for i in range(count - 1)]
        down = [(j, i) for i, j in up]
        last = lax.slice_in_dim(shard, length - width, length, axis=dim)
        first = lax.slice_in_dim(shard, 0, width, axis=dim)
        before = lax.ppermute(last, axis, up)
        after = lax.ppermute(first, axis, down)
        shard = jnp.concatenate([before, shard, after], axis=dim)
    return shard


def cell_head(gates, cell_prev, valid, head_w):
    width = cell_prev.shape[-1]
    gate_in = jax.nn.sigmoid(gates[..., :width])
    gate_forget = jax.nn.sigmoid(gates[..., width : 2 * width])
    gate_out = jax.nn.sigmoid(gates[..., 2 * width : 3 * width])
    candidate = jnp.tanh(gates[..., 3 * width :])
    cell_new = (gate_forget * cell_prev + gate_in * candidate) * valid
    hidden_new = gate_out * jnp.tanh(cell_new) * valid
    return (hidden_new, cell_new, jnp.sum(hidden_new * head_w, axis=-1))


def adam_update(weight, first, second, grad):
    first = BETA1 * first + (1.0 - BETA1) * grad
    second = BETA2 * second + (1.0 - BETA2) * grad * grad
    first_hat = first / (1.0 - BETA1**STEP)
    second_hat = second / (1.0 - BETA2**STEP)
    weight = weight - RATE * (first_hat / (jnp.sqrt(second_hat) + EPS_ADAM) + DECAY * weight)
    return (weight, first, second)


def gather_weights(conv_weight, gates_vec, chan_vec):
    col_block = lax.all_gather(conv_weight.astype(jnp.bfloat16), "fsdp", axis=1, tiled=True)
    kernel, gains, chans = (
        lax.all_gather(col_block, "space", axis=0, tiled=True),
        lax.all_gather(gates_vec.astype(jnp.bfloat16), "space", axis=1, tiled=True),
        lax.all_gather(chan_vec.astype(jnp.bfloat16), "space", axis=1, tiled=True),
    )
    inputs_n = kernel.shape[0] // 25
    gates_n = kernel.shape[1]
    flipped = (
        kernel.reshape(25, inputs_n, gates_n).transpose(0, 2, 1).reshape(25 * gates_n, inputs_n)
    )
    return (kernel, flipped, gains.astype(jnp.float32), chans.astype(jnp.float32))


def lifted_patches(joined):
    rows, cols = (joined.shape[1], joined.shape[2])
    padded = with_halo(joined, (("space", 1),), 2)
    padded = jnp.pad(padded, ((0, 0), (0, 0), (2, 2), (0, 0)))
    pieces = [padded[:, a : a + rows, b : b + cols, :] for a in range(5) for b in range(5)]
    return jnp.concatenate(pieces, -1).reshape(-1, 25 * joined.shape[3])


def spread_back(delta, flipped):
    rows, cols = (delta.shape[1], delta.shape[2])
    padded = with_halo(delta, (("space", 1),), 2)
    padded = jnp.pad(padded, ((0, 0), (0, 0), (2, 2), (0, 0)))
    pieces = [
        padded[:, 4 - a : 4 - a + rows, 4 - b : 4 - b + cols, :] for a in range(5) for b in range(5)
    ]
    stacked = jnp.concatenate(pieces, -1).reshape(-1, 25 * delta.shape[3])
    result = jnp.dot(stacked, flipped, preferred_element_type=jnp.float32)
    return result.reshape(delta.shape[0], rows, cols, -1)


def time_major(array):
    return jnp.moveaxis(array, 1, 0)


def forward(weights, seq, goal, chosen, inside, count, hweight):
    kernel, flipped, gains, chans = weights
    streams, nframes, rows, cols = seq.shape
    width = chans.shape[1]
    valid = inside[:, :, None, None]

    def forward_frame(carry, inputs):
        hidden, cell = carry
        pixels, target, picked = inputs
        lifted = (pixels[..., None] * chans[0] + chans[1]) * valid
        joined = jnp.concatenate([lifted, hidden], -1).astype(jnp.bfloat16)
        patches = lifted_patches(joined)
        pre = jnp.dot(patches, kernel, preferred_element_type=jnp.float32).reshape(
            streams, rows, cols, GROUPS, -1
        )
        weighted = pre * valid[..., None]
        first, second = lax.psum(
            (jnp.sum(weighted, axis=(1, 2, 4)), jnp.sum(weighted * pre, axis=(1, 2, 4))), "space"
        )
        centre = first / count[:, None]
        scale = lax.rsqrt(second / count[:, None] - centre * centre + EPS_NORM)
        normed = ((pre - centre[:, None, None, :, None]) * scale[:, None, None, :, None]).reshape(
            streams, rows, cols, 4 * width
        )
        gates = normed * gains[0] + gains[1]
        hidden_new, cell_new, output = cell_head(gates, cell, valid, chans[2])
        error = output - target
        sse = jnp.sum(picked * (error * error)[..., None], axis=(0, 1, 2))
        slope = 2.0 * error * jnp.sum(picked * hweight, axis=-1)
        return ((hidden_new, cell_new), (sse, (patches, normed, scale, cell, gates, slope)))

    zeros = jnp.zeros((streams, rows, cols, width), jnp.float32)
    (hidden, cell), (sse, kept) = lax.scan(
        forward_frame, (zeros, zeros), (time_major(seq), time_major(goal), time_major(chosen))
    )
    return (hidden, cell, jnp.sum(sse, axis=0), kept)


def backward(weights, kept, seq, inside, count):
    kernel, flipped, gains, chans = weights
    patches, normed, scale, cells, gates, slope = kept
    streams, nframes, rows, cols = seq.shape
    width = chans.shape[1]
    valid = inside[:, :, None, None]

    def cell_part(gate_vals, cell_prev, head_w):
        return cell_head(gate_vals, cell_prev, valid, head_w)

    def backward_frame(carry, inputs):
        d_hidden, d_cell, d_gain, d_bias, d_head, d_lift_w, d_lift_b = carry
        normed_t, scale_t, cell_prev, gates_t, slope_t, pixels = inputs
        unused, pull = jax.vjp(cell_part, gates_t, cell_prev, chans[2])
        d_gates, d_cell_prev, d_head_t = pull((d_hidden, d_cell, slope_t))
        d_normed = (d_gates * gains[0]).reshape(streams, rows, cols, GROUPS, -1)
        grouped = normed_t.reshape(streams, rows, cols, GROUPS, -1)
        masked = d_normed * valid[..., None]
        first, second = lax.psum(
            (jnp.sum(masked, axis=(1, 2, 4)), jnp.sum(masked * grouped, axis=(1, 2, 4))), "space"
        )
        first = (first / count[:, None])[:, None, None, :, None]
        second = (second / count[:, None])[:, None, None, :, None]
        d_pre = (
            scale_t[:, None, None, :, None]
            * (d_normed - first - grouped * second)
            * valid[..., None]
        )
        d_pre = d_pre.reshape(streams, rows, cols, -1).astype(jnp.bfloat16)
        d_joined = spread_back(d_pre, flipped)
        d_lifted = d_joined[..., :width] * valid
        carry_new = (
            d_joined[..., width:],
            d_cell_prev,
            d_gain + jnp.sum(d_gates * normed_t, axis=(0, 1, 2)),
            d_bias + jnp.sum(d_gates, axis=(0, 1, 2)),
            d_head + d_head_t,
            d_lift_w + jnp.sum(d_lifted * pixels[..., None], axis=(0, 1, 2)),
            d_lift_b + jnp.sum(d_lifted, axis=(0, 1, 2)),
        )
        return (carry_new, d_pre)

    zeros = jnp.zeros((streams, rows, cols, width), jnp.float32)
    wide_zero = jnp.zeros((4 * width,), jnp.float32)
    narrow_zero = jnp.zeros((width,), jnp.float32)
    start = (zeros, zeros, wide_zero, wide_zero, narrow_zero, narrow_zero, narrow_zero)
    final, d_pre_all = lax.scan(
        backward_frame, start, (normed, scale, cells, gates, slope, time_major(seq)), reverse=True
    )
    d_kernel = lax.dot_general(
        patches.reshape(-1, patches.shape[-1]),
        d_pre_all.reshape(-1, 4 * width),
        (((0,), (0,)), ((), ())),
        preferred_element_type=jnp.float32,
    )
    d_gains = jnp.stack([final[2], final[3]])
    d_chans = jnp.stack([final[5], final[6], final[4]])
    return (d_kernel, d_gains, d_chans)


def reduce_grads(d_kernel, d_gains, d_chans):
    col_part = lax.psum_scatter(d_kernel, "fsdp", scatter_dimension=1, tiled=True)
    kernel_part, gains_part, chans_part = (
        lax.psum_scatter(col_part, "space", scatter_dimension=0, tiled=True),
        lax.psum_scatter(d_gains, "space", scatter_dimension=1, tiled=True),
        lax.psum_scatter(d_chans, "space", scatter_dimension=1, tiled=True),
    )
    gains_part, chans_part = lax.psum((gains_part, chans_part), "fsdp")
    return (kernel_part, gains_part, chans_part)


def per_device(
    frames,
    targets,
    sizes,
    horizon,
    conv_weight,
    conv_m,
    conv_v,
    gates_vec,
    gates_m,
    gates_v,
    chan_vec,
    chan_m,
    chan_v,
):
    micro, streams, nframes, rows, cols = frames.shape
    width = chan_vec.shape[1] * lax.axis_size("space")
    total_rows = rows * lax.axis_size("space")
    row_ids = lax.axis_index("space") * rows + jnp.arange(rows, dtype=jnp.int32)
    inside = (row_ids[None, None, :] >= total_rows - sizes[:, :, None]).astype(jnp.float32)
    select = (horizon[..., None] == jnp.arange(HOR, dtype=jnp.int32)).astype(jnp.float32) * inside[
        :, :, None, :, None, None
    ]
    counts = lax.psum(jnp.sum(select, axis=(0, 1, 2, 3, 4)), ("space", "fsdp"))
    hweight = 1.0 / (HOR * jnp.maximum(counts, 1.0))
    group_count = sizes.astype(jnp.float32) * (cols * (4 * width // GROUPS))
    held = gather_weights(conv_weight, gates_vec, chan_vec)
    sse_total = jnp.zeros((HOR,), jnp.float32)
    summed = None
    for batch in range(micro):
        hidden, cell, sse, kept = forward(
            held,
            frames[batch],
            targets[batch],
            select[batch],
            inside[batch],
            group_count[batch],
            hweight,
        )
        sse_total = sse_total + sse
        grads = backward(held, kept, frames[batch], inside[batch], group_count[batch])
        summed = grads if summed is None else jax.tree.map(jnp.add, summed, grads)
    summed = reduce_grads(*summed)
    kernel_grad, gains_grad, chans_grad = summed
    leading = (lax.axis_index("fsdp") == 0).astype(jnp.float32)
    squares = jnp.sum(kernel_grad * kernel_grad) + leading * (
        jnp.sum(gains_grad * gains_grad) + jnp.sum(chans_grad * chans_grad)
    )
    sse_total, squares = lax.psum((sse_total, squares), ("space", "fsdp"))
    loss = jnp.sum(sse_total * hweight)
    norm = jnp.sqrt(squares)
    factor = jnp.minimum(1.0, CLIP / (norm + 1e-06))
    conv_new, conv_m_new, conv_v_new = adam_update(
        conv_weight, conv_m, conv_v, kernel_grad * factor
    )
    gates_new, gates_m_new, gates_v_new = adam_update(
        gates_vec, gates_m, gates_v, gains_grad * factor
    )
    chan_new, chan_m_new, chan_v_new = adam_update(chan_vec, chan_m, chan_v, chans_grad * factor)
    return (
        loss,
        norm,
        conv_new,
        conv_m_new,
        conv_v_new,
        gates_new,
        gates_m_new,
        gates_v_new,
        chan_new,
        chan_m_new,
        chan_v_new,
        hidden,
        cell,
    )


MESH = pl.DeviceIdType.MESH
F32 = jnp.float32
BF16 = jnp.bfloat16
TAPS = 25


def low(v):
    return v.astype(BF16).astype(F32)


def dot(a, b):
    return jnp.dot(a, b, preferred_element_type=F32)


def dot_nt(a, b):
    return lax.dot_general(a, b, (((1,), (1,)), ((), ())), preferred_element_type=F32)


def step_kernel(
    geo,
    frames_in,
    targets_in,
    horizon_in,
    sizes_in,
    gates_in,
    chan_in,
    w_ref,
    m_ref,
    v_ref,
    grad,
    wf,
    m_out,
    v_out,
    small_ref,
    h_ref,
    c_ref,
    frames_ref,
    targets_ref,
    horizon_ref,
    sizes_ref,
    gates_ref,
    chan_ref,
    stage,
    wr,
    wl,
    wh,
    wht,
    tiles,
    pix,
    cols,
    xb,
    sa,
    sb,
    pre1,
    save,
    h1,
    yrow,
    dst,
    dhp,
    dhy,
    dhr,
    d_own,
    dall,
    dt,
    ht,
    hr,
    xt,
    ps,
    vt,
    vf,
    vs,
    qf,
    qs,
    in_sem,
    w_sem,
    w_out,
    w_in,
    x_out,
    x_in,
    c_in,
    sp_out,
    sp_in,
    f_out,
    f_in,
):
    S, F, R, rows, PX = geo
    width = 8 * 32
    s, f = lax.axis_index("space"), lax.axis_index("fsdp")
    xx, cc = f // 2, lax.rem(f, 2)
    f_x, f_c, f_d = (1 - xx) * 2 + cc, xx * 2 + 1 - cc, (1 - xx) * 2 + 1 - cc
    fpeers = (f_x, f_c, f_d)

    def ahead(k):
        return lax.rem(s + k, S)

    def behind(k):
        return lax.rem(s - k + S, S)

    def only(when, do):
        if when is None:
            do()
        else:
            pl.when(when)(do)

    def copy_to(src, dst_, ssem, rsem, dev):
        return pltpu.make_async_remote_copy(
            src_ref=src, dst_ref=dst_, send_sem=ssem, recv_sem=rsem,
            device_id=dev, device_id_type=MESH,
        )

    def send(src, dst_, ssem, rsem, dev, priority=0):
        copy_to(src, dst_, ssem, rsem, dev).start(priority=priority)

    def arrived(slot, rsem):
        copy_to(slot, slot, rsem, rsem, (s, f_c)).wait_recv()

    def left(slot, ssem):
        copy_to(slot, slot, ssem, ssem, (s, f_c)).wait_send()

    def each(first, last, do):
        def step(k, carry):
            do(k)
            return carry

        lax.fori_loop(first, last, step, 0)

    TILE, H1, Y, DHY, DHL, BLK, END, VEC, SQ = 0, 1, 2, 3, 4, 5, 7, 8, 9
    DHY_IN, LINE_IN, ACROSS_IN = 10, 14, 22
    F_TILE, F_H1, F_H1C, F_VEC, F_SQ, F_D = 0, 1, 2, 3, 4, 5

    barrier = pltpu.get_barrier_semaphore()
    for k in range(1, S):
        pl.semaphore_signal(barrier, inc=1, device_id=(ahead(k), f), device_id_type=MESH)
    for p in fpeers:
        pl.semaphore_signal(barrier, inc=1, device_id=(s, p), device_id_type=MESH)
    small_ins = []
    for n, (src, held) in enumerate(
        (
            (frames_in, frames_ref), (targets_in, targets_ref), (horizon_in, horizon_ref),
            (sizes_in, sizes_ref), (gates_in, gates_ref), (chan_in, chan_ref),
        )
    ):
        small_ins.append(pltpu.make_async_copy(src, held, in_sem.at[n]))
        small_ins[-1].start()
    base = lax.rem(s * R, 2 * width)
    zero_rows = jnp.zeros((2 * width, wf.shape[1]), F32)
    wf[0 : 2 * width, :] = zero_rows
    wf[wf.shape[0] - 2 * width :, :] = zero_rows
    get_w = []
    for q in range(4):
        own_w = wf.at[pl.ds(pl.multiple_of(base + R // 4 * q, 16), R // 4), :]
        get_w.append(
            pltpu.make_async_copy(w_ref.at[R // 4 * q : R // 4 * (q + 1), :], own_w, w_sem.at[q])
        )
        get_w[-1].start()

    pl.semaphore_wait(barrier, S - 1 + 3)

    def holders(kind, i):
        lo = 512 * i + 256 * kind
        return [q for q in range(S) if (q * R) % 512 + R > lo and (q * R) % 512 < lo + 256]

    def holds(src, kind, i):
        if len(holders(kind, i)) == S:
            return None
        lo, first = 512 * i + 256 * kind, lax.rem(src * R, 512)
        return (lo < first + R) & (lo + 256 > first)

    def stage_slot(kind, i):
        for j in range(2):
            r0 = 512 * i + 256 * kind + 128 * j
            block = wf[r0 : r0 + 128, :].T.astype(BF16)
            stage[kind, i, j] = block.reshape(8, 32, 128)

    def send_slot(kind, i):
        def to(k):
            send(
                stage.at[kind, i, :, ahead(k)], wr.at[s, kind, i, :, f],
                w_out.at[kind, i], w_in.at[kind, i], (ahead(k), f),
            )

        only(holds(s, kind, i), lambda: each(1, S, to))

    order = {kind: sorted(range(4), key=lambda i: -len(holders(kind, i))) for kind in range(2)}
    for q in (0, 1):
        get_w[q].wait()
    stage_slot(0, order[0][0])
    send_slot(0, order[0][0])
    for cp in small_ins:
        cp.wait()

    def line(ref):
        parts = [
            ref[m, 0, t, r : r + 1, :].astype(F32)
            for t in range(2) for r in range(2) for m in range(2)
        ]
        return jnp.concatenate(parts, axis=1)

    lane128 = lax.broadcasted_iota(jnp.int32, (1, 128), 1)
    tall = jnp.where(lax.rem(lane128 // 16, 2) == 0, sizes_ref[0:1, 0:1], sizes_ref[0:1, 1:2])
    chans = [chan_ref[q : q + 1, :] for q in range(3)] + [jnp.zeros((1, 32), F32)]
    tiles[f, s] = jnp.concatenate(
        [
            line(frames_ref), line(targets_ref), line(horizon_ref), gates_ref[...],
            jnp.concatenate(chans, axis=1), tall.astype(F32), jnp.zeros((1, 128), F32),
        ],
        axis=0,
    )
    each(1, S, lambda k: send(
        tiles.at[f, s], tiles.at[f, s], sp_out.at[TILE], sp_in.at[TILE], (ahead(k), f)
    ))
    for q in (2, 3):
        get_w[q].wait()
    for i in order[0][1:]:
        stage_slot(0, i)
        send_slot(0, i)
    stage_slot(1, order[1][0])
    stage_slot(1, order[1][1])
    for i in range(4):
        wr[s, 0, i, :, f] = stage[0, i, :, s]

    arrived(tiles.at[f, 1:S], sp_in.at[TILE])
    for p in fpeers:
        send(tiles.at[f], tiles.at[f], f_out.at[F_TILE], f_in.at[F_TILE], (s, p))

    lane = lax.broadcasted_iota(jnp.int32, (1, PX), 1)
    row_of = lane // 32
    micro_of = lax.rem(lane // 16, 2)
    col_of = lax.rem(lane, 16)

    def build_pix(p):
        for t in range(2):
            halves = []
            for k in range(4):
                left = tiles[p, 2 * k][:, t * 64 : t * 64 + 64]
                right = tiles[p, 2 * k + 1][:, t * 64 : t * 64 + 64]
                halves.append(jnp.concatenate([left, right], axis=1))
            whole = jnp.concatenate(halves, axis=1)
            within = (row_of.astype(F32) >= rows - whole[6:7, :]).astype(F32)
            sub = lax.broadcasted_iota(jnp.int32, (8, PX), 0)
            pix[p, t] = jnp.where(sub == 7, within, whole)

    build_pix(f)

    sub32 = lax.broadcasted_iota(jnp.int32, (32, 128), 0)
    lane32 = lax.broadcasted_iota(jnp.int32, (32, 128), 1)

    def column(row, first):
        picked = jnp.where(lane32 == sub32 + first, row, 0.0)
        return low(jnp.sum(picked, axis=1, keepdims=True))

    for g in range(4):
        at = 2 * g + s // 4
        off = 32 * lax.rem(s, 4)
        for q in range(2):
            cols[q, 32 * g : 32 * g + 32, :] = jnp.broadcast_to(
                column(tiles[f, at][3 + q : 4 + q, :], off), (32, 128)
            )
    cols[2, 0:32, :] = jnp.broadcast_to(column(tiles[f, s][5:6, :], 64), (32, 128))
    for k in range(8):
        row5 = tiles[f, k][5:6, :]
        for q in range(2):
            cols[3 + q, 32 * k : 32 * k + 32, :] = jnp.broadcast_to(
                column(row5, 32 * q), (32, 128)
            )

    gain, shift, head = cols[0, 0:128, 0:1], cols[1, 0:128, 0:1], cols[2, 0:32, 0:1]

    def lifted(pixels, within):
        return ((pixels * cols[3, :, 0:1] + cols[4, :, 0:1]) * within).astype(BF16)

    inside = pix[f, 0, 7:8, :]

    def relay(kind):
        counts = [len(holders(kind, i)) for i in range(4)]

        def first_hop(i):
            when = holds(s, kind, i)
            n = counts[i]
            if when is None:
                arrived(wr.at[1:S, kind, i, :, f], w_in.at[kind, i])
            else:
                pl.when(when)(lambda: arrived(wr.at[1:n, kind, i, :, f], w_in.at[kind, i]))
                other = jnp.logical_not(when)
                pl.when(other)(lambda: arrived(wr.at[0:n, kind, i, :, f], w_in.at[kind, i]))

            def hop(k):
                src = behind(k)
                block = wr.at[src, kind, i, :, f]

                def go():
                    send(block, block, x_out.at[kind, 0], x_in.at[kind, i], (s, f_x))
                    send(block, block, x_out.at[kind, 1], c_in.at[kind, 0], (s, f_c))

                only(holds(src, kind, i), go)

            each(0, S, hop)

        def second_hop(i):
            arrived(wr.at[0 : counts[i], kind, i, :, f_x], x_in.at[kind, i])

            def hop(k):
                src = behind(k)
                block = wr.at[src, kind, i, :, f_x]
                only(
                    holds(src, kind, i),
                    lambda: send(block, block, x_out.at[kind, 2], c_in.at[kind, 1], (s, f_c)),
                )

            each(0, S, hop)

        for n, i in enumerate(order[kind]):
            first_hop(i)
            if kind == 0 and n > 0:
                send_slot(1, order[1][n - 1])
            if kind == 0 and n == 3:
                send_slot(1, order[1][3])
            if n > 0:
                second_hop(order[kind][n - 1])
        second_hop(order[kind][3])
        blocks = sum(counts) // 4
        arrived(wr.at[0:blocks, kind, :, :, f_c], c_in.at[kind, 0])
        arrived(wr.at[0:blocks, kind, :, :, f_d], c_in.at[kind, 1])

    def merge(kind, out):
        for tap in range(TAPS):
            lo = 512 * tap + 256 * kind
            total = None
            for sp in range(S):
                if sp * R < lo + 256 and sp * R + R > lo:
                    part = wr[sp, kind, tap - (sp * R) // 512]
                    total = part if total is None else total + part
            total = total.reshape(2, 128, 128)
            a, b = tap // 5, tap % 5
            out[128 * a : 128 * a + 128, 256 * b : 256 * b + 128] = total[0]
            out[128 * a : 128 * a + 128, 256 * b + 128 : 256 * b + 256] = total[1]

    cmask = [
        ((col_of + (b - 2) >= 0) & (col_of + (b - 2) < 16)).astype(F32) for b in range(5)
    ]
    rmask = [
        ((row_of + (a - 2) >= 0) & (row_of + (a - 2) < rows)).astype(F32) for a in range(5)
    ]

    def slide(v, d):
        if d == 0:
            return v
        parts = [
            pltpu.roll(v[:, q : q + 128], (-d) % 128, 1) for q in range(0, v.shape[1], 128)
        ]
        return jnp.concatenate(parts, axis=1) * cmask[d + 2]

    def conv(weights):
        sa[...] = dot(weights[...], xb[...]).reshape(5, 128, PX)
        out = sa[2]
        for a in (0, 1, 3, 4):
            out = out + pltpu.roll(sa[a], (-32 * (a - 2)) % PX, 1) * rmask[a]
        return out

    def slid_lift(t):
        line = jnp.concatenate([pix[f, t, 0:1, :], inside], axis=0)
        for b in range(5):
            moved = slide(line, b - 2)
            xb[256 * b : 256 * b + 256, :] = lifted(moved[0:1], moved[1:2])

    count = pix[f, 0, 6:7, :] * (16.0 * 32.0)

    def per_stream(v):
        first = jnp.sum(jnp.where(micro_of == 0, v, 0.0), axis=1, keepdims=True)
        second = jnp.sum(jnp.where(micro_of == 0, 0.0, v), axis=1, keepdims=True)
        return jnp.where(micro_of == 0, first, second)

    def cell_forward(t, pre, cell_prev):
        groups = [pre[32 * g : 32 * g + 32, :] for g in range(4)]
        sums = [
            jnp.sum(v * inside, axis=0, keepdims=True) for v in groups
        ] + [jnp.sum(v * inside * v, axis=0, keepdims=True) for v in groups]
        sums = per_stream(jnp.concatenate(sums, axis=0)) / count
        centre = sums[0:4]
        scale = lax.rsqrt(sums[4:8] - centre * centre + EPS_NORM)
        acts = []
        for g in range(4):
            normed = (groups[g] - centre[g : g + 1]) * scale[g : g + 1]
            save[t, 0, 32 * g : 32 * g + 32, :] = normed
            z = normed * gain[32 * g : 32 * g + 32] + shift[32 * g : 32 * g + 32]
            act = jnp.tanh(z) if g == 3 else 1.0 / (1.0 + jnp.exp(-z))
            save[t, 1, 32 * g : 32 * g + 32, :] = act
            acts.append(act)
        i, fo, o, cand = acts
        cell = i * cand * inside if cell_prev is None else (fo * cell_prev + i * cand) * inside
        tanh_c = jnp.tanh(cell)
        hidden = o * tanh_c * inside
        save[t, 2, 0:8, :] = jnp.concatenate([scale, scale], axis=0)
        save[t, 2, 32:64, :] = cell
        save[t, 2, 64:96, :] = tanh_c
        save[t, 2, 96:128, :] = hidden
        yrow[s, t : t + 1, :] = jnp.sum(hidden * head, axis=0, keepdims=True)
        return hidden, cell

    moments = [
        pltpu.make_async_copy(m_ref, m_out, in_sem.at[6]),
        pltpu.make_async_copy(v_ref, v_out, in_sem.at[7]),
    ]
    for cp in moments:
        cp.start()
    stage_slot(1, order[1][2])
    stage_slot(1, order[1][3])
    for i in range(4):
        wr[s, 1, i, :, f] = stage[1, i, :, s]
    slid_lift(0)
    relay(0)
    merge(0, wl)
    hidden0, cell0 = cell_forward(0, conv(wl), None)
    mine = pl.ds(pl.multiple_of(32 * s, 32), 32)
    h1[f, mine, :] = hidden0.astype(BF16)
    each(1, S, lambda k: send(
        h1.at[f, mine, :], h1.at[f, mine, :], sp_out.at[H1], sp_in.at[H1], (ahead(k), f)
    ))

    relay(1)
    slid_lift(1)
    pre1[...] = conv(wl)
    merge(1, wh)
    for a in range(5):
        for b in range(5):
            block = wh[128 * a : 128 * a + 128, 256 * b : 256 * b + 256]
            wht[256 * a : 256 * a + 256, 128 * b : 128 * b + 128] = block.astype(F32).T.astype(BF16)
    arrived(h1.at[f, 32 : 32 * S, :], sp_in.at[H1])
    send(h1.at[f], h1.at[f], f_out.at[F_H1], f_in.at[F_H1], (s, f_x))
    send(h1.at[f], h1.at[f], f_out.at[F_H1], f_in.at[F_H1C], (s, f_c))
    hidden_in = h1[f].astype(F32)
    for b in range(5):
        xb[256 * b : 256 * b + 256, :] = slide(hidden_in, b - 2).astype(BF16)
    pre1[...] = pre1[...] + conv(wh)
    hidden1, cell1 = cell_forward(1, pre1[...], cell0)
    each(1, S, lambda k: send(
        yrow.at[s], yrow.at[s], sp_out.at[Y], sp_in.at[Y], (ahead(k), f)
    ))

    arrived(tiles.at[0:3], f_in.at[F_TILE])
    for p in fpeers:
        build_pix(p)
    weight_rows = []
    for k in range(HOR):
        total = None
        for p in range(F):
            for t in range(2):
                picked = jnp.where(pix[p, t, 2:3, :] == float(k), pix[p, t, 7:8, :], 0.0)
                total = picked if total is None else total + picked
        counted = jnp.sum(total, axis=1, keepdims=True)
        weight_rows.append(1.0 / (HOR * jnp.maximum(counted, 1.0)))
    state = jnp.concatenate([hidden1, cell1, hidden1, cell1], axis=0).T
    state = state.reshape(rows // 2, 2, 2, 16, 128)
    ht[...] = jnp.where(
        lax.broadcasted_iota(jnp.int32, (rows // 2, 16, 128), 2) < 64,
        state[:, 0, 1], state[:, 1, 1],
    )
    hr[s] = ht[s]

    arrived(yrow.at[1:S], sp_in.at[Y])
    ysum = yrow[0]
    for k in range(1, S):
        ysum = ysum + yrow[k]
    slopes, sse = [], [None] * HOR
    for t in range(2):
        err = ysum[t : t + 1] - pix[f, t, 1:2, :]
        which = pix[f, t, 2:3, :]
        hw = jnp.zeros((1, PX), F32)
        for k in range(HOR):
            chosen = jnp.where(which == float(k), inside, 0.0)
            hw = hw + chosen * weight_rows[k]
            part = chosen * (err * err)
            sse[k] = part if sse[k] is None else sse[k] + part
        slopes.append(2.0 * err * hw)
    sse = [jnp.sum(v, axis=1, keepdims=True) for v in sse]

    def cell_backward(t, d_hidden, d_cell, cell_prev):
        slope = slopes[t]
        i, fo = save[t, 1, 0:32, :], save[t, 1, 32:64, :]
        o, cand = save[t, 1, 64:96, :], save[t, 1, 96:128, :]
        tanh_c, hidden = save[t, 2, 64:96, :], save[t, 2, 96:128, :]
        dh = slope * head
        if d_hidden is not None:
            dh = dh + d_hidden
        dh = dh * inside
        d_o = dh * tanh_c
        dc = dh * o * (1.0 - tanh_c * tanh_c)
        if d_cell is not None:
            dc = dc + d_cell
        dc = dc * inside
        d_f = jnp.zeros_like(dc) if cell_prev is None else dc * cell_prev
        raw = [
            dc * cand * i * (1.0 - i),
            d_f * fo * (1.0 - fo),
            d_o * o * (1.0 - o),
            dc * i * (1.0 - cand * cand),
        ]
        scale = save[t, 2, 0:8, :]
        d_head = jnp.sum(hidden * slope, axis=1, keepdims=True)
        d_gain, d_shift, dn, sums = [], [], [], [[], []]
        for g in range(4):
            normed = save[t, 0, 32 * g : 32 * g + 32, :]
            d_gain.append(jnp.sum(raw[g] * normed, axis=1, keepdims=True))
            d_shift.append(jnp.sum(raw[g], axis=1, keepdims=True))
            v = raw[g] * gain[32 * g : 32 * g + 32]
            dn.append(v)
            sums[0].append(jnp.sum(v * inside, axis=0, keepdims=True))
            sums[1].append(jnp.sum(v * inside * normed, axis=0, keepdims=True))
        sums = per_stream(jnp.concatenate(sums[0] + sums[1], axis=0)) / count
        for g in range(4):
            normed = save[t, 0, 32 * g : 32 * g + 32, :]
            d_pre = scale[g : g + 1] * (dn[g] - sums[g : g + 1] - normed * sums[4 + g : 5 + g])
            d_own[t, g] = (d_pre * inside).astype(BF16)
        return (
            dc * fo,
            d_head,
            jnp.concatenate(d_gain, axis=0),
            jnp.concatenate(d_shift, axis=0),
        )

    def share_gates(t):
        for n, p in enumerate(fpeers):
            send(
                d_own.at[t, p], dall.at[t, f, s], f_out.at[F_D + t], f_in.at[F_D + 3 * t + n], (s, p)
            )
        dall[t, f, s] = d_own[t, f]

    z, y = s // 2, lax.rem(s, 2)
    across = 2 * z + 1 - y

    def line_peer(k):
        return lax.rem(z + k, 4) * 2 + y

    def line_source(k):
        return lax.rem(z + 4 - k, 4) * 2 + y

    pieces = ((f, None), (f_c, 1), (f_x, 0), (f_d, 2))

    def share_piece(t, n):
        p, peer = pieces[n]
        block = dall.at[t, p, s]
        if peer is not None:
            arrived(block, f_in.at[F_D + 3 * t + peer])
        for k in (2, 3, 1):
            send(
                block, block, sp_out.at[BLK + t], sp_in.at[LINE_IN + 4 * t + n], (line_peer(k), f)
            )
        send(block, block, sp_out.at[BLK + t], sp_in.at[ACROSS_IN + 4 * t + n], (across, f))

    def relay_piece(t, n):
        p, unused = pieces[n]
        arrived(dall.at[t, p, 0:3], sp_in.at[LINE_IN + 4 * t + n])
        for k in (1, 3, 2):
            block = dall.at[t, p, line_source(k)]
            send(block, block, sp_out.at[BLK + t], sp_in.at[ACROSS_IN + 4 * t + n], (across, f))

    def gathered(t, n):
        p, unused = pieces[n]
        arrived(dall.at[t, p, 0:4], sp_in.at[ACROSS_IN + 4 * t + n])
        dt[p] = dall[t, p].reshape(256, PX).astype(F32).T.astype(BF16)
        return p

    each(1, S, lambda k: send(
        ht.at[ahead(k)], hr.at[s], sp_out.at[END], sp_in.at[END], (ahead(k), f)
    ))
    d_cell0, d_head1, d_gain1, d_shift1 = cell_backward(1, None, None, cell0)
    share_gates(1)

    d1 = d_own[1].reshape(128, PX).astype(F32)
    for b in range(5):
        dst[128 * b : 128 * b + 128, :] = slide(d1, 2 - b).astype(BF16)
    sb[...] = dot(wht[...], dst[...]).reshape(5, 256, PX)
    dh = sb[2]
    for a in (0, 1, 3, 4):
        dh = dh + pltpu.roll(sb[a], (32 * (a - 2)) % PX, 1) * rmask[4 - a]
    dhp[...] = dh
    steps = (2, 1, 3, 0)

    def part_of(zz, yy):
        return pl.ds(pl.multiple_of(32 * (2 * zz + yy), 32), 32)

    for k in steps:
        zz = lax.rem(z + k, 4)
        send(
            dhp.at[part_of(zz, 1 - y), :], dhy.at[k], sp_out.at[DHY], sp_in.at[DHY_IN + k], (across, f)
        )
    for k in steps:
        zz = lax.rem(z + k, 4)
        arrived(dhy.at[k], sp_in.at[DHY_IN + k])
        both = dhp[part_of(zz, y), :] + dhy[k]
        if k == 0:
            dhr[z] = both
        else:
            dhy[k] = both
            send(
                dhy.at[k], dhr.at[z], sp_out.at[DHL], sp_in.at[DHL], (line_peer(k), f)
            )
    for n in range(4):
        share_piece(1, n)

    first_tap = (s * R) // 512

    def tap_inputs(n, carry):
        p, i = n // 4, lax.rem(n, 4)
        tap = first_tap + i
        da, db = tap // 5 - 2, lax.rem(tap, 5) - 2
        back = lax.rem(2 * PX - 32 * da - db, PX)
        ok = (row_of + da >= 0) & (row_of + da < rows) & (col_of + db >= 0) & (col_of + db < 16)
        ok = ok.astype(F32)
        for t in range(2):
            moved = pltpu.roll(pix[p, t], back, 1)
            xt[t, p, i] = lifted(moved[0:1], moved[7:8] * ok)
        return carry

    arrived(h1.at[f_x], f_in.at[F_H1])
    send(h1.at[f_x], h1.at[f_x], f_out.at[F_H1], f_in.at[F_H1C], (s, f_c))
    lax.fori_loop(0, 4 * F, tap_inputs, 0)
    arrived(h1.at[0:2], f_in.at[F_H1C])

    def tap_hidden(n, carry):
        p, i = n // 4, lax.rem(n, 4)
        tap = first_tap + i
        da, db = tap // 5 - 2, lax.rem(tap, 5) - 2
        back = lax.rem(2 * PX - 32 * da - db, PX)
        ok = (row_of + da >= 0) & (row_of + da < rows) & (col_of + db >= 0) & (col_of + db < 16)
        xt[2, p, i] = (pltpu.roll(h1[p].astype(F32), back, 1) * ok.astype(F32)).astype(BF16)
        return carry

    lax.fori_loop(0, 4 * F, tap_hidden, 0)

    def moved_pixels(t):
        pixels = pix[f, t, 0:1, :] * inside
        high = low(pixels)
        mid = low(pixels - high)
        rest = low(pixels - high - mid)
        four = jnp.concatenate([high, mid, rest, inside, jnp.zeros((4, PX), F32)], axis=0)
        for a in range(5):
            lines = four if a == 2 else pltpu.roll(four, (-32 * (a - 2)) % PX, 1) * rmask[a]
            for b in range(5):
                n = 8 * (5 * a + b)
                ps[t, n : n + 8, :] = slide(lines, b - 2)
        return dot_nt(d_own[t].reshape(128, PX), ps[t].astype(BF16))

    q1 = moved_pixels(1)

    arrived(dhr.at[0:3], sp_in.at[DHL])
    d_hidden0 = (dhr[0] + dhr[1]) + (dhr[2] + dhr[3])
    unused, d_head0, d_gain0, d_shift0 = cell_backward(0, d_hidden0, d_cell0, None)
    share_gates(0)
    share_piece(0, 0)

    q = q1 + moved_pixels(0)
    total_w = jnp.zeros((128, 256), F32)
    total_b = jnp.zeros((128, 256), F32)
    for tap in range(TAPS):
        a, b = tap // 5, tap % 5
        w = wl[128 * a : 128 * a + 128, 256 * b : 256 * b + 256].astype(F32)
        n = 8 * tap
        total_w = total_w + w * (q[:, n : n + 1] + q[:, n + 1 : n + 2] + q[:, n + 2 : n + 3])
        total_b = total_b + w * q[:, n + 3 : n + 4]
    lift_w = jnp.sum(total_w, axis=0, keepdims=True)
    lift_b = jnp.sum(total_b, axis=0, keepdims=True)

    for n in range(1, 4):
        share_piece(0, n)

    lane_sq = lax.broadcasted_iota(jnp.int32, (128, 128), 1)
    d_head = jnp.concatenate(
        [d_head0 + d_head1] + sse_rows(sse), axis=0
    )
    packed = jnp.where(lane_sq == 0, d_gain0 + d_gain1, 0.0)
    packed = jnp.where(lane_sq == 1, d_shift0 + d_shift1, packed)
    packed = jnp.where(lane_sq == 2, d_head, packed)
    packed = packed.T[0:3, :]
    vt[...] = jnp.concatenate(
        [packed, lift_w[:, 0:128], lift_w[:, 128:256], lift_b[:, 0:128], lift_b[:, 128:256],
         jnp.zeros((1, 128), F32)], axis=0,
    )
    vf[f] = vt[...]
    for p in fpeers:
        send(vt, vf.at[f], f_out.at[F_VEC], f_in.at[F_VEC], (s, p))
    for n in range(4):
        relay_piece(1, n)
    arrived(vf.at[0:3], f_in.at[F_VEC])
    vs[s] = (vf[0] + vf[1]) + (vf[2] + vf[3])
    each(1, S, lambda k: send(
        vs.at[s], vs.at[s], sp_out.at[VEC], sp_in.at[VEC], (ahead(k), f)
    ))

    for n in range(4):
        relay_piece(0, n)
    for n in range(4):
        gathered(1, n)

    def grad_one(i, carry):
        for kind in range(2):
            total = None
            for p in range(F):
                part = dot(xt[1 + kind, p, i], dt[p])
                total = part if total is None else total + part
            grad[pl.ds(pl.multiple_of(512 * i + 256 * kind, 256), 256), :] = total
        return carry

    lax.fori_loop(0, 4, grad_one, 0)

    arrived(hr.at[1:S], sp_in.at[END])
    for k in range(S):
        for r in range(2):
            h_ref[16 * r : 16 * r + 16, 32 * k : 32 * k + 32] = hr[k, :, 64 * r : 64 * r + 32]
            c_ref[16 * r : 16 * r + 16, 32 * k : 32 * k + 32] = hr[k, :, 64 * r + 32 : 64 * r + 64]

    arrived(vs.at[1:S], sp_in.at[VEC])
    lane8 = lax.broadcasted_iota(jnp.int32, (8, 128), 1)
    sub8 = lax.broadcasted_iota(jnp.int32, (8, 128), 0)
    lift = vs[0]
    small_sq = jnp.zeros((8, 128), F32)
    for k in range(S):
        own_rows = jnp.where((sub8 < 2) | ((sub8 == 2) & (lane8 < 32)), vs[k], 0.0)
        small_sq = small_sq + own_rows * own_rows
        if k > 0:
            lift = lift + vs[k]
    lift = jnp.where((sub8 >= 3) & (sub8 < 7), lift, 0.0)
    small_sq = jnp.sum(small_sq + lift * lift)
    gate, half = s // 2, lax.rem(s, 2)
    d_gates = jnp.zeros((8, 128), F32)
    for k in range(4):
        turned = pltpu.roll(vs[4 * half + k], lax.rem(32 * k - 32 * gate + 128, 128), 1)
        d_gates = jnp.where((lane8 >= 32 * k) & (lane8 < 32 * k + 32), turned, d_gates)
    quarter = 32 * lax.rem(s, 4)
    upper = s // 4
    turned = pltpu.roll(lift, lax.rem(128 - quarter, 128), 1)
    line_w = jnp.where(upper == 0, turned[3:4], turned[4:5])
    line_b = jnp.where(upper == 0, turned[5:6], turned[6:7])
    line_h = vs[s][2:3, :]
    lane1 = lane8[0:1]
    d_chans = jnp.where(
        lane1 < 32, line_w,
        jnp.where(lane1 < 64, pltpu.roll(line_b, 32, 1), pltpu.roll(line_h, 64, 1)),
    )
    loss = jnp.zeros((1, 1), F32)
    for k in range(HOR):
        loss = loss + vs[s][2:3, 32 + k : 33 + k] * weight_rows[k]

    for n in range(4):
        p = gathered(0, n)

        def grad_zero(i):
            at = pl.ds(pl.multiple_of(512 * i, 256), 256)
            grad[at, :] = grad[at, :] + dot(xt[0, p, i], dt[p])

        each(0, 4, grad_zero)

    def square(n, carry):
        v = grad[pl.ds(pl.multiple_of(base + 64 * n, 64), 64), :]
        return carry + v * v

    total = lax.fori_loop(0, R // 64, square, jnp.zeros((64, 256), F32))
    qf[f] = jnp.full((8, 128), jnp.sum(total), F32)
    for p in fpeers:
        send(qf.at[f], qf.at[f], f_out.at[F_SQ], f_in.at[F_SQ], (s, p))
    arrived(qf.at[0:3], f_in.at[F_SQ])
    qs[s] = (qf[0] + qf[1]) + (qf[2] + qf[3])
    each(1, S, lambda k: send(
        qs.at[s], qs.at[s], sp_out.at[SQ], sp_in.at[SQ], (ahead(k), f)
    ))
    arrived(qs.at[1:S], sp_in.at[SQ])
    squares = qs[0]
    for k in range(1, S):
        squares = squares + qs[k]
    norm = jnp.sqrt(squares + small_sq)
    factor = jnp.minimum(1.0, CLIP / (norm + 1e-06))
    out = jnp.where(sub8 < 2, d_gates, d_chans)
    out = jnp.where(sub8 == 3, loss, out)
    out = jnp.where(sub8 == 4, norm, out)
    out = jnp.where(sub8 == 5, factor, out)
    small_ref[...] = out

    for cp in moments:
        cp.wait()
    for kind in range(2):
        blocks = sum(len(holders(kind, i)) for i in range(4)) // 4
        for i in range(4):
            sent = functools.partial(left, wr.at[1:S, kind, i, :, f], w_out.at[kind, i])
            only(holds(s, kind, i), sent)
        for hop in range(3):
            left(wr.at[0:blocks, kind, :, :, f], x_out.at[kind, hop])
    left(tiles.at[f, 1:S], sp_out.at[TILE])
    left(h1.at[f, 32 : 32 * S, :], sp_out.at[H1])
    left(yrow.at[1:S], sp_out.at[Y])
    left(dhy, sp_out.at[DHY])
    left(dhr.at[0:3], sp_out.at[DHL])
    for t in range(2):
        left(dall.at[t, :, 1:S], sp_out.at[BLK + t])
        left(dall.at[t, 0:3, s], f_out.at[F_D + t])
    left(hr.at[1:S], sp_out.at[END])
    left(vs.at[1:S], sp_out.at[VEC])
    left(qs.at[1:S], sp_out.at[SQ])
    left(tiles.at[0:3], f_out.at[F_TILE])
    left(h1.at[0:3], f_out.at[F_H1])
    left(vf.at[0:3], f_out.at[F_VEC])
    left(qf.at[0:3], f_out.at[F_SQ])


def sse_rows(sse):
    return sse + [jnp.zeros((128 - 32 - HOR, 1), F32)]


def step_fast(
    frames, targets, sizes, horizon, conv_weight, conv_m, conv_v, gates_vec, chan_vec
):
    S, F = lax.axis_size("space"), lax.axis_size("fsdp")
    R, N = conv_weight.shape
    rows, cols = frames.shape[3] * S, frames.shape[4]
    PX = 2 * rows * cols

    VM = pltpu.VMEM
    DMA = pltpu.SemaphoreType.DMA
    geo = (S, F, R, rows, PX)
    out = pl.pallas_call(
        functools.partial(step_kernel, geo),
        out_shape=(
            VM((2048, N), F32),
            VM((2048, N), F32),
            VM((R, N), F32),
            VM((R, N), F32),
            VM((8, 128), F32),
            VM((32, 256), F32),
            VM((32, 256), F32),
        ),
        in_specs=[pl.BlockSpec(memory_space=pltpu.HBM)] * 9,
        out_specs=(pl.BlockSpec(memory_space=VM),) * 7,
        scratch_shapes=[
            VM(frames.shape, F32),
            VM(frames.shape, F32),
            VM(frames.shape, jnp.int32),
            VM((1, 2), jnp.int32),
            VM(gates_vec.shape, F32),
            VM(chan_vec.shape, F32),
            VM((2, 4, 2, 8, 32, 128), BF16),
            VM((S, 2, 4, 2, 4, 32, 128), BF16),
            VM((640, 1280), BF16),
            VM((640, 1280), BF16),
            VM((1280, 640), BF16),
            VM((F, S, 8, 128), F32),
            VM((F, 2, 8, PX), F32),
            VM((5, 256, 128), F32),
            VM((1280, PX), BF16),
            VM((5, 128, PX), F32),
            VM((5, 256, PX), F32),
            VM((128, PX), F32),
            VM((2, 3, 128, PX), F32),
            VM((F, 256, PX), BF16),
            VM((S, 2, PX), F32),
            VM((640, PX), BF16),
            VM((256, PX), F32),
            VM((4, 32, PX), F32),
            VM((4, 32, PX), F32),
            VM((2, 4, 32, PX), BF16),
            VM((2, F, S, 32, PX), BF16),
            VM((F, PX, 256), BF16),
            VM((rows // 2, cols, 128), F32),
            VM((S, cols, 128), F32),
            VM((3, F, 4, 256, PX), BF16),
            VM((2, 8 * TAPS, PX), F32),
            VM((8, 128), F32),
            VM((F, 8, 128), F32),
            VM((S, 8, 128), F32),
            VM((F, 8, 128), F32),
            VM((S, 8, 128), F32),
            DMA((8,)),
            DMA((4,)),
            DMA((2, 4)),
            DMA((2, 4)),
            DMA((2, 3)),
            DMA((2, 4)),
            DMA((2, 2)),
            DMA((10,)),
            DMA((30,)),
            DMA((7,)),
            DMA((11,)),
        ],
        compiler_params=pltpu.CompilerParams(
            collective_id=0, has_side_effects=True, vmem_limit_bytes=44 * 2**20
        ),
    )(
        *(
            pltpu.with_memory_space_constraint(v, pltpu.HBM)
            for v in (
                frames, targets, horizon, sizes.reshape(1, 2), gates_vec, chan_vec,
                conv_weight, conv_m, conv_v,
            )
        )
    )
    return out


def adam_kernel(steps, *refs):
    small_ref, h_ref, c_ref, g_ref = refs[:4]
    (w_ref, m_ref, v_ref), gates, chan = refs[4:7], refs[7:10], refs[10:13]
    outs, held, sem, sems = refs[13:26], refs[26:39], refs[39], refs[40]
    conv_held, conv_outs = held[2:5], outs[2:5]
    factor = small_ref[5:6, 0:1]
    R = m_ref.shape[0]
    size = R // steps
    base = lax.rem(lax.axis_index("space") * R, 512)
    held[0][...] = small_ref[3:4, 0:1]
    held[1][...] = small_ref[4:5, 0:1]

    def update(weights, grad, news):
        w, m, v = weights
        for ref, new in zip(news, adam_update(w[...], m[...], v[...], grad * factor)):
            ref[...] = new

    update(gates, small_ref[0:2, :], held[5:8])
    chans = [small_ref[2:3, 32 * q : 32 * q + 32] for q in range(3)]
    update(chan, jnp.concatenate(chans, axis=0), held[8:11])
    for r in range(2):
        held[11][0, r] = h_ref[16 * r : 16 * r + 16, :]
        held[12][0, r] = c_ref[16 * r : 16 * r + 16, :]
    copies = []
    for n in (0, 1, *range(5, 13)):
        copies.append(pltpu.make_async_copy(held[n], outs[n], sem.at[n]))
        copies[-1].start()
    for n in range(steps):
        at = slice(size * n, size * n + size)
        moved = pl.ds(pl.multiple_of(base + size * n, 64), size)
        news = adam_update(w_ref[moved, :], m_ref[at, :], v_ref[at, :], g_ref[moved, :] * factor)
        for q, new in enumerate(news):
            conv_held[q][at, :] = new
            copies.append(
                pltpu.make_async_copy(conv_held[q].at[at, :], conv_outs[q].at[at, :], sems.at[q, n])
            )
            copies[-1].start()
    for copy in copies:
        copy.wait()


def adam_step(small, hidden, cell, grad, weights, frame_shape):
    steps = 5
    rows, cols = frame_shape
    conv, gates, chan = weights
    flat = [*conv, *gates, *chan]
    shapes = [v.shape for v in (*conv[1:], conv[1], *gates, *chan)]
    state = (1, rows, cols, hidden.shape[1])
    shapes = [(1, 1), (1, 1), *shapes, state, state]
    out = pl.pallas_call(
        functools.partial(adam_kernel, steps),
        out_shape=tuple(jax.ShapeDtypeStruct(v, F32) for v in shapes),
        in_specs=[pl.BlockSpec(memory_space=pltpu.VMEM)] * (4 + len(flat)),
        out_specs=(pl.BlockSpec(memory_space=pl.ANY),) * len(shapes),
        scratch_shapes=[pltpu.VMEM(v, F32) for v in shapes]
        + [pltpu.SemaphoreType.DMA((13,)), pltpu.SemaphoreType.DMA((3, steps))],
        compiler_params=pltpu.CompilerParams(vmem_limit_bytes=8 * 2**20),
    )(small, hidden, cell, grad, *flat)
    return (out[0].reshape(()), out[1].reshape(()), *out[2:])


def per_device_fast(
    frames, targets, sizes, horizon,
    conv_weight, conv_m, conv_v,
    gates_vec, gates_m, gates_v,
    chan_vec, chan_m, chan_v,
):
    grad, weight, first, second, small, hidden, cell = step_fast(
        frames, targets, sizes, horizon, conv_weight, conv_m, conv_v, gates_vec, chan_vec
    )
    weights = ((weight, first, second), (gates_vec, gates_m, gates_v), (chan_vec, chan_m, chan_v))
    return adam_step(small, hidden, cell, grad, weights, frames.shape[3:])


def fits(mesh, shapes):
    S, F = mesh.shape["space"], mesh.shape["fsdp"]
    frames, conv, chan = shapes
    return (
        (S, F) == (8, 4)
        and frames == (2, F, 2, 2 * S, 16)
        and conv == (TAPS * 512, 1024)
        and chan == (3, 256)
    )


def solution(mesh):
    in_specs = (
        P(None, "fsdp", None, "space", None),
        P(None, "fsdp", None, "space", None),
        P(None, "fsdp"),
        P(None, "fsdp", None, "space", None),
        P("space", "fsdp"),
        P("space", "fsdp"),
        P("space", "fsdp"),
        P(None, "space"),
        P(None, "space"),
        P(None, "space"),
        P(None, "space"),
        P(None, "space"),
        P(None, "space"),
    )
    out_specs = (
        P(),
        P(),
        P("space", "fsdp"),
        P("space", "fsdp"),
        P("space", "fsdp"),
        P(None, "space"),
        P(None, "space"),
        P(None, "space"),
        P(None, "space"),
        P(None, "space"),
        P(None, "space"),
        P("fsdp", "space", None, None),
        P("fsdp", "space", None, None),
    )

    def run(*args):
        shapes = (args[0].shape, args[4].shape, args[10].shape)
        body = per_device_fast if fits(mesh, shapes) else per_device
        return jax.shard_map(
            body, mesh=mesh, in_specs=in_specs, out_specs=out_specs, check_vma=False
        )(*args)

    return run
```

```python
import functools

import jax
import jax.numpy as jnp
from jax import lax
from jax.experimental import pallas as pl
from jax.experimental.pallas import tpu as pltpu
from jax.sharding import PartitionSpec as P

GROUPS = 32
HOR = 4
STEP = 10


EPS_NORM = 1e-05
CLIP = 0.01
RATE = 0.01
BETA1 = 0.9
BETA2 = 0.999
DECAY = 0.01
EPS_ADAM = 1e-08


def with_halo(shard, sides, width):
    for axis, dim in sides:
        count, length = (lax.axis_size(axis), shard.shape[dim])
        up = [(i, (i + 1) % count) for i in range(count - 1)]
        down = [(j, i) for i, j in up]
        last = lax.slice_in_dim(shard, length - width, length, axis=dim)
        first = lax.slice_in_dim(shard, 0, width, axis=dim)
        before = lax.ppermute(last, axis, up)
        after = lax.ppermute(first, axis, down)
        shard = jnp.concatenate([before, shard, after], axis=dim)
    return shard


def cell_head(gates, cell_prev, valid, head_w):
    width = cell_prev.shape[-1]
    gate_in = jax.nn.sigmoid(gates[..., :width])
    gate_forget = jax.nn.sigmoid(gates[..., width : 2 * width])
    gate_out = jax.nn.sigmoid(gates[..., 2 * width : 3 * width])
    candidate = jnp.tanh(gates[..., 3 * width :])
    cell_new = (gate_forget * cell_prev + gate_in * candidate) * valid
    hidden_new = gate_out * jnp.tanh(cell_new) * valid
    return (hidden_new, cell_new, jnp.sum(hidden_new * head_w, axis=-1))


def adam_update(weight, first, second, grad):
    first = BETA1 * first + (1.0 - BETA1) * grad
    second = BETA2 * second + (1.0 - BETA2) * grad * grad
    first_hat = first / (1.0 - BETA1**STEP)
    second_hat = second / (1.0 - BETA2**STEP)
    weight = weight - RATE * (first_hat / (jnp.sqrt(second_hat) + EPS_ADAM) + DECAY * weight)
    return (weight, first, second)


def gather_weights(conv_weight, gates_vec, chan_vec):
    col_block = lax.all_gather(conv_weight.astype(jnp.bfloat16), "fsdp", axis=1, tiled=True)
    kernel, gains, chans = (
        lax.all_gather(col_block, "space", axis=0, tiled=True),
        lax.all_gather(gates_vec.astype(jnp.bfloat16), "space", axis=1, tiled=True),
        lax.all_gather(chan_vec.astype(jnp.bfloat16), "space", axis=1, tiled=True),
    )
    inputs_n = kernel.shape[0] // 25
    gates_n = kernel.shape[1]
    flipped = (
        kernel.reshape(25, inputs_n, gates_n).transpose(0, 2, 1).reshape(25 * gates_n, inputs_n)
    )
    return (kernel, flipped, gains.astype(jnp.float32), chans.astype(jnp.float32))


def lifted_patches(joined):
    rows, cols = (joined.shape[1], joined.shape[2])
    padded = with_halo(joined, (("space", 1),), 2)
    padded = jnp.pad(padded, ((0, 0), (0, 0), (2, 2), (0, 0)))
    pieces = [padded[:, a : a + rows, b : b + cols, :] for a in range(5) for b in range(5)]
    return jnp.concatenate(pieces, -1).reshape(-1, 25 * joined.shape[3])


def spread_back(delta, flipped):
    rows, cols = (delta.shape[1], delta.shape[2])
    padded = with_halo(delta, (("space", 1),), 2)
    padded = jnp.pad(padded, ((0, 0), (0, 0), (2, 2), (0, 0)))
    pieces = [
        padded[:, 4 - a : 4 - a + rows, 4 - b : 4 - b + cols, :] for a in range(5) for b in range(5)
    ]
    stacked = jnp.concatenate(pieces, -1).reshape(-1, 25 * delta.shape[3])
    result = jnp.dot(stacked, flipped, preferred_element_type=jnp.float32)
    return result.reshape(delta.shape[0], rows, cols, -1)


def time_major(array):
    return jnp.moveaxis(array, 1, 0)


def forward(weights, seq, goal, chosen, inside, count, hweight):
    kernel, flipped, gains, chans = weights
    streams, nframes, rows, cols = seq.shape
    width = chans.shape[1]
    valid = inside[:, :, None, None]

    def forward_frame(carry, inputs):
        hidden, cell = carry
        pixels, target, picked = inputs
        lifted = (pixels[..., None] * chans[0] + chans[1]) * valid
        joined = jnp.concatenate([lifted, hidden], -1).astype(jnp.bfloat16)
        patches = lifted_patches(joined)
        pre = jnp.dot(patches, kernel, preferred_element_type=jnp.float32).reshape(
            streams, rows, cols, GROUPS, -1
        )
        weighted = pre * valid[..., None]
        first, second = lax.psum(
            (jnp.sum(weighted, axis=(1, 2, 4)), jnp.sum(weighted * pre, axis=(1, 2, 4))), "space"
        )
        centre = first / count[:, None]
        scale = lax.rsqrt(second / count[:, None] - centre * centre + EPS_NORM)
        normed = ((pre - centre[:, None, None, :, None]) * scale[:, None, None, :, None]).reshape(
            streams, rows, cols, 4 * width
        )
        gates = normed * gains[0] + gains[1]
        hidden_new, cell_new, output = cell_head(gates, cell, valid, chans[2])
        error = output - target
        sse = jnp.sum(picked * (error * error)[..., None], axis=(0, 1, 2))
        slope = 2.0 * error * jnp.sum(picked * hweight, axis=-1)
        return ((hidden_new, cell_new), (sse, (patches, normed, scale, cell, gates, slope)))

    zeros = jnp.zeros((streams, rows, cols, width), jnp.float32)
    (hidden, cell), (sse, kept) = lax.scan(
        forward_frame, (zeros, zeros), (time_major(seq), time_major(goal), time_major(chosen))
    )
    return (hidden, cell, jnp.sum(sse, axis=0), kept)


def backward(weights, kept, seq, inside, count):
    kernel, flipped, gains, chans = weights
    patches, normed, scale, cells, gates, slope = kept
    streams, nframes, rows, cols = seq.shape
    width = chans.shape[1]
    valid = inside[:, :, None, None]

    def cell_part(gate_vals, cell_prev, head_w):
        return cell_head(gate_vals, cell_prev, valid, head_w)

    def backward_frame(carry, inputs):
        d_hidden, d_cell, d_gain, d_bias, d_head, d_lift_w, d_lift_b = carry
        normed_t, scale_t, cell_prev, gates_t, slope_t, pixels = inputs
        unused, pull = jax.vjp(cell_part, gates_t, cell_prev, chans[2])
        d_gates, d_cell_prev, d_head_t = pull((d_hidden, d_cell, slope_t))
        d_normed = (d_gates * gains[0]).reshape(streams, rows, cols, GROUPS, -1)
        grouped = normed_t.reshape(streams, rows, cols, GROUPS, -1)
        masked = d_normed * valid[..., None]
        first, second = lax.psum(
            (jnp.sum(masked, axis=(1, 2, 4)), jnp.sum(masked * grouped, axis=(1, 2, 4))), "space"
        )
        first = (first / count[:, None])[:, None, None, :, None]
        second = (second / count[:, None])[:, None, None, :, None]
        d_pre = (
            scale_t[:, None, None, :, None]
            * (d_normed - first - grouped * second)
            * valid[..., None]
        )
        d_pre = d_pre.reshape(streams, rows, cols, -1).astype(jnp.bfloat16)
        d_joined = spread_back(d_pre, flipped)
        d_lifted = d_joined[..., :width] * valid
        carry_new = (
            d_joined[..., width:],
            d_cell_prev,
            d_gain + jnp.sum(d_gates * normed_t, axis=(0, 1, 2)),
            d_bias + jnp.sum(d_gates, axis=(0, 1, 2)),
            d_head + d_head_t,
            d_lift_w + jnp.sum(d_lifted * pixels[..., None], axis=(0, 1, 2)),
            d_lift_b + jnp.sum(d_lifted, axis=(0, 1, 2)),
        )
        return (carry_new, d_pre)

    zeros = jnp.zeros((streams, rows, cols, width), jnp.float32)
    wide_zero = jnp.zeros((4 * width,), jnp.float32)
    narrow_zero = jnp.zeros((width,), jnp.float32)
    start = (zeros, zeros, wide_zero, wide_zero, narrow_zero, narrow_zero, narrow_zero)
    final, d_pre_all = lax.scan(
        backward_frame, start, (normed, scale, cells, gates, slope, time_major(seq)), reverse=True
    )
    d_kernel = lax.dot_general(
        patches.reshape(-1, patches.shape[-1]),
        d_pre_all.reshape(-1, 4 * width),
        (((0,), (0,)), ((), ())),
        preferred_element_type=jnp.float32,
    )
    d_gains = jnp.stack([final[2], final[3]])
    d_chans = jnp.stack([final[5], final[6], final[4]])
    return (d_kernel, d_gains, d_chans)


def reduce_grads(d_kernel, d_gains, d_chans):
    col_part = lax.psum_scatter(d_kernel, "fsdp", scatter_dimension=1, tiled=True)
    kernel_part, gains_part, chans_part = (
        lax.psum_scatter(col_part, "space", scatter_dimension=0, tiled=True),
        lax.psum_scatter(d_gains, "space", scatter_dimension=1, tiled=True),
        lax.psum_scatter(d_chans, "space", scatter_dimension=1, tiled=True),
    )
    gains_part, chans_part = lax.psum((gains_part, chans_part), "fsdp")
    return (kernel_part, gains_part, chans_part)


def per_device(
    frames,
    targets,
    sizes,
    horizon,
    conv_weight,
    conv_m,
    conv_v,
    gates_vec,
    gates_m,
    gates_v,
    chan_vec,
    chan_m,
    chan_v,
):
    micro, streams, nframes, rows, cols = frames.shape
    width = chan_vec.shape[1] * lax.axis_size("space")
    total_rows = rows * lax.axis_size("space")
    row_ids = lax.axis_index("space") * rows + jnp.arange(rows, dtype=jnp.int32)
    inside = (row_ids[None, None, :] >= total_rows - sizes[:, :, None]).astype(jnp.float32)
    select = (horizon[..., None] == jnp.arange(HOR, dtype=jnp.int32)).astype(jnp.float32) * inside[
        :, :, None, :, None, None
    ]
    counts = lax.psum(jnp.sum(select, axis=(0, 1, 2, 3, 4)), ("space", "fsdp"))
    hweight = 1.0 / (HOR * jnp.maximum(counts, 1.0))
    group_count = sizes.astype(jnp.float32) * (cols * (4 * width // GROUPS))
    held = gather_weights(conv_weight, gates_vec, chan_vec)
    sse_total = jnp.zeros((HOR,), jnp.float32)
    summed = None
    for batch in range(micro):
        hidden, cell, sse, kept = forward(
            held,
            frames[batch],
            targets[batch],
            select[batch],
            inside[batch],
            group_count[batch],
            hweight,
        )
        sse_total = sse_total + sse
        grads = backward(held, kept, frames[batch], inside[batch], group_count[batch])
        summed = grads if summed is None else jax.tree.map(jnp.add, summed, grads)
    summed = reduce_grads(*summed)
    kernel_grad, gains_grad, chans_grad = summed
    leading = (lax.axis_index("fsdp") == 0).astype(jnp.float32)
    squares = jnp.sum(kernel_grad * kernel_grad) + leading * (
        jnp.sum(gains_grad * gains_grad) + jnp.sum(chans_grad * chans_grad)
    )
    sse_total, squares = lax.psum((sse_total, squares), ("space", "fsdp"))
    loss = jnp.sum(sse_total * hweight)
    norm = jnp.sqrt(squares)
    factor = jnp.minimum(1.0, CLIP / (norm + 1e-06))
    conv_new, conv_m_new, conv_v_new = adam_update(
        conv_weight, conv_m, conv_v, kernel_grad * factor
    )
    gates_new, gates_m_new, gates_v_new = adam_update(
        gates_vec, gates_m, gates_v, gains_grad * factor
    )
    chan_new, chan_m_new, chan_v_new = adam_update(chan_vec, chan_m, chan_v, chans_grad * factor)
    return (
        loss,
        norm,
        conv_new,
        conv_m_new,
        conv_v_new,
        gates_new,
        gates_m_new,
        gates_v_new,
        chan_new,
        chan_m_new,
        chan_v_new,
        hidden,
        cell,
    )


MESH = pl.DeviceIdType.MESH
F32 = jnp.float32
BF16 = jnp.bfloat16
TAPS = 25


def low(v):
    return v.astype(BF16).astype(F32)


def dot(a, b):
    return jnp.dot(a, b, preferred_element_type=F32)


def dot_nt(a, b):
    return lax.dot_general(a, b, (((1,), (1,)), ((), ())), preferred_element_type=F32)


def step_kernel(
    geo,
    frames_in,
    targets_in,
    horizon_in,
    sizes_in,
    gates_in,
    chan_in,
    w_ref,
    m_ref,
    v_ref,
    grad,
    wf,
    m_out,
    v_out,
    small_ref,
    h_ref,
    c_ref,
    frames_ref,
    targets_ref,
    horizon_ref,
    sizes_ref,
    gates_ref,
    chan_ref,
    stage,
    wr,
    wl,
    wh,
    wht,
    tiles,
    pix,
    cols,
    xb,
    sa,
    sb,
    pre1,
    save,
    h1,
    yrow,
    dst,
    dhp,
    dhy,
    dhr,
    d_own,
    dall,
    dt,
    ht,
    hr,
    xt,
    ps,
    vt,
    vf,
    vs,
    qf,
    qs,
    in_sem,
    w_sem,
    w_out,
    w_in,
    x_out,
    x_in,
    c_in,
    sp_out,
    sp_in,
    y_out,
    chain_in,
    f_out,
    f_in,
):
    S, F, R, rows, PX = geo
    width = 8 * 32
    s, f = lax.axis_index("space"), lax.axis_index("fsdp")
    xx, cc = f // 2, lax.rem(f, 2)
    f_x, f_c, f_d = (1 - xx) * 2 + cc, xx * 2 + 1 - cc, (1 - xx) * 2 + 1 - cc
    fpeers = (f_x, f_c, f_d)

    def ahead(k):
        return lax.rem(s + k, S)

    def behind(k):
        return lax.rem(s - k + S, S)

    def only(when, do):
        if when is None:
            do()
        else:
            pl.when(when)(do)

    def copy_to(src, dst_, ssem, rsem, dev):
        return pltpu.make_async_remote_copy(
            src_ref=src, dst_ref=dst_, send_sem=ssem, recv_sem=rsem,
            device_id=dev, device_id_type=MESH,
        )

    def send(src, dst_, ssem, rsem, dev, priority=0):
        copy_to(src, dst_, ssem, rsem, dev).start(priority=priority)

    def arrived(slot, rsem):
        copy_to(slot, slot, rsem, rsem, (s, f_c)).wait_recv()

    def left(slot, ssem):
        copy_to(slot, slot, ssem, ssem, (s, f_c)).wait_send()

    def each(first, last, do):
        def step(k, carry):
            do(k)
            return carry

        lax.fori_loop(first, last, step, 0)

    TILE, H1, Y, DHY, DHL, BLK, END, VEC, SQ = 0, 1, 2, 3, 4, 5, 7, 8, 9
    DHY_IN, LINE_IN, ACROSS_IN = 10, 14, 22
    F_TILE, F_H1, F_H1C, F_VEC, F_SQ, F_D = 0, 1, 2, 3, 4, 5

    barrier = pltpu.get_barrier_semaphore()
    for k in range(1, S):
        pl.semaphore_signal(barrier, inc=1, device_id=(ahead(k), f), device_id_type=MESH)
    for p in fpeers:
        pl.semaphore_signal(barrier, inc=1, device_id=(s, p), device_id_type=MESH)
    small_ins = []
    for n, (src, held) in enumerate(
        (
            (frames_in, frames_ref), (targets_in, targets_ref), (horizon_in, horizon_ref),
            (sizes_in, sizes_ref), (gates_in, gates_ref), (chan_in, chan_ref),
        )
    ):
        small_ins.append(pltpu.make_async_copy(src, held, in_sem.at[n]))
        small_ins[-1].start()
    base = lax.rem(s * R, 2 * width)
    zero_rows = jnp.zeros((2 * width, wf.shape[1]), F32)
    wf[0 : 2 * width, :] = zero_rows
    wf[wf.shape[0] - 2 * width :, :] = zero_rows
    get_w = []
    for q in range(4):
        own_w = wf.at[pl.ds(pl.multiple_of(base + R // 4 * q, 16), R // 4), :]
        get_w.append(
            pltpu.make_async_copy(w_ref.at[R // 4 * q : R // 4 * (q + 1), :], own_w, w_sem.at[q])
        )
        get_w[-1].start()

    pl.semaphore_wait(barrier, S - 1 + 3)

    def holders(kind, i):
        lo = 512 * i + 256 * kind
        return [q for q in range(S) if (q * R) % 512 + R > lo and (q * R) % 512 < lo + 256]

    def holds(src, kind, i):
        if len(holders(kind, i)) == S:
            return None
        lo, first = 512 * i + 256 * kind, lax.rem(src * R, 512)
        return (lo < first + R) & (lo + 256 > first)

    def stage_slot(kind, i):
        for j in range(2):
            r0 = 512 * i + 256 * kind + 128 * j
            block = wf[r0 : r0 + 128, :].T.astype(BF16)
            stage[kind, i, j] = block.reshape(8, 32, 128)

    def send_slot(kind, i):
        def to(k):
            send(
                stage.at[kind, i, :, ahead(k)], wr.at[s, kind, i, :, f],
                w_out.at[kind, i], w_in.at[kind, i], (ahead(k), f),
            )

        only(holds(s, kind, i), lambda: each(1, S, to))

    order = {kind: sorted(range(4), key=lambda i: -len(holders(kind, i))) for kind in range(2)}
    for q in (0, 1):
        get_w[q].wait()
    stage_slot(0, order[0][0])
    send_slot(0, order[0][0])
    for cp in small_ins:
        cp.wait()

    def line(ref):
        parts = [
            ref[m, 0, t, r : r + 1, :].astype(F32)
            for t in range(2) for r in range(2) for m in range(2)
        ]
        return jnp.concatenate(parts, axis=1)

    lane128 = lax.broadcasted_iota(jnp.int32, (1, 128), 1)
    tall = jnp.where(lax.rem(lane128 // 16, 2) == 0, sizes_ref[0:1, 0:1], sizes_ref[0:1, 1:2])
    chans = [chan_ref[q : q + 1, :] for q in range(3)] + [jnp.zeros((1, 32), F32)]
    tiles[f, s] = jnp.concatenate(
        [
            line(frames_ref), line(targets_ref), line(horizon_ref), gates_ref[...],
            jnp.concatenate(chans, axis=1), tall.astype(F32), jnp.zeros((1, 128), F32),
        ],
        axis=0,
    )
    each(1, S, lambda k: send(
        tiles.at[f, s], tiles.at[f, s], sp_out.at[TILE], sp_in.at[TILE], (ahead(k), f)
    ))
    for q in (2, 3):
        get_w[q].wait()
    for i in order[0][1:]:
        stage_slot(0, i)
        send_slot(0, i)
    for i in order[1]:
        stage_slot(1, i)
        send_slot(1, i)
    for i in range(4):
        wr[s, 0, i, :, f] = stage[0, i, :, s]

    arrived(tiles.at[f, 1:S], sp_in.at[TILE])
    for p in fpeers:
        send(tiles.at[f], tiles.at[f], f_out.at[F_TILE], f_in.at[F_TILE], (s, p))

    lane = lax.broadcasted_iota(jnp.int32, (1, PX), 1)
    row_of = lane // 32
    micro_of = lax.rem(lane // 16, 2)
    col_of = lax.rem(lane, 16)

    def build_pix(p):
        for t in range(2):
            halves = []
            for k in range(4):
                left = tiles[p, 2 * k][:, t * 64 : t * 64 + 64]
                right = tiles[p, 2 * k + 1][:, t * 64 : t * 64 + 64]
                halves.append(jnp.concatenate([left, right], axis=1))
            whole = jnp.concatenate(halves, axis=1)
            within = (row_of.astype(F32) >= rows - whole[6:7, :]).astype(F32)
            sub = lax.broadcasted_iota(jnp.int32, (8, PX), 0)
            pix[p, t] = jnp.where(sub == 7, within, whole)

    build_pix(f)

    sub32 = lax.broadcasted_iota(jnp.int32, (32, 128), 0)
    lane32 = lax.broadcasted_iota(jnp.int32, (32, 128), 1)

    def column(row, first):
        picked = jnp.where(lane32 == sub32 + first, row, 0.0)
        return low(jnp.sum(picked, axis=1, keepdims=True))

    for g in range(4):
        at = 2 * g + s // 4
        off = 32 * lax.rem(s, 4)
        for q in range(2):
            cols[q, 32 * g : 32 * g + 32, :] = jnp.broadcast_to(
                column(tiles[f, at][3 + q : 4 + q, :], off), (32, 128)
            )
    cols[2, 0:32, :] = jnp.broadcast_to(column(tiles[f, s][5:6, :], 64), (32, 128))
    for k in range(8):
        row5 = tiles[f, k][5:6, :]
        for q in range(2):
            cols[3 + q, 32 * k : 32 * k + 32, :] = jnp.broadcast_to(
                column(row5, 32 * q), (32, 128)
            )

    gain, shift, head = cols[0, 0:128, 0:1], cols[1, 0:128, 0:1], cols[2, 0:32, 0:1]

    def lifted(pixels, within):
        return ((pixels * cols[3, :, 0:1] + cols[4, :, 0:1]) * within).astype(BF16)

    inside = pix[f, 0, 7:8, :]

    def relay(kind):
        counts = [len(holders(kind, i)) for i in range(4)]

        def first_hop(i):
            when = holds(s, kind, i)
            n = counts[i]
            if when is None:
                arrived(wr.at[1:S, kind, i, :, f], w_in.at[kind, i])
            else:
                pl.when(when)(lambda: arrived(wr.at[1:n, kind, i, :, f], w_in.at[kind, i]))
                other = jnp.logical_not(when)
                pl.when(other)(lambda: arrived(wr.at[0:n, kind, i, :, f], w_in.at[kind, i]))

            def hop(k):
                src = behind(k)
                block = wr.at[src, kind, i, :, f]

                def go():
                    send(block, block, x_out.at[kind, 0], x_in.at[kind, i], (s, f_x))
                    send(block, block, x_out.at[kind, 1], c_in.at[kind, 0], (s, f_c))

                only(holds(src, kind, i), go)

            each(0, S, hop)

        def second_hop(i):
            arrived(wr.at[0 : counts[i], kind, i, :, f_x], x_in.at[kind, i])

            def hop(k):
                src = behind(k)
                block = wr.at[src, kind, i, :, f_x]
                only(
                    holds(src, kind, i),
                    lambda: send(block, block, x_out.at[kind, 2], c_in.at[kind, 1], (s, f_c)),
                )

            each(0, S, hop)

        def finish():
            blocks = sum(counts) // 4
            arrived(wr.at[0:blocks, kind, :, :, f_c], c_in.at[kind, 0])
            arrived(wr.at[0:blocks, kind, :, :, f_d], c_in.at[kind, 1])

        def first(n):
            first_hop(order[kind][n])

        def second(n):
            second_hop(order[kind][n])

        return first, second, finish

    first_l, second_l, finish_l = relay(0)
    first_h, second_h, finish_h = relay(1)

    def merge(kind, out):
        for tap in range(TAPS):
            lo = 512 * tap + 256 * kind
            total = None
            for sp in range(S):
                if sp * R < lo + 256 and sp * R + R > lo:
                    part = wr[sp, kind, tap - (sp * R) // 512]
                    total = part if total is None else total + part
            total = total.reshape(2, 128, 128)
            a, b = tap // 5, tap % 5
            out[128 * a : 128 * a + 128, 256 * b : 256 * b + 128] = total[0]
            out[128 * a : 128 * a + 128, 256 * b + 128 : 256 * b + 256] = total[1]

    cmask = [
        ((col_of + (b - 2) >= 0) & (col_of + (b - 2) < 16)).astype(F32) for b in range(5)
    ]
    rmask = [
        ((row_of + (a - 2) >= 0) & (row_of + (a - 2) < rows)).astype(F32) for a in range(5)
    ]

    def slide(v, d):
        if d == 0:
            return v
        parts = [
            pltpu.roll(v[:, q : q + 128], (-d) % 128, 1) for q in range(0, v.shape[1], 128)
        ]
        return jnp.concatenate(parts, axis=1) * cmask[d + 2]

    def conv(weights):
        sa[...] = dot(weights[...], xb[...]).reshape(5, 128, PX)
        out = sa[2]
        for a in (0, 1, 3, 4):
            out = out + pltpu.roll(sa[a], (-32 * (a - 2)) % PX, 1) * rmask[a]
        return out

    def slid_lift(t):
        line = jnp.concatenate([pix[f, t, 0:1, :], inside], axis=0)
        for b in range(5):
            moved = slide(line, b - 2)
            xb[256 * b : 256 * b + 256, :] = lifted(moved[0:1], moved[1:2])

    count = pix[f, 0, 6:7, :] * (16.0 * 32.0)

    def per_stream(v):
        first = jnp.sum(jnp.where(micro_of == 0, v, 0.0), axis=1, keepdims=True)
        second = jnp.sum(jnp.where(micro_of == 0, 0.0, v), axis=1, keepdims=True)
        return jnp.where(micro_of == 0, first, second)

    def cell_forward(t, pre, cell_prev):
        groups = [pre[32 * g : 32 * g + 32, :] for g in range(4)]
        sums = [
            jnp.sum(v * inside, axis=0, keepdims=True) for v in groups
        ] + [jnp.sum(v * inside * v, axis=0, keepdims=True) for v in groups]
        sums = per_stream(jnp.concatenate(sums, axis=0)) / count
        centre = sums[0:4]
        scale = lax.rsqrt(sums[4:8] - centre * centre + EPS_NORM)
        acts = []
        for g in range(4):
            normed = (groups[g] - centre[g : g + 1]) * scale[g : g + 1]
            save[t, 0, 32 * g : 32 * g + 32, :] = normed
            z = normed * gain[32 * g : 32 * g + 32] + shift[32 * g : 32 * g + 32]
            act = jnp.tanh(z) if g == 3 else 1.0 / (1.0 + jnp.exp(-z))
            save[t, 1, 32 * g : 32 * g + 32, :] = act
            acts.append(act)
        i, fo, o, cand = acts
        cell = i * cand * inside if cell_prev is None else (fo * cell_prev + i * cand) * inside
        tanh_c = jnp.tanh(cell)
        hidden = o * tanh_c * inside
        save[t, 2, 0:8, :] = jnp.concatenate([scale, scale], axis=0)
        save[t, 2, 32:64, :] = cell
        save[t, 2, 64:96, :] = tanh_c
        save[t, 2, 96:128, :] = hidden
        yrow[s, t : t + 1, :] = jnp.sum(hidden * head, axis=0, keepdims=True)
        return hidden, cell

    moments = [
        pltpu.make_async_copy(m_ref, m_out, in_sem.at[6]),
        pltpu.make_async_copy(v_ref, v_out, in_sem.at[7]),
    ]
    for cp in moments:
        cp.start()
    slid_lift(0)
    for i in range(4):
        wr[s, 1, i, :, f] = stage[1, i, :, s]
    first_l(0)
    for n in range(1, 4):
        first_l(n)
        second_l(n - 1)
    first_h(0)
    second_l(3)
    first_h(1)
    finish_l()
    merge(0, wl)
    hidden0, cell0 = cell_forward(0, conv(wl), None)
    mine = pl.ds(pl.multiple_of(32 * s, 32), 32)
    h1[f, mine, :] = hidden0.astype(BF16)
    each(1, S, lambda k: send(
        h1.at[f, mine, :], h1.at[f, mine, :], sp_out.at[H1], sp_in.at[H1], (ahead(k), f)
    ))

    first_h(2)
    second_h(0)
    second_h(1)
    first_h(3)
    second_h(2)
    second_h(3)
    finish_h()
    slid_lift(1)
    pre1[...] = conv(wl)
    merge(1, wh)
    for a in range(5):
        for b in range(5):
            block = wh[128 * a : 128 * a + 128, 256 * b : 256 * b + 256]
            wht[256 * a : 256 * a + 256, 128 * b : 128 * b + 128] = block.astype(F32).T.astype(BF16)
    arrived(h1.at[f, 32 : 32 * S, :], sp_in.at[H1])
    send(h1.at[f], h1.at[f], f_out.at[F_H1], f_in.at[F_H1], (s, f_x))
    send(h1.at[f], h1.at[f], f_out.at[F_H1], f_in.at[F_H1C], (s, f_c))
    hidden_in = h1[f].astype(F32)
    for b in range(5):
        xb[256 * b : 256 * b + 256, :] = slide(hidden_in, b - 2).astype(BF16)
    pre1[...] = pre1[...] + conv(wh)
    hidden1, cell1 = cell_forward(1, pre1[...], cell0)
    each(1, S, lambda k: send(
        yrow.at[s], yrow.at[s], sp_out.at[Y], sp_in.at[Y], (ahead(k), f)
    ))

    arrived(tiles.at[0:3], f_in.at[F_TILE])
    for p in fpeers:
        build_pix(p)
    weight_rows = []
    for k in range(HOR):
        total = None
        for p in range(F):
            for t in range(2):
                picked = jnp.where(pix[p, t, 2:3, :] == float(k), pix[p, t, 7:8, :], 0.0)
                total = picked if total is None else total + picked
        counted = jnp.sum(total, axis=1, keepdims=True)
        weight_rows.append(1.0 / (HOR * jnp.maximum(counted, 1.0)))
    state = jnp.concatenate([hidden1, cell1, hidden1, cell1], axis=0).T
    state = state.reshape(rows // 2, 2, 2, 16, 128)
    ht[...] = jnp.where(
        lax.broadcasted_iota(jnp.int32, (rows // 2, 16, 128), 2) < 64,
        state[:, 0, 1], state[:, 1, 1],
    )
    hr[s] = ht[s]

    arrived(yrow.at[1:S], sp_in.at[Y])
    ysum = yrow[0]
    for k in range(1, S):
        ysum = ysum + yrow[k]
    slopes, sse = [], [None] * HOR
    for t in range(2):
        err = ysum[t : t + 1] - pix[f, t, 1:2, :]
        which = pix[f, t, 2:3, :]
        hw = jnp.zeros((1, PX), F32)
        for k in range(HOR):
            chosen = jnp.where(which == float(k), inside, 0.0)
            hw = hw + chosen * weight_rows[k]
            part = chosen * (err * err)
            sse[k] = part if sse[k] is None else sse[k] + part
        slopes.append(2.0 * err * hw)
    sse = [jnp.sum(v, axis=1, keepdims=True) for v in sse]

    def cell_backward(t, d_hidden, d_cell, cell_prev):
        slope = slopes[t]
        i, fo = save[t, 1, 0:32, :], save[t, 1, 32:64, :]
        o, cand = save[t, 1, 64:96, :], save[t, 1, 96:128, :]
        tanh_c, hidden = save[t, 2, 64:96, :], save[t, 2, 96:128, :]
        dh = slope * head
        if d_hidden is not None:
            dh = dh + d_hidden
        dh = dh * inside
        d_o = dh * tanh_c
        dc = dh * o * (1.0 - tanh_c * tanh_c)
        if d_cell is not None:
            dc = dc + d_cell
        dc = dc * inside
        d_f = jnp.zeros_like(dc) if cell_prev is None else dc * cell_prev
        raw = [
            dc * cand * i * (1.0 - i),
            d_f * fo * (1.0 - fo),
            d_o * o * (1.0 - o),
            dc * i * (1.0 - cand * cand),
        ]
        scale = save[t, 2, 0:8, :]
        d_head = jnp.sum(hidden * slope, axis=1, keepdims=True)
        d_gain, d_shift, dn, sums = [], [], [], [[], []]
        for g in range(4):
            normed = save[t, 0, 32 * g : 32 * g + 32, :]
            d_gain.append(jnp.sum(raw[g] * normed, axis=1, keepdims=True))
            d_shift.append(jnp.sum(raw[g], axis=1, keepdims=True))
            v = raw[g] * gain[32 * g : 32 * g + 32]
            dn.append(v)
            sums[0].append(jnp.sum(v * inside, axis=0, keepdims=True))
            sums[1].append(jnp.sum(v * inside * normed, axis=0, keepdims=True))
        sums = per_stream(jnp.concatenate(sums[0] + sums[1], axis=0)) / count
        for g in range(4):
            normed = save[t, 0, 32 * g : 32 * g + 32, :]
            d_pre = scale[g : g + 1] * (dn[g] - sums[g : g + 1] - normed * sums[4 + g : 5 + g])
            d_own[t, g] = (d_pre * inside).astype(BF16)
        return (
            dc * fo,
            d_head,
            jnp.concatenate(d_gain, axis=0),
            jnp.concatenate(d_shift, axis=0),
        )

    def share_gates(t):
        for n, p in enumerate(fpeers):
            send(
                d_own.at[t, p], dall.at[t, f, s], f_out.at[F_D + t], f_in.at[F_D + 3 * t + n], (s, p)
            )
        dall[t, f, s] = d_own[t, f]

    z, y = s // 2, lax.rem(s, 2)
    across = 2 * z + 1 - y

    def line_peer(k):
        return lax.rem(z + k, 4) * 2 + y

    def line_source(k):
        return lax.rem(z + 4 - k, 4) * 2 + y

    pieces = ((f, None), (f_c, 1), (f_x, 0), (f_d, 2))

    def share_piece(t, n):
        p, peer = pieces[n]
        block = dall.at[t, p, s]
        if peer is not None:
            arrived(block, f_in.at[F_D + 3 * t + peer])
        if CHAIN[t]:
            for way in range(2):
                pass_on(t, n, 0, way, block)
        else:
            for k in (2, 3, 1):
                send(
                    block, block, sp_out.at[BLK + t], sp_in.at[LINE_IN + 4 * t + n],
                    (line_peer(k), f),
                )
        send(block, block, y_out.at[t], sp_in.at[ACROSS_IN + 4 * t + n], (across, f))

    def pass_on(t, n, hop, way, block):
        inside_line, to = ((z < 3, z + 1), (z > 0, z - 1))[way]
        pl.when(inside_line)(lambda: send(
            block, block, sp_out.at[BLK + t], chain_in.at[t, n, hop, way], (2 * to + y, f)
        ))

    def relay_hop(t, n, hop):
        p, unused = pieces[n]
        for way, there in ((0, z >= hop), (1, z + hop <= 3)):
            block = dall.at[t, p, 2 * lax.rem(z + (4 - hop, hop)[way], 4) + y]

            def come():
                arrived(block, chain_in.at[t, n, hop - 1, way])
                if hop < 3:
                    pass_on(t, n, hop, way, block)
                send(block, block, y_out.at[t], sp_in.at[ACROSS_IN + 4 * t + n], (across, f))

            pl.when(there)(come)

    def relay_wave(t, wave):
        if CHAIN[t]:
            for hop in range(1, 4):
                if 0 <= wave - hop < 4:
                    relay_hop(t, wave - hop, hop)
            return
        n = wave - 1
        p, unused = pieces[n]
        arrived(dall.at[t, p, 0:3], sp_in.at[LINE_IN + 4 * t + n])
        for k in (1, 3, 2):
            block = dall.at[t, p, line_source(k)]
            send(block, block, y_out.at[t], sp_in.at[ACROSS_IN + 4 * t + n], (across, f))

    CHAIN = (True, False)
    WAVES = [6 if chain else 4 for chain in CHAIN]

    def gathered(t, n):
        p, unused = pieces[n]
        arrived(dall.at[t, p, 0:4], sp_in.at[ACROSS_IN + 4 * t + n])
        dt[p] = dall[t, p].reshape(256, PX).astype(F32).T.astype(BF16)
        return p

    each(1, S, lambda k: send(
        ht.at[ahead(k)], hr.at[s], sp_out.at[END], sp_in.at[END], (ahead(k), f)
    ))
    d_cell0, d_head1, d_gain1, d_shift1 = cell_backward(1, None, None, cell0)
    share_gates(1)

    d1 = d_own[1].reshape(128, PX).astype(F32)
    for b in range(5):
        dst[128 * b : 128 * b + 128, :] = slide(d1, 2 - b).astype(BF16)
    sb[...] = dot(wht[...], dst[...]).reshape(5, 256, PX)
    dh = sb[2]
    for a in (0, 1, 3, 4):
        dh = dh + pltpu.roll(sb[a], (32 * (a - 2)) % PX, 1) * rmask[4 - a]
    dhp[...] = dh
    steps = (2, 1, 3, 0)

    def part_of(zz, yy):
        return pl.ds(pl.multiple_of(32 * (2 * zz + yy), 32), 32)

    for k in steps:
        zz = lax.rem(z + k, 4)
        send(
            dhp.at[part_of(zz, 1 - y), :], dhy.at[k], sp_out.at[DHY], sp_in.at[DHY_IN + k], (across, f)
        )
    for k in steps:
        zz = lax.rem(z + k, 4)
        arrived(dhy.at[k], sp_in.at[DHY_IN + k])
        both = dhp[part_of(zz, y), :] + dhy[k]
        if k == 0:
            dhr[z] = both
        else:
            dhy[k] = both
            send(
                dhy.at[k], dhr.at[z], sp_out.at[DHL], sp_in.at[DHL], (line_peer(k), f)
            )
    for n in range(4):
        share_piece(1, n)

    first_tap = (s * R) // 512

    def tap_inputs(n, carry):
        p, i = n // 4, lax.rem(n, 4)
        tap = first_tap + i
        da, db = tap // 5 - 2, lax.rem(tap, 5) - 2
        back = lax.rem(2 * PX - 32 * da - db, PX)
        ok = (row_of + da >= 0) & (row_of + da < rows) & (col_of + db >= 0) & (col_of + db < 16)
        ok = ok.astype(F32)
        for t in range(2):
            moved = pltpu.roll(pix[p, t], back, 1)
            xt[t, p, i] = lifted(moved[0:1], moved[7:8] * ok)
        return carry

    arrived(h1.at[f_x], f_in.at[F_H1])
    send(h1.at[f_x], h1.at[f_x], f_out.at[F_H1], f_in.at[F_H1C], (s, f_c))
    lax.fori_loop(0, 4 * F, tap_inputs, 0)
    arrived(h1.at[0:2], f_in.at[F_H1C])

    def tap_hidden(n, carry):
        p, i = n // 4, lax.rem(n, 4)
        tap = first_tap + i
        da, db = tap // 5 - 2, lax.rem(tap, 5) - 2
        back = lax.rem(2 * PX - 32 * da - db, PX)
        ok = (row_of + da >= 0) & (row_of + da < rows) & (col_of + db >= 0) & (col_of + db < 16)
        xt[2, p, i] = (pltpu.roll(h1[p].astype(F32), back, 1) * ok.astype(F32)).astype(BF16)
        return carry

    lax.fori_loop(0, 4 * F, tap_hidden, 0)

    def moved_pixels(t):
        pixels = pix[f, t, 0:1, :] * inside
        high = low(pixels)
        mid = low(pixels - high)
        rest = low(pixels - high - mid)
        four = jnp.concatenate([high, mid, rest, inside, jnp.zeros((4, PX), F32)], axis=0)
        for a in range(5):
            lines = four if a == 2 else pltpu.roll(four, (-32 * (a - 2)) % PX, 1) * rmask[a]
            for b in range(5):
                n = 8 * (5 * a + b)
                ps[t, n : n + 8, :] = slide(lines, b - 2)
        return dot_nt(d_own[t].reshape(128, PX), ps[t].astype(BF16))

    q1 = moved_pixels(1)

    arrived(dhr.at[0:3], sp_in.at[DHL])
    d_hidden0 = (dhr[0] + dhr[1]) + (dhr[2] + dhr[3])
    unused, d_head0, d_gain0, d_shift0 = cell_backward(0, d_hidden0, d_cell0, None)
    share_gates(0)
    share_piece(0, 0)

    q = q1 + moved_pixels(0)
    total_w = jnp.zeros((128, 256), F32)
    total_b = jnp.zeros((128, 256), F32)
    for tap in range(TAPS):
        a, b = tap // 5, tap % 5
        w = wl[128 * a : 128 * a + 128, 256 * b : 256 * b + 256].astype(F32)
        n = 8 * tap
        total_w = total_w + w * (q[:, n : n + 1] + q[:, n + 1 : n + 2] + q[:, n + 2 : n + 3])
        total_b = total_b + w * q[:, n + 3 : n + 4]
    lift_w = jnp.sum(total_w, axis=0, keepdims=True)
    lift_b = jnp.sum(total_b, axis=0, keepdims=True)

    relay_wave(1, 1)
    share_piece(0, 1)
    relay_wave(1, 2)
    for n in range(2, 4):
        share_piece(0, n)
    relay_wave(1, 3)

    lane_sq = lax.broadcasted_iota(jnp.int32, (128, 128), 1)
    d_head = jnp.concatenate(
        [d_head0 + d_head1] + sse_rows(sse), axis=0
    )
    packed = jnp.where(lane_sq == 0, d_gain0 + d_gain1, 0.0)
    packed = jnp.where(lane_sq == 1, d_shift0 + d_shift1, packed)
    packed = jnp.where(lane_sq == 2, d_head, packed)
    packed = packed.T[0:3, :]
    vt[...] = jnp.concatenate(
        [packed, lift_w[:, 0:128], lift_w[:, 128:256], lift_b[:, 0:128], lift_b[:, 128:256],
         jnp.zeros((1, 128), F32)], axis=0,
    )
    vf[f] = vt[...]
    for p in fpeers:
        send(vt, vf.at[f], f_out.at[F_VEC], f_in.at[F_VEC], (s, p))
    for wave in range(4, WAVES[1] + 1):
        relay_wave(1, wave)
    arrived(vf.at[0:3], f_in.at[F_VEC])
    vs[s] = (vf[0] + vf[1]) + (vf[2] + vf[3])
    each(1, S, lambda k: send(
        vs.at[s], vs.at[s], sp_out.at[VEC], sp_in.at[VEC], (ahead(k), f)
    ))

    for wave in range(1, WAVES[0] + 1):
        relay_wave(0, wave)
    for n in range(4):
        gathered(1, n)

    def grad_one(i, carry):
        for kind in range(2):
            total = None
            for p in range(F):
                part = dot(xt[1 + kind, p, i], dt[p])
                total = part if total is None else total + part
            grad[pl.ds(pl.multiple_of(512 * i + 256 * kind, 256), 256), :] = total
        return carry

    lax.fori_loop(0, 4, grad_one, 0)

    arrived(hr.at[1:S], sp_in.at[END])
    for k in range(S):
        for r in range(2):
            h_ref[16 * r : 16 * r + 16, 32 * k : 32 * k + 32] = hr[k, :, 64 * r : 64 * r + 32]
            c_ref[16 * r : 16 * r + 16, 32 * k : 32 * k + 32] = hr[k, :, 64 * r + 32 : 64 * r + 64]

    arrived(vs.at[1:S], sp_in.at[VEC])
    lane8 = lax.broadcasted_iota(jnp.int32, (8, 128), 1)
    sub8 = lax.broadcasted_iota(jnp.int32, (8, 128), 0)
    lift = vs[0]
    small_sq = jnp.zeros((8, 128), F32)
    for k in range(S):
        own_rows = jnp.where((sub8 < 2) | ((sub8 == 2) & (lane8 < 32)), vs[k], 0.0)
        small_sq = small_sq + own_rows * own_rows
        if k > 0:
            lift = lift + vs[k]
    lift = jnp.where((sub8 >= 3) & (sub8 < 7), lift, 0.0)
    small_sq = jnp.sum(small_sq + lift * lift)
    gate, half = s // 2, lax.rem(s, 2)
    d_gates = jnp.zeros((8, 128), F32)
    for k in range(4):
        turned = pltpu.roll(vs[4 * half + k], lax.rem(32 * k - 32 * gate + 128, 128), 1)
        d_gates = jnp.where((lane8 >= 32 * k) & (lane8 < 32 * k + 32), turned, d_gates)
    quarter = 32 * lax.rem(s, 4)
    upper = s // 4
    turned = pltpu.roll(lift, lax.rem(128 - quarter, 128), 1)
    line_w = jnp.where(upper == 0, turned[3:4], turned[4:5])
    line_b = jnp.where(upper == 0, turned[5:6], turned[6:7])
    line_h = vs[s][2:3, :]
    lane1 = lane8[0:1]
    d_chans = jnp.where(
        lane1 < 32, line_w,
        jnp.where(lane1 < 64, pltpu.roll(line_b, 32, 1), pltpu.roll(line_h, 64, 1)),
    )
    loss = jnp.zeros((1, 1), F32)
    for k in range(HOR):
        loss = loss + vs[s][2:3, 32 + k : 33 + k] * weight_rows[k]

    for n in range(4):
        p = gathered(0, n)

        def grad_zero(i):
            at = pl.ds(pl.multiple_of(512 * i, 256), 256)
            grad[at, :] = grad[at, :] + dot(xt[0, p, i], dt[p])

        each(0, 4, grad_zero)

    def square(n, carry):
        v = grad[pl.ds(pl.multiple_of(base + 64 * n, 64), 64), :]
        return carry + v * v

    total = lax.fori_loop(0, R // 64, square, jnp.zeros((64, 256), F32))
    qf[f] = jnp.full((8, 128), jnp.sum(total), F32)
    for p in fpeers:
        send(qf.at[f], qf.at[f], f_out.at[F_SQ], f_in.at[F_SQ], (s, p))
    arrived(qf.at[0:3], f_in.at[F_SQ])
    qs[s] = (qf[0] + qf[1]) + (qf[2] + qf[3])
    each(1, S, lambda k: send(
        qs.at[s], qs.at[s], sp_out.at[SQ], sp_in.at[SQ], (ahead(k), f)
    ))
    arrived(qs.at[1:S], sp_in.at[SQ])
    squares = qs[0]
    for k in range(1, S):
        squares = squares + qs[k]
    norm = jnp.sqrt(squares + small_sq)
    factor = jnp.minimum(1.0, CLIP / (norm + 1e-06))
    out = jnp.where(sub8 < 2, d_gates, d_chans)
    out = jnp.where(sub8 == 3, loss, out)
    out = jnp.where(sub8 == 4, norm, out)
    out = jnp.where(sub8 == 5, factor, out)
    small_ref[...] = out

    for cp in moments:
        cp.wait()
    for kind in range(2):
        blocks = sum(len(holders(kind, i)) for i in range(4)) // 4
        for i in range(4):
            sent = functools.partial(left, wr.at[1:S, kind, i, :, f], w_out.at[kind, i])
            only(holds(s, kind, i), sent)
        for hop in range(3):
            left(wr.at[0:blocks, kind, :, :, f], x_out.at[kind, hop])
    left(tiles.at[f, 1:S], sp_out.at[TILE])
    left(h1.at[f, 32 : 32 * S, :], sp_out.at[H1])
    left(yrow.at[1:S], sp_out.at[Y])
    left(dhy, sp_out.at[DHY])
    left(dhr.at[0:3], sp_out.at[DHL])
    for t in range(2):
        left(dall.at[t, :, 0:4], y_out.at[t])
        if CHAIN[t]:
            edge = (z == 0) | (z == 3)
            pl.when(edge)(lambda: left(dall.at[t, :, 0:1], sp_out.at[BLK + t]))
            middle = jnp.logical_not(edge)
            pl.when(middle)(lambda: left(dall.at[t, :, 0:5], sp_out.at[BLK + t]))
        else:
            left(dall.at[t, :, 0:3], sp_out.at[BLK + t])
        left(dall.at[t, 0:3, s], f_out.at[F_D + t])
    left(hr.at[1:S], sp_out.at[END])
    left(vs.at[1:S], sp_out.at[VEC])
    left(qs.at[1:S], sp_out.at[SQ])
    left(tiles.at[0:3], f_out.at[F_TILE])
    left(h1.at[0:3], f_out.at[F_H1])
    left(vf.at[0:3], f_out.at[F_VEC])
    left(qf.at[0:3], f_out.at[F_SQ])


def sse_rows(sse):
    return sse + [jnp.zeros((128 - 32 - HOR, 1), F32)]


def step_fast(
    frames, targets, sizes, horizon, conv_weight, conv_m, conv_v, gates_vec, chan_vec
):
    S, F = lax.axis_size("space"), lax.axis_size("fsdp")
    R, N = conv_weight.shape
    rows, cols = frames.shape[3] * S, frames.shape[4]
    PX = 2 * rows * cols

    VM = pltpu.VMEM
    DMA = pltpu.SemaphoreType.DMA
    geo = (S, F, R, rows, PX)
    out = pl.pallas_call(
        functools.partial(step_kernel, geo),
        out_shape=(
            VM((2048, N), F32),
            VM((2048, N), F32),
            VM((R, N), F32),
            VM((R, N), F32),
            VM((8, 128), F32),
            VM((32, 256), F32),
            VM((32, 256), F32),
        ),
        in_specs=[pl.BlockSpec(memory_space=pltpu.HBM)] * 9,
        out_specs=(pl.BlockSpec(memory_space=VM),) * 7,
        scratch_shapes=[
            VM(frames.shape, F32),
            VM(frames.shape, F32),
            VM(frames.shape, jnp.int32),
            VM((1, 2), jnp.int32),
            VM(gates_vec.shape, F32),
            VM(chan_vec.shape, F32),
            VM((2, 4, 2, 8, 32, 128), BF16),
            VM((S, 2, 4, 2, 4, 32, 128), BF16),
            VM((640, 1280), BF16),
            VM((640, 1280), BF16),
            VM((1280, 640), BF16),
            VM((F, S, 8, 128), F32),
            VM((F, 2, 8, PX), F32),
            VM((5, 256, 128), F32),
            VM((1280, PX), BF16),
            VM((5, 128, PX), F32),
            VM((5, 256, PX), F32),
            VM((128, PX), F32),
            VM((2, 3, 128, PX), F32),
            VM((F, 256, PX), BF16),
            VM((S, 2, PX), F32),
            VM((640, PX), BF16),
            VM((256, PX), F32),
            VM((4, 32, PX), F32),
            VM((4, 32, PX), F32),
            VM((2, 4, 32, PX), BF16),
            VM((2, F, S, 32, PX), BF16),
            VM((F, PX, 256), BF16),
            VM((rows // 2, cols, 128), F32),
            VM((S, cols, 128), F32),
            VM((3, F, 4, 256, PX), BF16),
            VM((2, 8 * TAPS, PX), F32),
            VM((8, 128), F32),
            VM((F, 8, 128), F32),
            VM((S, 8, 128), F32),
            VM((F, 8, 128), F32),
            VM((S, 8, 128), F32),
            DMA((8,)),
            DMA((4,)),
            DMA((2, 4)),
            DMA((2, 4)),
            DMA((2, 3)),
            DMA((2, 4)),
            DMA((2, 2)),
            DMA((10,)),
            DMA((30,)),
            DMA((2,)),
            DMA((2, 4, 3, 2)),
            DMA((7,)),
            DMA((11,)),
        ],
        compiler_params=pltpu.CompilerParams(
            collective_id=0, has_side_effects=True, vmem_limit_bytes=44 * 2**20
        ),
    )(
        *(
            pltpu.with_memory_space_constraint(v, pltpu.HBM)
            for v in (
                frames, targets, horizon, sizes.reshape(1, 2), gates_vec, chan_vec,
                conv_weight, conv_m, conv_v,
            )
        )
    )
    return out


def adam_kernel(steps, *refs):
    small_ref, h_ref, c_ref, g_ref = refs[:4]
    (w_ref, m_ref, v_ref), gates, chan = refs[4:7], refs[7:10], refs[10:13]
    outs, held, sem, sems = refs[13:26], refs[26:39], refs[39], refs[40]
    conv_held, conv_outs = held[2:5], outs[2:5]
    factor = small_ref[5:6, 0:1]
    R = m_ref.shape[0]
    size = R // steps
    base = lax.rem(lax.axis_index("space") * R, 512)
    held[0][...] = small_ref[3:4, 0:1]
    held[1][...] = small_ref[4:5, 0:1]

    def update(weights, grad, news):
        w, m, v = weights
        for ref, new in zip(news, adam_update(w[...], m[...], v[...], grad * factor)):
            ref[...] = new

    update(gates, small_ref[0:2, :], held[5:8])
    chans = [small_ref[2:3, 32 * q : 32 * q + 32] for q in range(3)]
    update(chan, jnp.concatenate(chans, axis=0), held[8:11])
    for r in range(2):
        held[11][0, r] = h_ref[16 * r : 16 * r + 16, :]
        held[12][0, r] = c_ref[16 * r : 16 * r + 16, :]
    copies = []
    for n in (0, 1, *range(5, 13)):
        copies.append(pltpu.make_async_copy(held[n], outs[n], sem.at[n]))
        copies[-1].start()
    for n in range(steps):
        at = slice(size * n, size * n + size)
        moved = pl.ds(pl.multiple_of(base + size * n, 64), size)
        news = adam_update(w_ref[moved, :], m_ref[at, :], v_ref[at, :], g_ref[moved, :] * factor)
        for q, new in enumerate(news):
            conv_held[q][at, :] = new
            copies.append(
                pltpu.make_async_copy(conv_held[q].at[at, :], conv_outs[q].at[at, :], sems.at[q, n])
            )
            copies[-1].start()
    for copy in copies:
        copy.wait()


def adam_step(small, hidden, cell, grad, weights, frame_shape):
    steps = 5
    rows, cols = frame_shape
    conv, gates, chan = weights
    flat = [*conv, *gates, *chan]
    shapes = [v.shape for v in (*conv[1:], conv[1], *gates, *chan)]
    state = (1, rows, cols, hidden.shape[1])
    shapes = [(1, 1), (1, 1), *shapes, state, state]
    out = pl.pallas_call(
        functools.partial(adam_kernel, steps),
        out_shape=tuple(jax.ShapeDtypeStruct(v, F32) for v in shapes),
        in_specs=[pl.BlockSpec(memory_space=pltpu.VMEM)] * (4 + len(flat)),
        out_specs=(pl.BlockSpec(memory_space=pl.ANY),) * len(shapes),
        scratch_shapes=[pltpu.VMEM(v, F32) for v in shapes]
        + [pltpu.SemaphoreType.DMA((13,)), pltpu.SemaphoreType.DMA((3, steps))],
        compiler_params=pltpu.CompilerParams(vmem_limit_bytes=8 * 2**20),
    )(small, hidden, cell, grad, *flat)
    return (out[0].reshape(()), out[1].reshape(()), *out[2:])


def per_device_fast(
    frames, targets, sizes, horizon,
    conv_weight, conv_m, conv_v,
    gates_vec, gates_m, gates_v,
    chan_vec, chan_m, chan_v,
):
    grad, weight, first, second, small, hidden, cell = step_fast(
        frames, targets, sizes, horizon, conv_weight, conv_m, conv_v, gates_vec, chan_vec
    )
    weights = ((weight, first, second), (gates_vec, gates_m, gates_v), (chan_vec, chan_m, chan_v))
    return adam_step(small, hidden, cell, grad, weights, frames.shape[3:])


def fits(mesh, shapes):
    S, F = mesh.shape["space"], mesh.shape["fsdp"]
    frames, conv, chan = shapes
    return (
        (S, F) == (8, 4)
        and frames == (2, F, 2, 2 * S, 16)
        and conv == (TAPS * 512, 1024)
        and chan == (3, 256)
    )


def solution(mesh):
    in_specs = (
        P(None, "fsdp", None, "space", None),
        P(None, "fsdp", None, "space", None),
        P(None, "fsdp"),
        P(None, "fsdp", None, "space", None),
        P("space", "fsdp"),
        P("space", "fsdp"),
        P("space", "fsdp"),
        P(None, "space"),
        P(None, "space"),
        P(None, "space"),
        P(None, "space"),
        P(None, "space"),
        P(None, "space"),
    )
    out_specs = (
        P(),
        P(),
        P("space", "fsdp"),
        P("space", "fsdp"),
        P("space", "fsdp"),
        P(None, "space"),
        P(None, "space"),
        P(None, "space"),
        P(None, "space"),
        P(None, "space"),
        P(None, "space"),
        P("fsdp", "space", None, None),
        P("fsdp", "space", None, None),
    )

    def run(*args):
        shapes = (args[0].shape, args[4].shape, args[10].shape)
        body = per_device_fast if fits(mesh, shapes) else per_device
        return jax.shard_map(
            body, mesh=mesh, in_specs=in_specs, out_specs=out_specs, check_vma=False
        )(*args)

    return run
```

```python
import functools

import jax
import jax.numpy as jnp
from jax import lax
from jax.experimental import pallas as pl
from jax.experimental.pallas import tpu as pltpu
from jax.sharding import PartitionSpec as P

GROUPS = 32
HOR = 4
STEP = 10


EPS_NORM = 1e-05
CLIP = 0.01
RATE = 0.01
BETA1 = 0.9
BETA2 = 0.999
DECAY = 0.01
EPS_ADAM = 1e-08


def with_halo(shard, sides, width):
    for axis, dim in sides:
        count, length = (lax.axis_size(axis), shard.shape[dim])
        up = [(i, (i + 1) % count) for i in range(count - 1)]
        down = [(j, i) for i, j in up]
        last = lax.slice_in_dim(shard, length - width, length, axis=dim)
        first = lax.slice_in_dim(shard, 0, width, axis=dim)
        before = lax.ppermute(last, axis, up)
        after = lax.ppermute(first, axis, down)
        shard = jnp.concatenate([before, shard, after], axis=dim)
    return shard


def cell_head(gates, cell_prev, valid, head_w):
    width = cell_prev.shape[-1]
    gate_in = jax.nn.sigmoid(gates[..., :width])
    gate_forget = jax.nn.sigmoid(gates[..., width : 2 * width])
    gate_out = jax.nn.sigmoid(gates[..., 2 * width : 3 * width])
    candidate = jnp.tanh(gates[..., 3 * width :])
    cell_new = (gate_forget * cell_prev + gate_in * candidate) * valid
    hidden_new = gate_out * jnp.tanh(cell_new) * valid
    return (hidden_new, cell_new, jnp.sum(hidden_new * head_w, axis=-1))


def adam_update(weight, first, second, grad):
    first = BETA1 * first + (1.0 - BETA1) * grad
    second = BETA2 * second + (1.0 - BETA2) * grad * grad
    first_hat = first / (1.0 - BETA1**STEP)
    second_hat = second / (1.0 - BETA2**STEP)
    weight = weight - RATE * (first_hat / (jnp.sqrt(second_hat) + EPS_ADAM) + DECAY * weight)
    return (weight, first, second)


def gather_weights(conv_weight, gates_vec, chan_vec):
    col_block = lax.all_gather(conv_weight.astype(jnp.bfloat16), "fsdp", axis=1, tiled=True)
    kernel, gains, chans = (
        lax.all_gather(col_block, "space", axis=0, tiled=True),
        lax.all_gather(gates_vec.astype(jnp.bfloat16), "space", axis=1, tiled=True),
        lax.all_gather(chan_vec.astype(jnp.bfloat16), "space", axis=1, tiled=True),
    )
    inputs_n = kernel.shape[0] // 25
    gates_n = kernel.shape[1]
    flipped = (
        kernel.reshape(25, inputs_n, gates_n).transpose(0, 2, 1).reshape(25 * gates_n, inputs_n)
    )
    return (kernel, flipped, gains.astype(jnp.float32), chans.astype(jnp.float32))


def lifted_patches(joined):
    rows, cols = (joined.shape[1], joined.shape[2])
    padded = with_halo(joined, (("space", 1),), 2)
    padded = jnp.pad(padded, ((0, 0), (0, 0), (2, 2), (0, 0)))
    pieces = [padded[:, a : a + rows, b : b + cols, :] for a in range(5) for b in range(5)]
    return jnp.concatenate(pieces, -1).reshape(-1, 25 * joined.shape[3])


def spread_back(delta, flipped):
    rows, cols = (delta.shape[1], delta.shape[2])
    padded = with_halo(delta, (("space", 1),), 2)
    padded = jnp.pad(padded, ((0, 0), (0, 0), (2, 2), (0, 0)))
    pieces = [
        padded[:, 4 - a : 4 - a + rows, 4 - b : 4 - b + cols, :] for a in range(5) for b in range(5)
    ]
    stacked = jnp.concatenate(pieces, -1).reshape(-1, 25 * delta.shape[3])
    result = jnp.dot(stacked, flipped, preferred_element_type=jnp.float32)
    return result.reshape(delta.shape[0], rows, cols, -1)


def time_major(array):
    return jnp.moveaxis(array, 1, 0)


def forward(weights, seq, goal, chosen, inside, count, hweight):
    kernel, flipped, gains, chans = weights
    streams, nframes, rows, cols = seq.shape
    width = chans.shape[1]
    valid = inside[:, :, None, None]

    def forward_frame(carry, inputs):
        hidden, cell = carry
        pixels, target, picked = inputs
        lifted = (pixels[..., None] * chans[0] + chans[1]) * valid
        joined = jnp.concatenate([lifted, hidden], -1).astype(jnp.bfloat16)
        patches = lifted_patches(joined)
        pre = jnp.dot(patches, kernel, preferred_element_type=jnp.float32).reshape(
            streams, rows, cols, GROUPS, -1
        )
        weighted = pre * valid[..., None]
        first, second = lax.psum(
            (jnp.sum(weighted, axis=(1, 2, 4)), jnp.sum(weighted * pre, axis=(1, 2, 4))), "space"
        )
        centre = first / count[:, None]
        scale = lax.rsqrt(second / count[:, None] - centre * centre + EPS_NORM)
        normed = ((pre - centre[:, None, None, :, None]) * scale[:, None, None, :, None]).reshape(
            streams, rows, cols, 4 * width
        )
        gates = normed * gains[0] + gains[1]
        hidden_new, cell_new, output = cell_head(gates, cell, valid, chans[2])
        error = output - target
        sse = jnp.sum(picked * (error * error)[..., None], axis=(0, 1, 2))
        slope = 2.0 * error * jnp.sum(picked * hweight, axis=-1)
        return ((hidden_new, cell_new), (sse, (patches, normed, scale, cell, gates, slope)))

    zeros = jnp.zeros((streams, rows, cols, width), jnp.float32)
    (hidden, cell), (sse, kept) = lax.scan(
        forward_frame, (zeros, zeros), (time_major(seq), time_major(goal), time_major(chosen))
    )
    return (hidden, cell, jnp.sum(sse, axis=0), kept)


def backward(weights, kept, seq, inside, count):
    kernel, flipped, gains, chans = weights
    patches, normed, scale, cells, gates, slope = kept
    streams, nframes, rows, cols = seq.shape
    width = chans.shape[1]
    valid = inside[:, :, None, None]

    def cell_part(gate_vals, cell_prev, head_w):
        return cell_head(gate_vals, cell_prev, valid, head_w)

    def backward_frame(carry, inputs):
        d_hidden, d_cell, d_gain, d_bias, d_head, d_lift_w, d_lift_b = carry
        normed_t, scale_t, cell_prev, gates_t, slope_t, pixels = inputs
        unused, pull = jax.vjp(cell_part, gates_t, cell_prev, chans[2])
        d_gates, d_cell_prev, d_head_t = pull((d_hidden, d_cell, slope_t))
        d_normed = (d_gates * gains[0]).reshape(streams, rows, cols, GROUPS, -1)
        grouped = normed_t.reshape(streams, rows, cols, GROUPS, -1)
        masked = d_normed * valid[..., None]
        first, second = lax.psum(
            (jnp.sum(masked, axis=(1, 2, 4)), jnp.sum(masked * grouped, axis=(1, 2, 4))), "space"
        )
        first = (first / count[:, None])[:, None, None, :, None]
        second = (second / count[:, None])[:, None, None, :, None]
        d_pre = (
            scale_t[:, None, None, :, None]
            * (d_normed - first - grouped * second)
            * valid[..., None]
        )
        d_pre = d_pre.reshape(streams, rows, cols, -1).astype(jnp.bfloat16)
        d_joined = spread_back(d_pre, flipped)
        d_lifted = d_joined[..., :width] * valid
        carry_new = (
            d_joined[..., width:],
            d_cell_prev,
            d_gain + jnp.sum(d_gates * normed_t, axis=(0, 1, 2)),
            d_bias + jnp.sum(d_gates, axis=(0, 1, 2)),
            d_head + d_head_t,
            d_lift_w + jnp.sum(d_lifted * pixels[..., None], axis=(0, 1, 2)),
            d_lift_b + jnp.sum(d_lifted, axis=(0, 1, 2)),
        )
        return (carry_new, d_pre)

    zeros = jnp.zeros((streams, rows, cols, width), jnp.float32)
    wide_zero = jnp.zeros((4 * width,), jnp.float32)
    narrow_zero = jnp.zeros((width,), jnp.float32)
    start = (zeros, zeros, wide_zero, wide_zero, narrow_zero, narrow_zero, narrow_zero)
    final, d_pre_all = lax.scan(
        backward_frame, start, (normed, scale, cells, gates, slope, time_major(seq)), reverse=True
    )
    d_kernel = lax.dot_general(
        patches.reshape(-1, patches.shape[-1]),
        d_pre_all.reshape(-1, 4 * width),
        (((0,), (0,)), ((), ())),
        preferred_element_type=jnp.float32,
    )
    d_gains = jnp.stack([final[2], final[3]])
    d_chans = jnp.stack([final[5], final[6], final[4]])
    return (d_kernel, d_gains, d_chans)


def reduce_grads(d_kernel, d_gains, d_chans):
    col_part = lax.psum_scatter(d_kernel, "fsdp", scatter_dimension=1, tiled=True)
    kernel_part, gains_part, chans_part = (
        lax.psum_scatter(col_part, "space", scatter_dimension=0, tiled=True),
        lax.psum_scatter(d_gains, "space", scatter_dimension=1, tiled=True),
        lax.psum_scatter(d_chans, "space", scatter_dimension=1, tiled=True),
    )
    gains_part, chans_part = lax.psum((gains_part, chans_part), "fsdp")
    return (kernel_part, gains_part, chans_part)


def per_device(
    frames,
    targets,
    sizes,
    horizon,
    conv_weight,
    conv_m,
    conv_v,
    gates_vec,
    gates_m,
    gates_v,
    chan_vec,
    chan_m,
    chan_v,
):
    micro, streams, nframes, rows, cols = frames.shape
    width = chan_vec.shape[1] * lax.axis_size("space")
    total_rows = rows * lax.axis_size("space")
    row_ids = lax.axis_index("space") * rows + jnp.arange(rows, dtype=jnp.int32)
    inside = (row_ids[None, None, :] >= total_rows - sizes[:, :, None]).astype(jnp.float32)
    select = (horizon[..., None] == jnp.arange(HOR, dtype=jnp.int32)).astype(jnp.float32) * inside[
        :, :, None, :, None, None
    ]
    counts = lax.psum(jnp.sum(select, axis=(0, 1, 2, 3, 4)), ("space", "fsdp"))
    hweight = 1.0 / (HOR * jnp.maximum(counts, 1.0))
    group_count = sizes.astype(jnp.float32) * (cols * (4 * width // GROUPS))
    held = gather_weights(conv_weight, gates_vec, chan_vec)
    sse_total = jnp.zeros((HOR,), jnp.float32)
    summed = None
    for batch in range(micro):
        hidden, cell, sse, kept = forward(
            held,
            frames[batch],
            targets[batch],
            select[batch],
            inside[batch],
            group_count[batch],
            hweight,
        )
        sse_total = sse_total + sse
        grads = backward(held, kept, frames[batch], inside[batch], group_count[batch])
        summed = grads if summed is None else jax.tree.map(jnp.add, summed, grads)
    summed = reduce_grads(*summed)
    kernel_grad, gains_grad, chans_grad = summed
    leading = (lax.axis_index("fsdp") == 0).astype(jnp.float32)
    squares = jnp.sum(kernel_grad * kernel_grad) + leading * (
        jnp.sum(gains_grad * gains_grad) + jnp.sum(chans_grad * chans_grad)
    )
    sse_total, squares = lax.psum((sse_total, squares), ("space", "fsdp"))
    loss = jnp.sum(sse_total * hweight)
    norm = jnp.sqrt(squares)
    factor = jnp.minimum(1.0, CLIP / (norm + 1e-06))
    conv_new, conv_m_new, conv_v_new = adam_update(
        conv_weight, conv_m, conv_v, kernel_grad * factor
    )
    gates_new, gates_m_new, gates_v_new = adam_update(
        gates_vec, gates_m, gates_v, gains_grad * factor
    )
    chan_new, chan_m_new, chan_v_new = adam_update(chan_vec, chan_m, chan_v, chans_grad * factor)
    return (
        loss,
        norm,
        conv_new,
        conv_m_new,
        conv_v_new,
        gates_new,
        gates_m_new,
        gates_v_new,
        chan_new,
        chan_m_new,
        chan_v_new,
        hidden,
        cell,
    )


MESH = pl.DeviceIdType.MESH
F32 = jnp.float32
BF16 = jnp.bfloat16
TAPS = 25


def low(v):
    return v.astype(BF16).astype(F32)


def dot(a, b):
    return jnp.dot(a, b, preferred_element_type=F32)


def dot_nt(a, b):
    return lax.dot_general(a, b, (((1,), (1,)), ((), ())), preferred_element_type=F32)


def step_kernel(
    geo,
    frames_in,
    targets_in,
    horizon_in,
    sizes_in,
    gates_in,
    chan_in,
    w_ref,
    m_ref,
    v_ref,
    grad,
    wf,
    m_out,
    v_out,
    small_ref,
    h_ref,
    c_ref,
    frames_ref,
    targets_ref,
    horizon_ref,
    sizes_ref,
    gates_ref,
    chan_ref,
    stage,
    wr,
    wl,
    wh,
    wht,
    tiles,
    pix,
    cols,
    xb,
    sa,
    sb,
    pre1,
    save,
    h1,
    yrow,
    dst,
    dhp,
    dhy,
    dhr,
    d_own,
    dall,
    dt,
    ht,
    hr,
    xt,
    ps,
    vt,
    vf,
    vs,
    qf,
    qs,
    in_sem,
    w_sem,
    w_out,
    w_in,
    x_out,
    x_in,
    c_in,
    sp_out,
    sp_in,
    y_out,
    chain_in,
    f_out,
    f_in,
):
    S, F, R, rows, PX = geo
    width = 8 * 32
    s, f = lax.axis_index("space"), lax.axis_index("fsdp")
    xx, cc = f // 2, lax.rem(f, 2)
    f_x, f_c, f_d = (1 - xx) * 2 + cc, xx * 2 + 1 - cc, (1 - xx) * 2 + 1 - cc
    fpeers = (f_x, f_c, f_d)

    def ahead(k):
        return lax.rem(s + k, S)

    def behind(k):
        return lax.rem(s - k + S, S)

    def only(when, do):
        if when is None:
            do()
        else:
            pl.when(when)(do)

    def copy_to(src, dst_, ssem, rsem, dev):
        return pltpu.make_async_remote_copy(
            src_ref=src, dst_ref=dst_, send_sem=ssem, recv_sem=rsem,
            device_id=dev, device_id_type=MESH,
        )

    def send(src, dst_, ssem, rsem, dev, priority=0):
        copy_to(src, dst_, ssem, rsem, dev).start(priority=priority)

    def arrived(slot, rsem):
        copy_to(slot, slot, rsem, rsem, (s, f_c)).wait_recv()

    def left(slot, ssem):
        copy_to(slot, slot, ssem, ssem, (s, f_c)).wait_send()

    def each(first, last, do):
        def step(k, carry):
            do(k)
            return carry

        lax.fori_loop(first, last, step, 0)

    TILE, H1, Y, DHY, DHL, BLK, END, VEC, SQ = 0, 1, 2, 3, 4, 5, 7, 8, 9
    DHY_IN, LINE_IN, ACROSS_IN = 10, 14, 22
    F_TILE, F_H1, F_H1C, F_VEC, F_SQ, F_D = 0, 1, 2, 3, 4, 5

    barrier = pltpu.get_barrier_semaphore()
    for k in range(1, S):
        pl.semaphore_signal(barrier, inc=1, device_id=(ahead(k), f), device_id_type=MESH)
    for p in fpeers:
        pl.semaphore_signal(barrier, inc=1, device_id=(s, p), device_id_type=MESH)
    small_ins = []
    for n, (src, held) in enumerate(
        (
            (frames_in, frames_ref), (targets_in, targets_ref), (horizon_in, horizon_ref),
            (sizes_in, sizes_ref), (gates_in, gates_ref), (chan_in, chan_ref),
        )
    ):
        small_ins.append(pltpu.make_async_copy(src, held, in_sem.at[n]))
        small_ins[-1].start()
    base = lax.rem(s * R, 2 * width)
    zero_rows = jnp.zeros((2 * width, wf.shape[1]), F32)
    wf[0 : 2 * width, :] = zero_rows
    wf[wf.shape[0] - 2 * width :, :] = zero_rows
    get_w = []
    for q in range(4):
        own_w = wf.at[pl.ds(pl.multiple_of(base + R // 4 * q, 16), R // 4), :]
        get_w.append(
            pltpu.make_async_copy(w_ref.at[R // 4 * q : R // 4 * (q + 1), :], own_w, w_sem.at[q])
        )
        get_w[-1].start()

    pl.semaphore_wait(barrier, S - 1 + 3)

    def holders(kind, i):
        lo = 512 * i + 256 * kind
        return [q for q in range(S) if (q * R) % 512 + R > lo and (q * R) % 512 < lo + 256]

    def holds(src, kind, i):
        if len(holders(kind, i)) == S:
            return None
        lo, first = 512 * i + 256 * kind, lax.rem(src * R, 512)
        return (lo < first + R) & (lo + 256 > first)

    def stage_slot(kind, i):
        for j in range(2):
            r0 = 512 * i + 256 * kind + 128 * j
            block = wf[r0 : r0 + 128, :].T.astype(BF16)
            stage[kind, i, j] = block.reshape(8, 32, 128)

    def send_slot(kind, i):
        def to(k):
            send(
                stage.at[kind, i, :, ahead(k)], wr.at[s, kind, i, :, f],
                w_out.at[kind, i], w_in.at[kind, i], (ahead(k), f),
            )

        only(holds(s, kind, i), lambda: each(1, S, to))

    order = {kind: sorted(range(4), key=lambda i: -len(holders(kind, i))) for kind in range(2)}
    for q in (0, 1):
        get_w[q].wait()
    stage_slot(0, order[0][0])
    send_slot(0, order[0][0])
    for cp in small_ins:
        cp.wait()

    def line(ref):
        parts = [
            ref[m, 0, t, r : r + 1, :].astype(F32)
            for t in range(2) for r in range(2) for m in range(2)
        ]
        return jnp.concatenate(parts, axis=1)

    lane128 = lax.broadcasted_iota(jnp.int32, (1, 128), 1)
    tall = jnp.where(lax.rem(lane128 // 16, 2) == 0, sizes_ref[0:1, 0:1], sizes_ref[0:1, 1:2])
    chans = [chan_ref[q : q + 1, :] for q in range(3)] + [jnp.zeros((1, 32), F32)]
    tiles[f, s] = jnp.concatenate(
        [
            line(frames_ref), line(targets_ref), line(horizon_ref), gates_ref[...],
            jnp.concatenate(chans, axis=1), tall.astype(F32), jnp.zeros((1, 128), F32),
        ],
        axis=0,
    )
    each(1, S, lambda k: send(
        tiles.at[f, s], tiles.at[f, s], sp_out.at[TILE], sp_in.at[TILE], (ahead(k), f)
    ))
    for q in (2, 3):
        get_w[q].wait()
    for i in order[0][1:]:
        stage_slot(0, i)
        send_slot(0, i)
    for i in order[1]:
        stage_slot(1, i)
        send_slot(1, i)
    for i in range(4):
        wr[s, 0, i, :, f] = stage[0, i, :, s]

    arrived(tiles.at[f, 1:S], sp_in.at[TILE])
    for p in fpeers:
        send(tiles.at[f], tiles.at[f], f_out.at[F_TILE], f_in.at[F_TILE], (s, p))

    lane = lax.broadcasted_iota(jnp.int32, (1, PX), 1)
    row_of = lane // 32
    micro_of = lax.rem(lane // 16, 2)
    col_of = lax.rem(lane, 16)

    def build_pix(p):
        for t in range(2):
            halves = []
            for k in range(4):
                left = tiles[p, 2 * k][:, t * 64 : t * 64 + 64]
                right = tiles[p, 2 * k + 1][:, t * 64 : t * 64 + 64]
                halves.append(jnp.concatenate([left, right], axis=1))
            whole = jnp.concatenate(halves, axis=1)
            within = (row_of.astype(F32) >= rows - whole[6:7, :]).astype(F32)
            sub = lax.broadcasted_iota(jnp.int32, (8, PX), 0)
            pix[p, t] = jnp.where(sub == 7, within, whole)

    build_pix(f)

    sub32 = lax.broadcasted_iota(jnp.int32, (32, 128), 0)
    lane32 = lax.broadcasted_iota(jnp.int32, (32, 128), 1)

    def column(row, first):
        picked = jnp.where(lane32 == sub32 + first, row, 0.0)
        return low(jnp.sum(picked, axis=1, keepdims=True))

    for g in range(4):
        at = 2 * g + s // 4
        off = 32 * lax.rem(s, 4)
        for q in range(2):
            cols[q, 32 * g : 32 * g + 32, :] = jnp.broadcast_to(
                column(tiles[f, at][3 + q : 4 + q, :], off), (32, 128)
            )
    cols[2, 0:32, :] = jnp.broadcast_to(column(tiles[f, s][5:6, :], 64), (32, 128))
    for k in range(8):
        row5 = tiles[f, k][5:6, :]
        for q in range(2):
            cols[3 + q, 32 * k : 32 * k + 32, :] = jnp.broadcast_to(
                column(row5, 32 * q), (32, 128)
            )

    gain, shift, head = cols[0, 0:128, 0:1], cols[1, 0:128, 0:1], cols[2, 0:32, 0:1]

    def lifted(pixels, within):
        return ((pixels * cols[3, :, 0:1] + cols[4, :, 0:1]) * within).astype(BF16)

    inside = pix[f, 0, 7:8, :]

    def relay(kind):
        counts = [len(holders(kind, i)) for i in range(4)]

        def first_hop(i):
            when = holds(s, kind, i)
            n = counts[i]
            if when is None:
                arrived(wr.at[1:S, kind, i, :, f], w_in.at[kind, i])
            else:
                pl.when(when)(lambda: arrived(wr.at[1:n, kind, i, :, f], w_in.at[kind, i]))
                other = jnp.logical_not(when)
                pl.when(other)(lambda: arrived(wr.at[0:n, kind, i, :, f], w_in.at[kind, i]))

            def hop(k):
                src = behind(k)
                block = wr.at[src, kind, i, :, f]

                def go():
                    send(block, block, x_out.at[kind, 0], x_in.at[kind, i], (s, f_x))
                    send(block, block, x_out.at[kind, 1], c_in.at[kind, 0], (s, f_c))

                only(holds(src, kind, i), go)

            each(0, S, hop)

        def second_hop(i):
            arrived(wr.at[0 : counts[i], kind, i, :, f_x], x_in.at[kind, i])

            def hop(k):
                src = behind(k)
                block = wr.at[src, kind, i, :, f_x]
                only(
                    holds(src, kind, i),
                    lambda: send(block, block, x_out.at[kind, 2], c_in.at[kind, 1], (s, f_c)),
                )

            each(0, S, hop)

        def finish():
            blocks = sum(counts) // 4
            arrived(wr.at[0:blocks, kind, :, :, f_c], c_in.at[kind, 0])
            arrived(wr.at[0:blocks, kind, :, :, f_d], c_in.at[kind, 1])

        def first(n):
            first_hop(order[kind][n])

        def second(n):
            second_hop(order[kind][n])

        return first, second, finish

    first_l, second_l, finish_l = relay(0)
    first_h, second_h, finish_h = relay(1)

    def merge(kind, out):
        for tap in range(TAPS):
            lo = 512 * tap + 256 * kind
            total = None
            for sp in range(S):
                if sp * R < lo + 256 and sp * R + R > lo:
                    part = wr[sp, kind, tap - (sp * R) // 512]
                    total = part if total is None else total + part
            total = total.reshape(2, 128, 128)
            a, b = tap // 5, tap % 5
            out[128 * a : 128 * a + 128, 256 * b : 256 * b + 128] = total[0]
            out[128 * a : 128 * a + 128, 256 * b + 128 : 256 * b + 256] = total[1]

    cmask = [
        ((col_of + (b - 2) >= 0) & (col_of + (b - 2) < 16)).astype(F32) for b in range(5)
    ]
    rmask = [
        ((row_of + (a - 2) >= 0) & (row_of + (a - 2) < rows)).astype(F32) for a in range(5)
    ]

    def slide(v, d):
        if d == 0:
            return v
        parts = [
            pltpu.roll(v[:, q : q + 128], (-d) % 128, 1) for q in range(0, v.shape[1], 128)
        ]
        return jnp.concatenate(parts, axis=1) * cmask[d + 2]

    def conv(weights):
        sa[...] = dot(weights[...], xb[...]).reshape(5, 128, PX)
        out = sa[2]
        for a in (0, 1, 3, 4):
            out = out + pltpu.roll(sa[a], (-32 * (a - 2)) % PX, 1) * rmask[a]
        return out

    def slid_lift(t):
        line = jnp.concatenate([pix[f, t, 0:1, :], inside], axis=0)
        for b in range(5):
            moved = slide(line, b - 2)
            xb[256 * b : 256 * b + 256, :] = lifted(moved[0:1], moved[1:2])

    count = pix[f, 0, 6:7, :] * (16.0 * 32.0)

    def per_stream(v):
        first = jnp.sum(jnp.where(micro_of == 0, v, 0.0), axis=1, keepdims=True)
        second = jnp.sum(jnp.where(micro_of == 0, 0.0, v), axis=1, keepdims=True)
        return jnp.where(micro_of == 0, first, second)

    def cell_forward(t, pre, cell_prev):
        groups = [pre[32 * g : 32 * g + 32, :] for g in range(4)]
        sums = [
            jnp.sum(v * inside, axis=0, keepdims=True) for v in groups
        ] + [jnp.sum(v * inside * v, axis=0, keepdims=True) for v in groups]
        sums = per_stream(jnp.concatenate(sums, axis=0)) / count
        centre = sums[0:4]
        scale = lax.rsqrt(sums[4:8] - centre * centre + EPS_NORM)
        acts = []
        for g in range(4):
            normed = (groups[g] - centre[g : g + 1]) * scale[g : g + 1]
            save[t, 0, 32 * g : 32 * g + 32, :] = normed
            z = normed * gain[32 * g : 32 * g + 32] + shift[32 * g : 32 * g + 32]
            act = jnp.tanh(z) if g == 3 else 1.0 / (1.0 + jnp.exp(-z))
            save[t, 1, 32 * g : 32 * g + 32, :] = act
            acts.append(act)
        i, fo, o, cand = acts
        cell = i * cand * inside if cell_prev is None else (fo * cell_prev + i * cand) * inside
        tanh_c = jnp.tanh(cell)
        hidden = o * tanh_c * inside
        save[t, 2, 0:8, :] = jnp.concatenate([scale, scale], axis=0)
        save[t, 2, 32:64, :] = cell
        save[t, 2, 64:96, :] = tanh_c
        save[t, 2, 96:128, :] = hidden
        yrow[s, t : t + 1, :] = jnp.sum(hidden * head, axis=0, keepdims=True)
        return hidden, cell

    moments = [
        pltpu.make_async_copy(m_ref, m_out, in_sem.at[6]),
        pltpu.make_async_copy(v_ref, v_out, in_sem.at[7]),
    ]
    for cp in moments:
        cp.start()
    slid_lift(0)
    for i in range(4):
        wr[s, 1, i, :, f] = stage[1, i, :, s]
    first_l(0)
    for n in range(1, 4):
        first_l(n)
        second_l(n - 1)
    first_h(0)
    second_l(3)
    first_h(1)
    finish_l()
    merge(0, wl)
    hidden0, cell0 = cell_forward(0, conv(wl), None)
    mine = pl.ds(pl.multiple_of(32 * s, 32), 32)
    h1[f, mine, :] = hidden0.astype(BF16)
    each(1, S, lambda k: send(
        h1.at[f, mine, :], h1.at[f, mine, :], sp_out.at[H1], sp_in.at[H1], (ahead(k), f)
    ))

    first_h(2)
    second_h(0)
    second_h(1)
    first_h(3)
    second_h(2)
    second_h(3)
    finish_h()
    slid_lift(1)
    pre1[...] = conv(wl)
    merge(1, wh)
    for a in range(5):
        for b in range(5):
            block = wh[128 * a : 128 * a + 128, 256 * b : 256 * b + 256]
            wht[256 * a : 256 * a + 256, 128 * b : 128 * b + 128] = block.astype(F32).T.astype(BF16)
    arrived(h1.at[f, 32 : 32 * S, :], sp_in.at[H1])
    send(h1.at[f], h1.at[f], f_out.at[F_H1], f_in.at[F_H1], (s, f_x))
    send(h1.at[f], h1.at[f], f_out.at[F_H1], f_in.at[F_H1C], (s, f_c))
    hidden_in = h1[f].astype(F32)
    for b in range(5):
        xb[256 * b : 256 * b + 256, :] = slide(hidden_in, b - 2).astype(BF16)
    pre1[...] = pre1[...] + conv(wh)
    hidden1, cell1 = cell_forward(1, pre1[...], cell0)
    each(1, S, lambda k: send(
        yrow.at[s], yrow.at[s], sp_out.at[Y], sp_in.at[Y], (ahead(k), f)
    ))

    arrived(tiles.at[0:3], f_in.at[F_TILE])
    for p in fpeers:
        build_pix(p)
    weight_rows = []
    for k in range(HOR):
        total = None
        for p in range(F):
            for t in range(2):
                picked = jnp.where(pix[p, t, 2:3, :] == float(k), pix[p, t, 7:8, :], 0.0)
                total = picked if total is None else total + picked
        counted = jnp.sum(total, axis=1, keepdims=True)
        weight_rows.append(1.0 / (HOR * jnp.maximum(counted, 1.0)))
    state = jnp.concatenate([hidden1, cell1, hidden1, cell1], axis=0).T
    state = state.reshape(rows // 2, 2, 2, 16, 128)
    ht[...] = jnp.where(
        lax.broadcasted_iota(jnp.int32, (rows // 2, 16, 128), 2) < 64,
        state[:, 0, 1], state[:, 1, 1],
    )
    hr[s] = ht[s]

    first_tap = (s * R) // 512

    def tap_inputs(n, carry):
        p, i = n // 4, lax.rem(n, 4)
        tap = first_tap + i
        da, db = tap // 5 - 2, lax.rem(tap, 5) - 2
        back = lax.rem(2 * PX - 32 * da - db, PX)
        ok = (row_of + da >= 0) & (row_of + da < rows) & (col_of + db >= 0) & (col_of + db < 16)
        ok = ok.astype(F32)
        for t in range(2):
            moved = pltpu.roll(pix[p, t], back, 1)
            xt[t, p, i] = lifted(moved[0:1], moved[7:8] * ok)
        return carry

    lax.fori_loop(0, 4 * F, tap_inputs, 0)
    arrived(yrow.at[1:S], sp_in.at[Y])
    ysum = yrow[0]
    for k in range(1, S):
        ysum = ysum + yrow[k]
    slopes, sse = [], [None] * HOR
    for t in range(2):
        err = ysum[t : t + 1] - pix[f, t, 1:2, :]
        which = pix[f, t, 2:3, :]
        hw = jnp.zeros((1, PX), F32)
        for k in range(HOR):
            chosen = jnp.where(which == float(k), inside, 0.0)
            hw = hw + chosen * weight_rows[k]
            part = chosen * (err * err)
            sse[k] = part if sse[k] is None else sse[k] + part
        slopes.append(2.0 * err * hw)
    sse = [jnp.sum(v, axis=1, keepdims=True) for v in sse]

    def cell_backward(t, d_hidden, d_cell, cell_prev):
        slope = slopes[t]
        i, fo = save[t, 1, 0:32, :], save[t, 1, 32:64, :]
        o, cand = save[t, 1, 64:96, :], save[t, 1, 96:128, :]
        tanh_c, hidden = save[t, 2, 64:96, :], save[t, 2, 96:128, :]
        dh = slope * head
        if d_hidden is not None:
            dh = dh + d_hidden
        dh = dh * inside
        d_o = dh * tanh_c
        dc = dh * o * (1.0 - tanh_c * tanh_c)
        if d_cell is not None:
            dc = dc + d_cell
        dc = dc * inside
        d_f = jnp.zeros_like(dc) if cell_prev is None else dc * cell_prev
        raw = [
            dc * cand * i * (1.0 - i),
            d_f * fo * (1.0 - fo),
            d_o * o * (1.0 - o),
            dc * i * (1.0 - cand * cand),
        ]
        scale = save[t, 2, 0:8, :]
        d_head = jnp.sum(hidden * slope, axis=1, keepdims=True)
        d_gain, d_shift, dn, sums = [], [], [], [[], []]
        for g in range(4):
            normed = save[t, 0, 32 * g : 32 * g + 32, :]
            d_gain.append(jnp.sum(raw[g] * normed, axis=1, keepdims=True))
            d_shift.append(jnp.sum(raw[g], axis=1, keepdims=True))
            v = raw[g] * gain[32 * g : 32 * g + 32]
            dn.append(v)
            sums[0].append(jnp.sum(v * inside, axis=0, keepdims=True))
            sums[1].append(jnp.sum(v * inside * normed, axis=0, keepdims=True))
        sums = per_stream(jnp.concatenate(sums[0] + sums[1], axis=0)) / count
        for g in range(4):
            normed = save[t, 0, 32 * g : 32 * g + 32, :]
            d_pre = scale[g : g + 1] * (dn[g] - sums[g : g + 1] - normed * sums[4 + g : 5 + g])
            d_own[t, g] = (d_pre * inside).astype(BF16)
        return (
            dc * fo,
            d_head,
            jnp.concatenate(d_gain, axis=0),
            jnp.concatenate(d_shift, axis=0),
        )

    def share_gates(t):
        for n, p in enumerate(fpeers):
            send(
                d_own.at[t, p], dall.at[t, f, s], f_out.at[F_D + t], f_in.at[F_D + 3 * t + n], (s, p)
            )
        dall[t, f, s] = d_own[t, f]

    z, y = s // 2, lax.rem(s, 2)
    across = 2 * z + 1 - y

    def line_peer(k):
        return lax.rem(z + k, 4) * 2 + y

    def line_source(k):
        return lax.rem(z + 4 - k, 4) * 2 + y

    pieces = ((f, None), (f_c, 1), (f_x, 0), (f_d, 2))

    def share_piece(t, n):
        p, peer = pieces[n]
        block = dall.at[t, p, s]
        if peer is not None:
            arrived(block, f_in.at[F_D + 3 * t + peer])
        if CHAIN[t]:
            for way in range(2):
                pass_on(t, n, 0, way, block)
        else:
            for k in (2, 3, 1):
                send(
                    block, block, sp_out.at[BLK + t], sp_in.at[LINE_IN + 4 * t + n],
                    (line_peer(k), f),
                )
        send(block, block, y_out.at[t], sp_in.at[ACROSS_IN + 4 * t + n], (across, f))

    def pass_on(t, n, hop, way, block):
        inside_line, to = ((z < 3, z + 1), (z > 0, z - 1))[way]
        pl.when(inside_line)(lambda: send(
            block, block, sp_out.at[BLK + t], chain_in.at[t, n, hop, way], (2 * to + y, f)
        ))

    def relay_hop(t, n, hop):
        p, unused = pieces[n]
        for way, there in ((0, z >= hop), (1, z + hop <= 3)):
            block = dall.at[t, p, 2 * lax.rem(z + (4 - hop, hop)[way], 4) + y]

            def come():
                arrived(block, chain_in.at[t, n, hop - 1, way])
                if hop < 3:
                    pass_on(t, n, hop, way, block)
                send(block, block, y_out.at[t], sp_in.at[ACROSS_IN + 4 * t + n], (across, f))

            pl.when(there)(come)

    def relay_wave(t, wave):
        if CHAIN[t]:
            for hop in range(1, 4):
                if 0 <= wave - hop < 4:
                    relay_hop(t, wave - hop, hop)
            return
        n = wave - 1
        p, unused = pieces[n]
        arrived(dall.at[t, p, 0:3], sp_in.at[LINE_IN + 4 * t + n])
        for k in (1, 3, 2):
            block = dall.at[t, p, line_source(k)]
            send(block, block, y_out.at[t], sp_in.at[ACROSS_IN + 4 * t + n], (across, f))

    CHAIN = (True, False)
    WAVES = [6 if chain else 4 for chain in CHAIN]

    def gathered(t, n):
        p, unused = pieces[n]
        arrived(dall.at[t, p, 0:4], sp_in.at[ACROSS_IN + 4 * t + n])
        dt[p] = dall[t, p].reshape(256, PX).astype(F32).T.astype(BF16)
        return p

    each(1, S, lambda k: send(
        ht.at[ahead(k)], hr.at[s], sp_out.at[END], sp_in.at[END], (ahead(k), f)
    ))
    d_cell0, d_head1, d_gain1, d_shift1 = cell_backward(1, None, None, cell0)
    share_gates(1)

    d1 = d_own[1].reshape(128, PX).astype(F32)
    for b in range(5):
        dst[128 * b : 128 * b + 128, :] = slide(d1, 2 - b).astype(BF16)
    sb[...] = dot(wht[...], dst[...]).reshape(5, 256, PX)
    dh = sb[2]
    for a in (0, 1, 3, 4):
        dh = dh + pltpu.roll(sb[a], (32 * (a - 2)) % PX, 1) * rmask[4 - a]
    dhp[...] = dh
    steps = (2, 1, 3, 0)

    def part_of(zz, yy):
        return pl.ds(pl.multiple_of(32 * (2 * zz + yy), 32), 32)

    for k in steps:
        zz = lax.rem(z + k, 4)
        send(
            dhp.at[part_of(zz, 1 - y), :], dhy.at[k], sp_out.at[DHY], sp_in.at[DHY_IN + k], (across, f)
        )
    for k in steps:
        zz = lax.rem(z + k, 4)
        arrived(dhy.at[k], sp_in.at[DHY_IN + k])
        both = dhp[part_of(zz, y), :] + dhy[k]
        if k == 0:
            dhr[z] = both
        else:
            dhy[k] = both
            send(
                dhy.at[k], dhr.at[z], sp_out.at[DHL], sp_in.at[DHL], (line_peer(k), f)
            )
    for n in range(4):
        share_piece(1, n)

    arrived(h1.at[f_x], f_in.at[F_H1])
    send(h1.at[f_x], h1.at[f_x], f_out.at[F_H1], f_in.at[F_H1C], (s, f_c))
    arrived(h1.at[0:2], f_in.at[F_H1C])

    def tap_hidden(n, carry):
        p, i = n // 4, lax.rem(n, 4)
        tap = first_tap + i
        da, db = tap // 5 - 2, lax.rem(tap, 5) - 2
        back = lax.rem(2 * PX - 32 * da - db, PX)
        ok = (row_of + da >= 0) & (row_of + da < rows) & (col_of + db >= 0) & (col_of + db < 16)
        xt[2, p, i] = (pltpu.roll(h1[p].astype(F32), back, 1) * ok.astype(F32)).astype(BF16)
        return carry

    lax.fori_loop(0, 4 * F, tap_hidden, 0)

    def moved_pixels(t):
        pixels = pix[f, t, 0:1, :] * inside
        high = low(pixels)
        mid = low(pixels - high)
        rest = low(pixels - high - mid)
        four = jnp.concatenate([high, mid, rest, inside, jnp.zeros((4, PX), F32)], axis=0)
        for a in range(5):
            lines = four if a == 2 else pltpu.roll(four, (-32 * (a - 2)) % PX, 1) * rmask[a]
            for b in range(5):
                n = 8 * (5 * a + b)
                ps[t, n : n + 8, :] = slide(lines, b - 2)
        return dot_nt(d_own[t].reshape(128, PX), ps[t].astype(BF16))

    q1 = moved_pixels(1)

    arrived(dhr.at[0:3], sp_in.at[DHL])
    d_hidden0 = (dhr[0] + dhr[1]) + (dhr[2] + dhr[3])
    unused, d_head0, d_gain0, d_shift0 = cell_backward(0, d_hidden0, d_cell0, None)
    share_gates(0)
    share_piece(0, 0)

    q = q1 + moved_pixels(0)
    total_w = jnp.zeros((128, 256), F32)
    total_b = jnp.zeros((128, 256), F32)
    for tap in range(TAPS):
        a, b = tap // 5, tap % 5
        w = wl[128 * a : 128 * a + 128, 256 * b : 256 * b + 256].astype(F32)
        n = 8 * tap
        total_w = total_w + w * (q[:, n : n + 1] + q[:, n + 1 : n + 2] + q[:, n + 2 : n + 3])
        total_b = total_b + w * q[:, n + 3 : n + 4]
    lift_w = jnp.sum(total_w, axis=0, keepdims=True)
    lift_b = jnp.sum(total_b, axis=0, keepdims=True)

    relay_wave(1, 1)
    share_piece(0, 1)
    relay_wave(1, 2)
    for n in range(2, 4):
        share_piece(0, n)
    relay_wave(1, 3)

    lane_sq = lax.broadcasted_iota(jnp.int32, (128, 128), 1)
    d_head = jnp.concatenate(
        [d_head0 + d_head1] + sse_rows(sse), axis=0
    )
    packed = jnp.where(lane_sq == 0, d_gain0 + d_gain1, 0.0)
    packed = jnp.where(lane_sq == 1, d_shift0 + d_shift1, packed)
    packed = jnp.where(lane_sq == 2, d_head, packed)
    packed = packed.T[0:3, :]
    vt[...] = jnp.concatenate(
        [packed, lift_w[:, 0:128], lift_w[:, 128:256], lift_b[:, 0:128], lift_b[:, 128:256],
         jnp.zeros((1, 128), F32)], axis=0,
    )
    vf[f] = vt[...]
    for p in fpeers:
        send(vt, vf.at[f], f_out.at[F_VEC], f_in.at[F_VEC], (s, p))
    for wave in range(4, WAVES[1] + 1):
        relay_wave(1, wave)
    arrived(vf.at[0:3], f_in.at[F_VEC])
    vs[s] = (vf[0] + vf[1]) + (vf[2] + vf[3])
    each(1, S, lambda k: send(
        vs.at[s], vs.at[s], sp_out.at[VEC], sp_in.at[VEC], (ahead(k), f)
    ))

    for wave in range(1, WAVES[0] + 1):
        relay_wave(0, wave)
    for n in range(4):
        gathered(1, n)

    def grad_one(i, carry):
        for kind in range(2):
            total = None
            for p in range(F):
                part = dot(xt[1 + kind, p, i], dt[p])
                total = part if total is None else total + part
            grad[pl.ds(pl.multiple_of(512 * i + 256 * kind, 256), 256), :] = total
        return carry

    lax.fori_loop(0, 4, grad_one, 0)

    for n in range(4):
        p = gathered(0, n)

        def grad_zero(i):
            at = pl.ds(pl.multiple_of(512 * i, 256), 256)
            grad[at, :] = grad[at, :] + dot(xt[0, p, i], dt[p])

        each(0, 4, grad_zero)

    def square(n, carry):
        v = grad[pl.ds(pl.multiple_of(base + 64 * n, 64), 64), :]
        return carry + v * v

    total = lax.fori_loop(0, R // 64, square, jnp.zeros((64, 256), F32))
    qf[f] = jnp.full((8, 128), jnp.sum(total), F32)
    for p in fpeers:
        send(qf.at[f], qf.at[f], f_out.at[F_SQ], f_in.at[F_SQ], (s, p))
    arrived(hr.at[1:S], sp_in.at[END])
    for k in range(S):
        for r in range(2):
            h_ref[16 * r : 16 * r + 16, 32 * k : 32 * k + 32] = hr[k, :, 64 * r : 64 * r + 32]
            c_ref[16 * r : 16 * r + 16, 32 * k : 32 * k + 32] = hr[k, :, 64 * r + 32 : 64 * r + 64]

    arrived(vs.at[1:S], sp_in.at[VEC])
    lane8 = lax.broadcasted_iota(jnp.int32, (8, 128), 1)
    sub8 = lax.broadcasted_iota(jnp.int32, (8, 128), 0)
    lift = vs[0]
    small_sq = jnp.zeros((8, 128), F32)
    for k in range(S):
        own_rows = jnp.where((sub8 < 2) | ((sub8 == 2) & (lane8 < 32)), vs[k], 0.0)
        small_sq = small_sq + own_rows * own_rows
        if k > 0:
            lift = lift + vs[k]
    lift = jnp.where((sub8 >= 3) & (sub8 < 7), lift, 0.0)
    small_sq = jnp.sum(small_sq + lift * lift)
    gate, half = s // 2, lax.rem(s, 2)
    d_gates = jnp.zeros((8, 128), F32)
    for k in range(4):
        turned = pltpu.roll(vs[4 * half + k], lax.rem(32 * k - 32 * gate + 128, 128), 1)
        d_gates = jnp.where((lane8 >= 32 * k) & (lane8 < 32 * k + 32), turned, d_gates)
    quarter = 32 * lax.rem(s, 4)
    upper = s // 4
    turned = pltpu.roll(lift, lax.rem(128 - quarter, 128), 1)
    line_w = jnp.where(upper == 0, turned[3:4], turned[4:5])
    line_b = jnp.where(upper == 0, turned[5:6], turned[6:7])
    line_h = vs[s][2:3, :]
    lane1 = lane8[0:1]
    d_chans = jnp.where(
        lane1 < 32, line_w,
        jnp.where(lane1 < 64, pltpu.roll(line_b, 32, 1), pltpu.roll(line_h, 64, 1)),
    )
    loss = jnp.zeros((1, 1), F32)
    for k in range(HOR):
        loss = loss + vs[s][2:3, 32 + k : 33 + k] * weight_rows[k]

    arrived(qf.at[0:3], f_in.at[F_SQ])
    qs[s] = (qf[0] + qf[1]) + (qf[2] + qf[3])
    each(1, S, lambda k: send(
        qs.at[s], qs.at[s], sp_out.at[SQ], sp_in.at[SQ], (ahead(k), f)
    ))
    arrived(qs.at[1:S], sp_in.at[SQ])
    squares = qs[0]
    for k in range(1, S):
        squares = squares + qs[k]
    norm = jnp.sqrt(squares + small_sq)
    factor = jnp.minimum(1.0, CLIP / (norm + 1e-06))
    out = jnp.where(sub8 < 2, d_gates, d_chans)
    out = jnp.where(sub8 == 3, loss, out)
    out = jnp.where(sub8 == 4, norm, out)
    out = jnp.where(sub8 == 5, factor, out)
    small_ref[...] = out

    for cp in moments:
        cp.wait()
    for kind in range(2):
        blocks = sum(len(holders(kind, i)) for i in range(4)) // 4
        for i in range(4):
            sent = functools.partial(left, wr.at[1:S, kind, i, :, f], w_out.at[kind, i])
            only(holds(s, kind, i), sent)
        for hop in range(3):
            left(wr.at[0:blocks, kind, :, :, f], x_out.at[kind, hop])
    left(tiles.at[f, 1:S], sp_out.at[TILE])
    left(h1.at[f, 32 : 32 * S, :], sp_out.at[H1])
    left(yrow.at[1:S], sp_out.at[Y])
    left(dhy, sp_out.at[DHY])
    left(dhr.at[0:3], sp_out.at[DHL])
    for t in range(2):
        left(dall.at[t, :, 0:4], y_out.at[t])
        if CHAIN[t]:
            edge = (z == 0) | (z == 3)
            pl.when(edge)(lambda: left(dall.at[t, :, 0:1], sp_out.at[BLK + t]))
            middle = jnp.logical_not(edge)
            pl.when(middle)(lambda: left(dall.at[t, :, 0:5], sp_out.at[BLK + t]))
        else:
            left(dall.at[t, :, 0:3], sp_out.at[BLK + t])
        left(dall.at[t, 0:3, s], f_out.at[F_D + t])
    left(hr.at[1:S], sp_out.at[END])
    left(vs.at[1:S], sp_out.at[VEC])
    left(qs.at[1:S], sp_out.at[SQ])
    left(tiles.at[0:3], f_out.at[F_TILE])
    left(h1.at[0:3], f_out.at[F_H1])
    left(vf.at[0:3], f_out.at[F_VEC])
    left(qf.at[0:3], f_out.at[F_SQ])


def sse_rows(sse):
    return sse + [jnp.zeros((128 - 32 - HOR, 1), F32)]


def step_fast(
    frames, targets, sizes, horizon, conv_weight, conv_m, conv_v, gates_vec, chan_vec
):
    S, F = lax.axis_size("space"), lax.axis_size("fsdp")
    R, N = conv_weight.shape
    rows, cols = frames.shape[3] * S, frames.shape[4]
    PX = 2 * rows * cols

    VM = pltpu.VMEM
    DMA = pltpu.SemaphoreType.DMA
    geo = (S, F, R, rows, PX)
    out = pl.pallas_call(
        functools.partial(step_kernel, geo),
        out_shape=(
            VM((2048, N), F32),
            VM((2048, N), F32),
            VM((R, N), F32),
            VM((R, N), F32),
            VM((8, 128), F32),
            VM((32, 256), F32),
            VM((32, 256), F32),
        ),
        in_specs=[pl.BlockSpec(memory_space=pltpu.HBM)] * 9,
        out_specs=(pl.BlockSpec(memory_space=VM),) * 7,
        scratch_shapes=[
            VM(frames.shape, F32),
            VM(frames.shape, F32),
            VM(frames.shape, jnp.int32),
            VM((1, 2), jnp.int32),
            VM(gates_vec.shape, F32),
            VM(chan_vec.shape, F32),
            VM((2, 4, 2, 8, 32, 128), BF16),
            VM((S, 2, 4, 2, 4, 32, 128), BF16),
            VM((640, 1280), BF16),
            VM((640, 1280), BF16),
            VM((1280, 640), BF16),
            VM((F, S, 8, 128), F32),
            VM((F, 2, 8, PX), F32),
            VM((5, 256, 128), F32),
            VM((1280, PX), BF16),
            VM((5, 128, PX), F32),
            VM((5, 256, PX), F32),
            VM((128, PX), F32),
            VM((2, 3, 128, PX), F32),
            VM((F, 256, PX), BF16),
            VM((S, 2, PX), F32),
            VM((640, PX), BF16),
            VM((256, PX), F32),
            VM((4, 32, PX), F32),
            VM((4, 32, PX), F32),
            VM((2, 4, 32, PX), BF16),
            VM((2, F, S, 32, PX), BF16),
            VM((F, PX, 256), BF16),
            VM((rows // 2, cols, 128), F32),
            VM((S, cols, 128), F32),
            VM((3, F, 4, 256, PX), BF16),
            VM((2, 8 * TAPS, PX), F32),
            VM((8, 128), F32),
            VM((F, 8, 128), F32),
            VM((S, 8, 128), F32),
            VM((F, 8, 128), F32),
            VM((S, 8, 128), F32),
            DMA((8,)),
            DMA((4,)),
            DMA((2, 4)),
            DMA((2, 4)),
            DMA((2, 3)),
            DMA((2, 4)),
            DMA((2, 2)),
            DMA((10,)),
            DMA((30,)),
            DMA((2,)),
            DMA((2, 4, 3, 2)),
            DMA((7,)),
            DMA((11,)),
        ],
        compiler_params=pltpu.CompilerParams(
            collective_id=0, has_side_effects=True, vmem_limit_bytes=44 * 2**20
        ),
    )(
        *(
            pltpu.with_memory_space_constraint(v, pltpu.HBM)
            for v in (
                frames, targets, horizon, sizes.reshape(1, 2), gates_vec, chan_vec,
                conv_weight, conv_m, conv_v,
            )
        )
    )
    return out


def adam_kernel(steps, *refs):
    small_ref, h_ref, c_ref, g_ref = refs[:4]
    (w_ref, m_ref, v_ref), gates, chan = refs[4:7], refs[7:10], refs[10:13]
    outs, held, sem, sems = refs[13:26], refs[26:39], refs[39], refs[40]
    conv_held, conv_outs = held[2:5], outs[2:5]
    factor = small_ref[5:6, 0:1]
    R = m_ref.shape[0]
    size = R // steps
    base = lax.rem(lax.axis_index("space") * R, 512)
    held[0][...] = small_ref[3:4, 0:1]
    held[1][...] = small_ref[4:5, 0:1]

    def update(weights, grad, news):
        w, m, v = weights
        for ref, new in zip(news, adam_update(w[...], m[...], v[...], grad * factor)):
            ref[...] = new

    update(gates, small_ref[0:2, :], held[5:8])
    chans = [small_ref[2:3, 32 * q : 32 * q + 32] for q in range(3)]
    update(chan, jnp.concatenate(chans, axis=0), held[8:11])
    for r in range(2):
        held[11][0, r] = h_ref[16 * r : 16 * r + 16, :]
        held[12][0, r] = c_ref[16 * r : 16 * r + 16, :]
    copies = []
    for n in (0, 1, *range(5, 13)):
        copies.append(pltpu.make_async_copy(held[n], outs[n], sem.at[n]))
        copies[-1].start()
    for n in range(steps):
        at = slice(size * n, size * n + size)
        moved = pl.ds(pl.multiple_of(base + size * n, 64), size)
        news = adam_update(w_ref[moved, :], m_ref[at, :], v_ref[at, :], g_ref[moved, :] * factor)
        for q, new in enumerate(news):
            conv_held[q][at, :] = new
            copies.append(
                pltpu.make_async_copy(conv_held[q].at[at, :], conv_outs[q].at[at, :], sems.at[q, n])
            )
            copies[-1].start()
    for copy in copies:
        copy.wait()


def adam_step(small, hidden, cell, grad, weights, frame_shape):
    steps = 25
    rows, cols = frame_shape
    conv, gates, chan = weights
    flat = [*conv, *gates, *chan]
    shapes = [v.shape for v in (*conv[1:], conv[1], *gates, *chan)]
    state = (1, rows, cols, hidden.shape[1])
    shapes = [(1, 1), (1, 1), *shapes, state, state]
    out = pl.pallas_call(
        functools.partial(adam_kernel, steps),
        out_shape=tuple(jax.ShapeDtypeStruct(v, F32) for v in shapes),
        in_specs=[pl.BlockSpec(memory_space=pltpu.VMEM)] * (4 + len(flat)),
        out_specs=(pl.BlockSpec(memory_space=pl.ANY),) * len(shapes),
        scratch_shapes=[pltpu.VMEM(v, F32) for v in shapes]
        + [pltpu.SemaphoreType.DMA((13,)), pltpu.SemaphoreType.DMA((3, steps))],
        compiler_params=pltpu.CompilerParams(vmem_limit_bytes=8 * 2**20),
    )(small, hidden, cell, grad, *flat)
    return (out[0].reshape(()), out[1].reshape(()), *out[2:])


def per_device_fast(
    frames, targets, sizes, horizon,
    conv_weight, conv_m, conv_v,
    gates_vec, gates_m, gates_v,
    chan_vec, chan_m, chan_v,
):
    grad, weight, first, second, small, hidden, cell = step_fast(
        frames, targets, sizes, horizon, conv_weight, conv_m, conv_v, gates_vec, chan_vec
    )
    weights = ((weight, first, second), (gates_vec, gates_m, gates_v), (chan_vec, chan_m, chan_v))
    return adam_step(small, hidden, cell, grad, weights, frames.shape[3:])


def fits(mesh, shapes):
    S, F = mesh.shape["space"], mesh.shape["fsdp"]
    frames, conv, chan = shapes
    return (
        (S, F) == (8, 4)
        and frames == (2, F, 2, 2 * S, 16)
        and conv == (TAPS * 512, 1024)
        and chan == (3, 256)
    )


def solution(mesh):
    in_specs = (
        P(None, "fsdp", None, "space", None),
        P(None, "fsdp", None, "space", None),
        P(None, "fsdp"),
        P(None, "fsdp", None, "space", None),
        P("space", "fsdp"),
        P("space", "fsdp"),
        P("space", "fsdp"),
        P(None, "space"),
        P(None, "space"),
        P(None, "space"),
        P(None, "space"),
        P(None, "space"),
        P(None, "space"),
    )
    out_specs = (
        P(),
        P(),
        P("space", "fsdp"),
        P("space", "fsdp"),
        P("space", "fsdp"),
        P(None, "space"),
        P(None, "space"),
        P(None, "space"),
        P(None, "space"),
        P(None, "space"),
        P(None, "space"),
        P("fsdp", "space", None, None),
        P("fsdp", "space", None, None),
    )

    def run(*args):
        shapes = (args[0].shape, args[4].shape, args[10].shape)
        body = per_device_fast if fits(mesh, shapes) else per_device
        return jax.shard_map(
            body, mesh=mesh, in_specs=in_specs, out_specs=out_specs, check_vma=False
        )(*args)

    return run
```
